512 devices in a mesh: shot: 4 (over x), gx: 4 (over y_lo, core), gy: 32 (over y_hi, z).
Axes of the slice: x: 4, y: 4 (y_hi: 2, y_lo: 2; y = y_hi * 2 + y_lo), z: 16, core: 2. Of those that a mesh axis runs over, the one named last changes fastest.
Arguments:
- model_vel2: float32 [128, 512, 512], P('gx', 'gy', 'shot'), may hold values from 0.04 to 0.18
- offsets: int32 [4], P('shot'), may hold values from 0 to 256
- wave_prev: float32 [4, 128, 512, 256], P('shot', 'gx', 'gy'), may hold values from -6 to 6
- wave_cur: float32 [4, 128, 512, 256], P('shot', 'gx', 'gy'), may hold values from -1.5 to 1.5
- adj_cur: float32 [4, 128, 512, 256], P('shot', 'gx', 'gy'), may hold values from -1.5 to 1.5
- adj_next: float32 [4, 128, 512, 256], P('shot', 'gx', 'gy'), may hold values from -0.6 to 0.6
- src_cell: int32 [4, 3], P('shot'), may hold values from 0 to 511, as said below
- src_amp: float32 [4, 2], P('shot'), may hold values from -32 to 32
- rec_cell: int32 [4, 256, 3], P('shot'), may hold values from 0 to 511, as said below
- rec_res: float32 [4, 256, 2], P('shot'), may hold values from -4 to 4
Outputs:
- model_grad: float32 [128, 512, 512], P('gx', 'gy', 'shot')
- adj_out: float32 [4, 128, 512, 256], P('shot', 'gx', 'gy')
The draws below stay inside these ranges and needn't reach their ends.
Inputs may be any that keep to these rules, and one draw needn't show every extreme that they name: Each shot group's aperture lies inside the model's depth: offsets[s] + 256 <= 512. `src_cell`: each row is a cell (x, y, z) of the aperture: 0 <= x < 128, 0 <= y < 512, 0 <= z < 256. `rec_cell`: each row is a cell (x, y, z) of the aperture: 0 <= x < 128, 0 <= y < 512, 0 <= z < 256; receivers may coincide.
All inputs are finite; a program needn't handle non-finite values.
Results may differ from the reference program's by a relative error of at most 0.0065.
Values sent between devices are 32-bit elements; how exact they have to be, the bound alone decides.
No kernel may reach another device: no remote copies, remote signals or barrier semaphores. Data moves between devices by JAX's collectives and lax.ppermute only.
A program may use at most 64 MiB of HBM per device.

```python
import jax
import jax.numpy as jnp
from jax import lax

CZ = 256
NREC = 256
NSHOT = 4
NX = 128
NY = 512
MZ = 512


def draw_src_cell(key, part):
    key = jax.random.fold_in(key, 11)
    key_x, key_y, key_z = jax.random.split(key, 3)
    cell_x = jax.random.randint(key_x, (NSHOT, 1), 0, NX)
    cell_y = jax.random.randint(key_y, (NSHOT, 1), 0, NY)
    cell_z = jax.random.randint(key_z, (NSHOT, 1), 0, CZ)
    placed = jnp.concatenate([cell_x, cell_y, cell_z], axis=1).astype(jnp.int32)
    limits = [NX, NY, CZ]
    largest = max(limits)
    chosen = limits.index(largest)
    placed = placed.at[0, chosen].set(largest - 1)
    placed = placed.at[1, 0].set(0)
    return placed


def draw_rec_cell(key, part):
    key = jax.random.fold_in(key, 23)
    key_x, key_y, key_z = jax.random.split(key, 3)
    cell_x = jax.random.randint(key_x, (NSHOT, NREC, 1), 0, NX)
    cell_y = jax.random.randint(key_y, (NSHOT, NREC, 1), 0, NY)
    cell_z = jax.random.randint(key_z, (NSHOT, NREC, 1), 0, CZ)
    placed = jnp.concatenate([cell_x, cell_y, cell_z], axis=2).astype(jnp.int32)
    limits = [NX, NY, CZ]
    largest = max(limits)
    chosen = limits.index(largest)
    placed = placed.at[0, 0, chosen].set(largest - 1)
    placed = placed.at[0, 1, 0].set(0)
    return placed


def with_ends(array, key, low, high):
    shape = array.shape
    place = [jax.random.randint(jax.random.fold_in(key, axis), (), 0, shape[axis]) for axis in range(len(shape))]
    array = array.at[tuple(place)].set(low)
    longest = shape.index(max(shape))
    place[longest] = (place[longest] + 1) % shape[longest]
    return array.at[tuple(place)].set(high)


def levels(key, shape, cuts, least, high):
    gain = 1.0
    for axis_at, blocks in cuts:
        draws = jax.random.uniform(jax.random.fold_in(jax.random.fold_in(key, 6), axis_at), (blocks,), jnp.float32, least / len(cuts), high / len(cuts))
        gain = gain * jnp.repeat(jnp.exp(draws), shape[axis_at] // blocks).reshape((-1,) + (1,) * (len(shape) - 1 - axis_at))
    return gain


def normal_values(stream_key, dims, width, reach, cuts=(), kind=jnp.bfloat16):
    drawn = jax.random.normal(stream_key, dims, jnp.float32) * width
    if len(cuts) > 0:
        drawn = levels(stream_key, dims, cuts, -0.22, 0.18) * drawn
    return jnp.clip(drawn, min=-reach, max=reach).astype(kind)


def setup_inputs(seed: int = 0) -> dict:
    key_of = jax.random.split(jax.random.key(seed), 11)
    return {
        "model_vel2": jnp.clip(0.04 + 0.14000001 * jax.random.uniform(key_of[0], (NX, NY, MZ), jnp.float32) ** levels(key_of[0], (NX, NY, MZ), ((0, 4), (1, 32), (2, 4)), -0.2, 0.2), 0.04, 0.18),
        "offsets": with_ends(jax.random.randint(key_of[1], (NSHOT,), 0, MZ - CZ + 1), jax.random.fold_in(key_of[1], 1), 0, MZ - CZ).astype(jnp.int32),
        "wave_prev": normal_values(key_of[2], (NSHOT, NX, NY, CZ), 1.0, 6.0, ((0, 4), (1, 4), (2, 32)), jnp.float32),
        "wave_cur": normal_values(key_of[3], (NSHOT, NX, NY, CZ), 0.25, 1.5, ((0, 4), (1, 4), (2, 32)), jnp.float32),
        "adj_cur": normal_values(key_of[4], (NSHOT, NX, NY, CZ), 0.25, 1.5, ((0, 4), (1, 4), (2, 32)), jnp.float32),
        "adj_next": normal_values(key_of[5], (NSHOT, NX, NY, CZ), 0.1, 0.6, ((0, 4), (1, 4), (2, 32)), jnp.float32),
        "src_cell": draw_src_cell(jax.random.fold_in(key_of[10], 71), 0),
        "src_amp": normal_values(key_of[7], (NSHOT, 2), 8.0, 32.0, ((0, 4),), jnp.float32),
        "rec_cell": draw_rec_cell(jax.random.fold_in(key_of[10], 71), 0),
        "rec_res": normal_values(key_of[9], (NSHOT, NREC, 2), 1.0, 4.0, ((0, 4),), jnp.float32),
    }


COEF = (-205.0 / 72.0, 8.0 / 5.0, -1.0 / 5.0, 8.0 / 315.0, -1.0 / 560.0)


def stencil(ext):
    size_x = ext.shape[0] - 8
    size_y = ext.shape[1] - 8
    depth = ext.shape[2]
    full = jnp.pad(ext, ((0, 0), (0, 0), (4, 4)))
    centre = full[4:4 + size_x, 4:4 + size_y, 4:4 + depth]
    total = (3.0 * COEF[0]) * centre
    for k in range(1, 5):
        near = full[4 + k:4 + k + size_x, 4:4 + size_y, 4:4 + depth] + full[4 - k:4 - k + size_x, 4:4 + size_y, 4:4 + depth]
        near = near + full[4:4 + size_x, 4 + k:4 + k + size_y, 4:4 + depth] + full[4:4 + size_x, 4 - k:4 - k + size_y, 4:4 + depth]
        near = near + full[4:4 + size_x, 4:4 + size_y, 4 + k:4 + k + depth] + full[4:4 + size_x, 4:4 + size_y, 4 - k:4 - k + depth]
        total = total + COEF[k] * near
    return total


def laplace(field):
    return stencil(jnp.pad(field, ((4, 4), (4, 4), (0, 0))))


def reference(model_vel2, offsets, wave_prev, wave_cur, adj_cur, adj_next, src_cell, src_amp, rec_cell, rec_res):
    model_grad = jnp.zeros((NX, NY, MZ), jnp.float32)
    adjoint_list = []
    for shot_id in range(NSHOT):
        start = offsets[shot_id].astype(jnp.int32)
        vel = lax.dynamic_slice_in_dim(model_vel2, start, CZ, 2)
        wave0 = wave_prev[shot_id]
        wave1 = wave_cur[shot_id]
        source = src_cell[shot_id]
        lap1 = laplace(wave1)
        wave2 = 2.0 * wave1 - wave0 + vel * lap1
        wave2 = wave2.at[source[0], source[1], source[2]].add(src_amp[shot_id, 0])
        lap2 = laplace(wave2)
        wave3 = 2.0 * wave2 - wave1 + vel * lap2
        wave3 = wave3.at[source[0], source[1], source[2]].add(src_amp[shot_id, 1])
        lap3 = laplace(wave3)
        adj4 = adj_cur[shot_id]
        adj5 = adj_next[shot_id]
        cells = rec_cell[shot_id]
        adj3 = 2.0 * adj4 - adj5 + laplace(vel * adj4)
        adj3 = adj3.at[cells[:, 0], cells[:, 1], cells[:, 2]].add(rec_res[shot_id, :, 0])
        adj2 = 2.0 * adj3 - adj4 + laplace(vel * adj3)
        adj2 = adj2.at[cells[:, 0], cells[:, 1], cells[:, 2]].add(rec_res[shot_id, :, 1])
        grad = adj4 * lap3 + adj3 * lap2 + adj2 * lap1
        placed = lax.dynamic_update_slice(jnp.zeros((NX, NY, MZ), jnp.float32), grad, (jnp.int32(0), jnp.int32(0), start))
        model_grad = model_grad + placed
        adjoint_list.append(adj2)
    return model_grad, jnp.stack(adjoint_list)
```

```python
import functools

import jax
import jax.numpy as jnp
from jax import lax
from jax.experimental import pallas as pl
from jax.experimental.pallas import tpu as pltpu
from jax.sharding import PartitionSpec as P

COEF = (-205.0 / 72.0, 8.0 / 5.0, -1.0 / 5.0, 8.0 / 315.0, -1.0 / 560.0)
F32 = jnp.float32
HALF = 128


def swap(value, axis, odd):
    pairs = []
    for i in range(odd, lax.axis_size(axis) - 1, 2):
        pairs += [(i, i + 1), (i + 1, i)]
    return lax.ppermute(value, axis, pairs)


def shift(value, axis, distance):
    size = lax.axis_size(axis)
    return lax.ppermute(value, axis, [(i, (i + distance) % size) for i in range(size)])


def exchange(payload):
    ya, yb, xa, xb = payload
    return swap(ya, "gy", 0), swap(yb, "gy", 1), swap(xa, "gx", 0), swap(xb, "gx", 1)


def call(body, out_shape, scratch=(), smem=0, n_in=0, flops=0):
    vmem = pl.BlockSpec(memory_space=pltpu.VMEM)
    scal = pl.BlockSpec(memory_space=pltpu.SMEM)
    return pl.pallas_call(
        body,
        out_shape=out_shape,
        in_specs=[scal] * smem + [vmem] * n_in,
        out_specs=jax.tree.map(lambda _: vmem, out_shape),
        scratch_shapes=list(scratch),
        compiler_params=pltpu.CompilerParams(vmem_limit_bytes=24 * 1024 * 1024),
        cost_estimate=pl.CostEstimate(flops=flops, bytes_accessed=1 << 20, transcendentals=0),
    )


def shaped(*dims):
    return jax.ShapeDtypeStruct(dims, F32)


def even(axis):
    return lax.rem(lax.axis_index(axis), 2) == 0


def put_edges(field, row, ya, yb, xa, xb, plane):
    even_y, even_x = even("gy"), even("gx")
    size_x, size_y = field.shape[0], field.shape[1]
    first, last = field[:, 0:4, :], field[:, size_y - 4 : size_y, :]
    ya[:, row : row + 4, :] = jnp.where(even_y, last, first)
    yb[:, row : row + 4, :] = jnp.where(even_y, first, last)
    top = size_x - 4
    xa[plane : plane + 4] = field[pl.ds(jnp.where(even_x, top, 0), 4)]
    xb[plane : plane + 4] = field[pl.ds(jnp.where(even_x, 0, top), 4)]


def fill(space, field, halos, row, plane):
    ya, yb, xa, xb = halos
    even_y, even_x = even("gy"), even("gx")
    size_x, size_y = field.shape[0], field.shape[1]
    place_a = jnp.where(even_x, size_x + 4, 0)
    place_b = jnp.where(even_x, 0, size_x + 4)
    for h in range(2):
        z = slice(h * HALF, (h + 1) * HALF)
        space[h, 4 : size_x + 4, 8 : size_y + 8, :] = field[:, :, z]
        space[h, pl.ds(place_a, 4), 8 : size_y + 8, :] = xa[plane : plane + 4, :, z]
        space[h, pl.ds(place_b, 4), 8 : size_y + 8, :] = xb[plane : plane + 4, :, z]
        a, b = ya[:, row : row + 4, z], yb[:, row : row + 4, z]
        space[h, 4 : size_x + 4, 4:8, :] = jnp.where(even_y, b, a)
        space[h, 4 : size_x + 4, size_y + 8 : size_y + 12, :] = jnp.where(even_y, a, b)


def depth_part(field, band, out):
    size_x, size_y, depth = field.shape

    def body(i, _):
        part = field[pl.ds(i * 8, 8)].reshape(8 * size_y, depth)
        done = jnp.dot(part, band[...], precision=lax.Precision.HIGHEST, preferred_element_type=F32)
        out[pl.ds(i * 8, 8)] = done.reshape(8, size_y, depth)
        return 0

    lax.fori_loop(0, size_x // 8, body, 0)


def laplacian(space, depthwise, x, h, size_y):
    centre = space[h, x + 4, 8 : size_y + 8, :]
    total = (3.0 * COEF[0]) * centre + depthwise[x, :, h * HALF : (h + 1) * HALF]
    for k in range(1, 5):
        near = space[h, x + 4 + k, 8 : size_y + 8, :] + space[h, x + 4 - k, 8 : size_y + 8, :]
        near = near + space[h, x + 4, 8 + k : size_y + 8 + k, :] + space[h, x + 4, 8 - k : size_y + 8 - k, :]
        total = total + COEF[k] * near
    return total


def add_source(cell, amount, field):
    size_x, size_y, depth = field.shape
    x = cell[0, 0] - lax.axis_index("gx") * size_x
    y = cell[0, 1] - lax.axis_index("gy") * size_y

    @pl.when((x >= 0) & (x < size_x) & (y >= 0) & (y < size_y))
    def _():
        at = (lax.broadcasted_iota(jnp.int32, (size_y, depth), 0) == y) & (
            lax.broadcasted_iota(jnp.int32, (size_y, depth), 1) == cell[0, 2]
        )
        field[x] = field[x] + jnp.where(at, amount, 0.0)


def edges_kernel(field, ya, yb, xa, xb):
    even_y, even_x = even("gy"), even("gx")
    size_x, size_y = field.shape[0], field.shape[1]
    half = size_x // 2
    for row in range(2):
        x = slice(row * half, (row + 1) * half)
        first, last = field[x, 0:4, :], field[x, size_y - 4 : size_y, :]
        ya[:, row * 4 : row * 4 + 4, :] = jnp.where(even_y, last, first)
        yb[:, row * 4 : row * 4 + 4, :] = jnp.where(even_y, first, last)
    top = size_x - 4
    xa[...] = field[pl.ds(jnp.where(even_x, top, 0), 4)]
    xb[...] = field[pl.ds(jnp.where(even_x, 0, top), 4)]


def tables_kernel(size_x, size_y, cells, res, band, inject0, inject1):
    depth = band.shape[0]
    i = lax.broadcasted_iota(jnp.int32, (depth, depth), 0)
    j = lax.broadcasted_iota(jnp.int32, (depth, depth), 1)
    away = jnp.abs(i - j)
    total = jnp.zeros((depth, depth), F32)
    for k in range(1, 5):
        total = jnp.where(away == k, COEF[k], total)
    band[...] = total
    count = cells.shape[1]
    lanes = 128
    pad = jnp.zeros((count, lanes - 3), jnp.int32)
    where = jnp.concatenate([cells[0], pad], axis=1).astype(F32)
    rows = jnp.transpose(where)[0:8].astype(jnp.int32)
    amounts = jnp.transpose(jnp.concatenate([res[0], jnp.zeros((count, lanes - 2), F32)], axis=1))
    x = rows[0:1, :] - lax.axis_index("gx") * size_x
    y = rows[1:2, :] - lax.axis_index("gy") * size_y
    inside = (x >= 0) & (x < size_x) & (y >= 0) & (y < size_y)
    place = jnp.where(inside, x * size_y + y, -1)
    deep = jnp.where(
        lax.broadcasted_iota(jnp.int32, (count, depth), 1) == cells[0, :, 2:3], 1.0, 0.0
    ).astype(F32)
    for n, out in enumerate((inject0, inject1)):
        for part in range(4):
            size = size_x * size_y // 4
            at = lax.broadcasted_iota(jnp.int32, (size, count), 0) + part * size
            flat = jnp.where(at == place, amounts[n : n + 1, :], 0.0)
            done = jnp.dot(flat, deep, precision=lax.Precision.HIGHEST, preferred_element_type=F32)
            out[part * size_x // 4 : (part + 1) * size_x // 4] = done.reshape(size_x // 4, size_y, depth)


def first_kernel(wave1, band, ya, yb, xa, xb, lap1, space, depthwise):
    size_x, size_y = wave1.shape[0], wave1.shape[1]
    even_y, even_x = even("gy"), even("gx")
    half = size_x // 2
    place_a = jnp.where(even_x, size_x + 4, 0)
    place_b = jnp.where(even_x, 0, size_x + 4)
    for h in range(2):
        z = slice(h * HALF, (h + 1) * HALF)
        space[h, 4 : size_x + 4, 8 : size_y + 8, :] = wave1[:, :, z]
        space[h, pl.ds(place_a, 4), 8 : size_y + 8, :] = xa[:, :, z]
        space[h, pl.ds(place_b, 4), 8 : size_y + 8, :] = xb[:, :, z]
        for row in range(2):
            a, b = ya[:, row * 4 : row * 4 + 4, z], yb[:, row * 4 : row * 4 + 4, z]
            x = slice(4 + row * half, 4 + (row + 1) * half)
            space[h, x, 4:8, :] = jnp.where(even_y, b, a)
            space[h, x, size_y + 8 : size_y + 12, :] = jnp.where(even_y, a, b)
    depth_part(wave1, band, depthwise)

    def body(x, _):
        for h in range(2):
            lap1[x, :, h * HALF : (h + 1) * HALF] = laplacian(space, depthwise, x, h, size_y)
        return 0

    lax.fori_loop(0, size_x, body, 0, unroll=2)


def second_kernel(
    offsets, cell, amp, tile0, tile1, tile2, tile3, lap1, wave0, wave1, adj4,
    vel, wave2, image, ya, yb, xa, xb, column,
):
    size_x, size_y = wave1.shape[0], wave1.shape[1]
    me = lax.axis_index("shot")
    for d, tile in enumerate((tile0, tile1, tile2, tile3)):
        column[lax.rem(me - d + 4, 4)] = tile[...]
    start = offsets[0]
    low = start // HALF
    shift_by = lax.rem(start, HALF)
    back = lax.rem(HALF - shift_by, HALF)
    third = jnp.minimum(low + 2, 3)

    def body(x, _):
        lane = lax.broadcasted_iota(jnp.int32, (size_y, HALF), 1)
        rolled = [pltpu.roll(column[i, x], back, 1) for i in (low, low + 1, third)]
        for h in range(2):
            z = slice(h * HALF, (h + 1) * HALF)
            v = jnp.where(lane < HALF - shift_by, rolled[h], rolled[h + 1])
            vel[x, :, z] = v
            image[x, :, z] = v * adj4[x, :, z]
            wave2[x, :, z] = 2.0 * wave1[x, :, z] - wave0[x, :, z] + v * lap1[x, :, z]
        return 0

    lax.fori_loop(0, size_x, body, 0, unroll=2)
    add_source(cell, amp[0, 0], wave2)
    put_edges(wave2, 0, ya, yb, xa, xb, 0)
    put_edges(image, 4, ya, yb, xa, xb, 4)


def third_kernel(
    cell, amp, ya, yb, xa, xb, wave1, wave2, adj4, adj5, vel, image, band, inject,
    lap2, wave3, adj3, image3, pya, pyb, pxa, pxb, space, depthwise, space2, depthwise2,
):
    size_x, size_y = wave1.shape[0], wave1.shape[1]
    halos = (ya, yb, xa, xb)
    fill(space, wave2, halos, 0, 0)
    fill(space2, image, halos, 4, 4)
    depth_part(wave2, band, depthwise)
    depth_part(image, band, depthwise2)

    def body(x, _):
        for h in range(2):
            z = slice(h * HALF, (h + 1) * HALF)
            v = vel[x, :, z]
            lap = laplacian(space, depthwise, x, h, size_y)
            lap2[x, :, z] = lap
            wave3[x, :, z] = 2.0 * wave2[x, :, z] - wave1[x, :, z] + v * lap
            adj = 2.0 * adj4[x, :, z] - adj5[x, :, z] + laplacian(space2, depthwise2, x, h, size_y)
            adj = adj + inject[x, :, z]
            adj3[x, :, z] = adj
            image3[x, :, z] = v * adj
        return 0

    lax.fori_loop(0, size_x, body, 0, unroll=2)
    add_source(cell, amp[0, 1], wave3)
    put_edges(wave3, 0, pya, pyb, pxa, pxb, 0)
    put_edges(image3, 4, pya, pyb, pxa, pxb, 4)


def fourth_kernel(
    offsets, ya, yb, xa, xb, wave3, image3, adj3, adj4, lap1, lap2, band, inject,
    adj2, placed, space, depthwise, space2, depthwise2, column,
):
    size_x, size_y = wave3.shape[0], wave3.shape[1]
    halos = (ya, yb, xa, xb)
    fill(space, wave3, halos, 0, 0)
    fill(space2, image3, halos, 4, 4)
    depth_part(wave3, band, depthwise)
    depth_part(image3, band, depthwise2)
    start = offsets[0]
    low = start // HALF
    shift_by = lax.rem(start, HALF)
    column[...] = jnp.zeros_like(column)

    def body(x, _):
        lane = lax.broadcasted_iota(jnp.int32, (size_y, HALF), 1)
        rolled = []
        for h in range(2):
            z = slice(h * HALF, (h + 1) * HALF)
            lap3 = laplacian(space, depthwise, x, h, size_y)
            old, mid = adj4[x, :, z], adj3[x, :, z]
            adj = 2.0 * mid - old + laplacian(space2, depthwise2, x, h, size_y)
            adj = adj + inject[x, :, z]
            adj2[x, :, z] = adj
            grad = old * lap3 + mid * lap2[x, :, z] + adj * lap1[x, :, z]
            rolled.append(pltpu.roll(grad, shift_by, 1))
        high = lane >= shift_by
        column[low, x] = jnp.where(high, rolled[0], 0.0)
        column[low + 1, x] = jnp.where(high, rolled[1], rolled[0])
        column[low + 2, x] = jnp.where(high, 0.0, rolled[1])
        return 0

    lax.fori_loop(0, size_x, body, 0, unroll=2)
    placed[...] = column[0:4]


def sum_kernel(parts, out):
    out[...] = (parts[0] + parts[1]) + (parts[2] + parts[3])


def local(model_vel2, offsets, wave_prev, wave_cur, adj_cur, adj_next, src_cell, src_amp, rec_cell, rec_res):
    size_x, size_y, depth = wave_cur.shape[1:]
    wave0, wave1, adj4, adj5 = wave_prev[0], wave_cur[0], adj_cur[0], adj_next[0]
    block = shaped(size_x, size_y, depth)
    edge_y, edge_x = shaped(size_x, 8, depth), shaped(8, size_y, depth)
    space = pltpu.VMEM((2, size_x + 8, size_y + 16, HALF), F32)
    whole = pltpu.VMEM((size_x, size_y, depth), F32)
    five = pltpu.VMEM((5, size_x, size_y, HALF), F32)

    tiles = [model_vel2] + [shift(model_vel2, "shot", d) for d in (1, 2, 3)]
    edges = call(
        edges_kernel,
        (shaped(size_x // 2, 8, depth),) * 2 + (shaped(4, size_y, depth),) * 2,
        n_in=1,
    )(wave1)
    halos = exchange(edges)
    band, inject0, inject1 = call(
        functools.partial(tables_kernel, size_x, size_y), (shaped(depth, depth), block, block), n_in=2
    )(rec_cell, rec_res)
    lap1 = call(first_kernel, block, (space, whole), n_in=6)(wave1, band, *halos)
    vel, wave2, image, *edges = call(
        second_kernel, (block,) * 3 + (edge_y,) * 2 + (edge_x,) * 2,
        (pltpu.VMEM((4, size_x, size_y, HALF), F32),), smem=3, n_in=8,
    )(offsets, src_cell, src_amp, *tiles, lap1, wave0, wave1, adj4)
    halos = exchange(edges)
    lap2, wave3, adj3, image3, *edges = call(
        third_kernel, (block,) * 4 + (edge_y,) * 2 + (edge_x,) * 2, (space, whole) * 2, smem=2, n_in=12
    )(src_cell, src_amp, *halos, wave1, wave2, adj4, adj5, vel, image, band, inject0)
    halos = exchange(edges)
    adj2, placed = call(
        fourth_kernel, (block, shaped(4, size_x, size_y, HALF)), (space, whole) * 2 + (five,), smem=1, n_in=12
    )(offsets, *halos, wave3, image3, adj3, adj4, lap1, lap2, band, inject1)
    parts = lax.all_to_all(placed, "shot", 0, 0)
    owned = call(sum_kernel, shaped(size_x, size_y, HALF), n_in=1)(parts)
    return owned, adj2[None]


def solution(mesh):
    return jax.shard_map(
        local,
        mesh=mesh,
        in_specs=(
            P("gx", "gy", "shot"),
            P("shot"),
            P("shot", "gx", "gy", None),
            P("shot", "gx", "gy", None),
            P("shot", "gx", "gy", None),
            P("shot", "gx", "gy", None),
            P("shot", None),
            P("shot", None),
            P("shot", None, None),
            P("shot", None, None),
        ),
        out_specs=(P("gx", "gy", "shot"), P("shot", "gx", "gy", None)),
        check_vma=False,
    )
```

```python
import functools

import jax
import jax.numpy as jnp
import numpy as np
from jax import lax
from jax.experimental import pallas as pl
from jax.experimental.pallas import tpu as pltpu
from jax.sharding import PartitionSpec as P

COEF = (-205.0 / 72.0, 8.0 / 5.0, -1.0 / 5.0, 8.0 / 315.0, -1.0 / 560.0)
SCALE = 5040.0
WEIGHT = (0.0, 8064.0, -1008.0, 128.0, -9.0)
F32 = jnp.float32
HALF = 128


def swap(value, axis, odd):
    pairs = []
    for i in range(odd, lax.axis_size(axis) - 1, 2):
        pairs += [(i, i + 1), (i + 1, i)]
    return lax.ppermute(value, axis, pairs)


def swap_shot(value, odd):
    size = lax.axis_size("shot")
    pairs = []
    for i in range(odd, size, 2):
        pairs += [(i, (i + 1) % size), ((i + 1) % size, i)]
    return lax.ppermute(value, "shot", pairs)


def swap_across(value):
    size = lax.axis_size("shot")
    return lax.ppermute(value, "shot", [(i, (i + size // 2) % size) for i in range(size)])


def exchange(payload):
    ya, yb, xa, xb = payload
    return swap(yb, "gy", 1), swap(ya, "gy", 0), swap(xb, "gx", 1), swap(xa, "gx", 0)


def call(body, out_shape, scratch=(), smem=0, n_in=0, room=4, aliases=None):
    vmem = pl.BlockSpec(memory_space=pltpu.VMEM)
    scal = pl.BlockSpec(memory_space=pltpu.SMEM)
    return pl.pallas_call(
        body,
        out_shape=out_shape,
        in_specs=[scal] * smem + [vmem] * n_in,
        out_specs=jax.tree.map(lambda _: vmem, out_shape),
        scratch_shapes=list(scratch),
        input_output_aliases=aliases or {},
        compiler_params=pltpu.CompilerParams(vmem_limit_bytes=room << 20),
    )


def shaped(*dims):
    return jax.ShapeDtypeStruct(dims, F32)


def even(axis):
    return lax.rem(lax.axis_index(axis), 2) == 0


def weight(distance):
    distance = np.abs(distance)
    return np.where(distance <= 4, np.take(np.asarray(WEIGHT), np.minimum(distance, 4)), 0.0)


def difference_tables(size_y, depth, chunk):
    z = np.arange(depth)
    along_z = weight(z[:, None] - z[None, :])
    row = np.arange(chunk * size_y)
    x, y = row // size_y, row % size_y
    along_y = np.where(x[:, None] == x[None, :], weight(y[:, None] - y[None, :]), 0.0)
    edge = np.arange(chunk * 8)
    edge_x, edge_field, edge_row = edge // 8, edge % 8 // 4, edge % 4
    outer = np.zeros((2, 2, chunk * size_y, 2, chunk * 8))
    for parity in range(2):
        for field in range(2):
            for message in range(2):
                place = edge_row + size_y if parity == message else edge_row - 4
                use = (x[:, None] == edge_x[None, :]) & (edge_field[None, :] == field)
                outer[parity, field, :, message] = np.where(use, weight(y[:, None] - place[None, :]), 0.0)
    outer = outer.reshape(2, 2, chunk * size_y, 2 * chunk * 8)
    return (
        jnp.asarray(np.concatenate([along_z] * 3, axis=0), jnp.bfloat16),
        jnp.asarray(np.concatenate([along_y] * 3, axis=1), jnp.bfloat16),
        jnp.asarray(np.concatenate([outer] * 3, axis=3), jnp.bfloat16),
    )


def three(value):
    first = value.astype(jnp.bfloat16)
    rest = value - first.astype(F32)
    second = rest.astype(jnp.bfloat16)
    return first, second, (rest - second.astype(F32)).astype(jnp.bfloat16)


def product(a, b):
    return jnp.dot(a, b, preferred_element_type=F32)


def flat_part(field, along_y, along_z, out):
    size_x, size_y, depth = field.shape
    chunk = along_y.shape[0] // size_y
    for at in range(0, size_x, chunk):
        parts = three(field[at : at + chunk].reshape(chunk * size_y, depth))
        total = product(jnp.concatenate(parts, axis=1), along_z[...])
        total = total + product(along_y[...], jnp.concatenate(parts, axis=0))
        out[at : at + chunk] = total.reshape(chunk, size_y, depth)


def outer_part(ya, yb, at, outer, field, size_y):
    depth = ya.shape[2]
    chunk = outer.shape[2] // size_y
    a, b = (three(m[at : at + chunk].reshape(chunk * 8, depth)) for m in (ya, yb))
    stacked = jnp.concatenate([a[0], b[0], a[1], b[1], a[2], b[2]], axis=0)
    parity = jnp.where(even("gy"), 0, 1)
    return product(outer[parity, field], stacked).reshape(chunk, size_y, depth)


def outside_x(xa, xb, plane, out):
    even_x = even("gx")
    low = [jnp.where(even_x, xb[plane + i], xa[plane + i]) for i in range(4)]
    high = [jnp.where(even_x, xa[plane + i], xb[plane + i]) for i in range(4)]
    for i in range(4):
        first, last = 0.0, 0.0
        for k in range(i + 1, 5):
            first = first + COEF[k] * low[4 + i - k]
            last = last + COEF[k] * high[k - i - 1]
        out[i] = first
        out[7 - i] = last


def outer_parts(ya, yb, xa, xb, outer, size_x, size_y, sides, extras):
    chunk = outer.shape[2] // size_y
    for field, (side, extra) in enumerate(zip(sides, extras)):
        outside_x(xa, xb, 4 * field, side)
        for at in range(0, size_x, chunk):
            extra[at : at + chunk] = outer_part(ya, yb, at, outer, field, size_y) * (1.0 / SCALE)
        extra[0:4] = extra[0:4] + side[0:4]
        extra[size_x - 4 : size_x] = extra[size_x - 4 : size_x] + side[4:8]


def across(plane, x, z):
    total = (3.0 * COEF[0]) * plane(x, z)
    for k in range(1, 5):
        near = [p for p in (plane(x - k, z), plane(x + k, z)) if p is not None]
        if near:
            total = total + COEF[k] * sum(near[1:], near[0])
    return total


def within(field):
    size_x = field.shape[0]
    return lambda x, z: field[x, :, z] if 0 <= x < size_x else None


def halves():
    return [slice(h * HALF, (h + 1) * HALF) for h in range(2)]


def put_edges(field, row, ya, yb, xa, xb, plane):
    even_y, even_x = even("gy"), even("gx")
    size_x, size_y = field.shape[0], field.shape[1]
    first, last = field[:, 0:4, :], field[:, size_y - 4 : size_y, :]
    ya[:, row : row + 4, :] = jnp.where(even_y, last, first)
    yb[:, row : row + 4, :] = jnp.where(even_y, first, last)
    top = size_x - 4
    xa[plane : plane + 4] = field[pl.ds(jnp.where(even_x, top, 0), 4)]
    xb[plane : plane + 4] = field[pl.ds(jnp.where(even_x, 0, top), 4)]


def add_source(cell, amount, field):
    size_x, size_y, depth = field.shape
    x = cell[0, 0] - lax.axis_index("gx") * size_x
    y = cell[0, 1] - lax.axis_index("gy") * size_y

    @pl.when((x >= 0) & (x < size_x) & (y >= 0) & (y < size_y))
    def _():
        at = (lax.broadcasted_iota(jnp.int32, (size_y, depth), 0) == y) & (
            lax.broadcasted_iota(jnp.int32, (size_y, depth), 1) == cell[0, 2]
        )
        field[x] = field[x] + jnp.where(at, amount, 0.0)


def edges_kernel(field, ya, yb, xa, xb):
    even_y, even_x = even("gy"), even("gx")
    size_x, size_y = field.shape[0], field.shape[1]
    half = size_x // 2
    for part in range(2):
        x = slice(part * half, (part + 1) * half)
        first, last = field[x, 0:4, :], field[x, size_y - 4 : size_y, :]
        ya[:, part * 4 : part * 4 + 4, :] = jnp.where(even_y, last, first)
        yb[:, part * 4 : part * 4 + 4, :] = jnp.where(even_y, first, last)
    top = size_x - 4
    xa[...] = field[pl.ds(jnp.where(even_x, top, 0), 4)]
    xb[...] = field[pl.ds(jnp.where(even_x, 0, top), 4)]


def tables_kernel(size_x, size_y, cells, res, inject0, inject1):
    depth = inject0.shape[2]
    count = cells.shape[1]
    pad = jnp.zeros((count, HALF - 3), jnp.int32)
    rows = jnp.transpose(jnp.concatenate([cells[0], pad], axis=1).astype(F32))[0:8].astype(jnp.int32)
    x = rows[0:1, :] - lax.axis_index("gx") * size_x
    y = rows[1:2, :] - lax.axis_index("gy") * size_y
    inside = (x >= 0) & (x < size_x) & (y >= 0) & (y < size_y)
    place = jnp.where(inside, x * size_y + y, -1)
    deep = lax.broadcasted_iota(jnp.int32, (count, depth), 1) == cells[0, :, 2:3]
    parts = [three(jnp.where(deep, res[0, :, n : n + 1], 0.0)) for n in range(2)]
    spread = jnp.concatenate([jnp.concatenate([parts[0][i], parts[1][i]], axis=1) for i in range(3)], axis=0)
    half = size_x // 2
    for part in range(2):
        at = lax.broadcasted_iota(jnp.int32, (half * size_y, count), 0) + part * half * size_y
        flat = jnp.where(at == place, 1.0, 0.0).astype(jnp.bfloat16)
        done = product(jnp.concatenate([flat] * 3, axis=1), spread)
        for n, out in enumerate((inject0, inject1)):
            block = done[:, n * depth : (n + 1) * depth]
            out[part * half : (part + 1) * half] = block.reshape(half, size_y, depth)


def first_kernel(wave1, yb, ya, xb, xa, along_y, along_z, outer, lap1, flat, space):
    size_x, size_y = wave1.shape[0], wave1.shape[1]
    even_x = even("gx")
    flat_part(wave1, along_y, along_z, flat)
    half = size_x // 2
    for part in range(2):
        x = slice(part * half, (part + 1) * half)
        flat[x] = flat[x] + outer_part(ya, yb, 0, outer, part, size_y)
    space[4 : size_x + 4] = wave1[...]
    space[pl.ds(jnp.where(even_x, size_x + 4, 0), 4)] = xa[...]
    space[pl.ds(jnp.where(even_x, 0, size_x + 4), 4)] = xb[...]
    for x in range(size_x):
        for z in halves():
            lap = across(lambda i, z: space[i + 4, :, z], x, z)
            lap1[x, :, z] = lap + flat[x, :, z] * (1.0 / SCALE)


def second_kernel(
    offsets, cell, amp, tile, tile_a, tile_b, tile_ab, lap1, wave0, wave1, adj4,
    vel, wave2, image, ya, yb, xa, xb, column,
):
    size_x, size_y = wave1.shape[0], wave1.shape[1]
    me = lax.axis_index("shot")
    turn = jnp.where(even("shot"), 1, 3)
    for part, away in ((tile, 0), (tile_a, turn), (tile_ab, 2), (tile_b, 4 - turn)):
        column[lax.rem(me + away, 4)] = part[...]
    start = offsets[0]
    low = start // HALF
    shift_by = lax.rem(start, HALF)
    back = lax.rem(HALF - shift_by, HALF)
    third = jnp.minimum(low + 2, 3)

    def body(x, _):
        lane = lax.broadcasted_iota(jnp.int32, (size_y, HALF), 1)
        rolled = [pltpu.roll(column[i, x], back, 1) for i in (low, low + 1, third)]
        for h, z in enumerate(halves()):
            v = jnp.where(lane < HALF - shift_by, rolled[h], rolled[h + 1])
            vel[x, :, z] = v
            image[x, :, z] = v * adj4[x, :, z]
            wave2[x, :, z] = 2.0 * wave1[x, :, z] - wave0[x, :, z] + v * lap1[x, :, z]
        return 0

    lax.fori_loop(0, size_x, body, 0, unroll=4)
    add_source(cell, amp[0, 0], wave2)
    put_edges(wave2, 0, ya, yb, xa, xb, 0)
    put_edges(image, 4, ya, yb, xa, xb, 4)


def third_inner_kernel(
    wave1, wave2, adj4, adj5, vel, image, inject, along_y, along_z,
    lap2, wave3, adj3, flat, flat2,
):
    flat_part(wave2, along_y, along_z, flat)
    flat_part(image, along_y, along_z, flat2)
    for x in range(wave1.shape[0]):
        for z in halves():
            lap = across(within(wave2), x, z) + flat[x, :, z] * (1.0 / SCALE)
            lap2[x, :, z] = lap
            wave3[x, :, z] = 2.0 * wave2[x, :, z] - wave1[x, :, z] + vel[x, :, z] * lap
            adj = across(within(image), x, z) + flat2[x, :, z] * (1.0 / SCALE)
            adj3[x, :, z] = 2.0 * adj4[x, :, z] - adj5[x, :, z] + adj + inject[x, :, z]


def third_kernel(
    cell, amp, yb, ya, xb, xa, lap2_in, wave3_in, adj3_in, vel, outer,
    lap2, wave3, adj3, image3, pya, pyb, pxa, pxb, side, side2, extra, extra2,
):
    size_x, size_y = vel.shape[0], vel.shape[1]
    outer_parts(ya, yb, xa, xb, outer, size_x, size_y, (side, side2), (extra, extra2))

    def body(x, _):
        v = vel[x]
        lap2[x] = lap2_in[x] + extra[x]
        wave3[x] = wave3_in[x] + v * extra[x]
        adj = adj3_in[x] + extra2[x]
        adj3[x] = adj
        image3[x] = v * adj
        return 0

    lax.fori_loop(0, size_x, body, 0, unroll=4)
    add_source(cell, amp[0, 1], wave3)
    put_edges(wave3, 0, pya, pyb, pxa, pxb, 0)
    put_edges(image3, 4, pya, pyb, pxa, pxb, 4)


def fourth_inner_kernel(
    wave3, image3, adj3, adj4, lap1, lap2, inject, along_y, along_z,
    adj2, grad, flat, flat2,
):
    flat_part(wave3, along_y, along_z, flat)
    flat_part(image3, along_y, along_z, flat2)
    for x in range(wave3.shape[0]):
        for z in halves():
            lap3 = across(within(wave3), x, z) + flat[x, :, z] * (1.0 / SCALE)
            adj = across(within(image3), x, z) + flat2[x, :, z] * (1.0 / SCALE)
            old, mid = adj4[x, :, z], adj3[x, :, z]
            adj = 2.0 * mid - old + adj + inject[x, :, z]
            adj2[x, :, z] = adj
            grad[x, :, z] = old * lap3 + mid * lap2[x, :, z] + adj * lap1[x, :, z]


def fourth_kernel(
    offsets, yb, ya, xb, xa, grad_in, adj4, lap1, outer,
    far0, far1, near_a, near_b, own, extra2, side, side2, extra,
):
    size_x, size_y = adj4.shape[0], adj4.shape[1]
    outer_parts(ya, yb, xa, xb, outer, size_x, size_y, (side, side2), (extra, extra2))
    start = offsets[0]
    low = start // HALF
    shift_by = lax.rem(start, HALF)
    me = lax.axis_index("shot")
    turn = jnp.where(even("shot"), 1, 3)
    which = [lax.rem(me + away, 4) - low for away in (2, turn, 4 - turn, 0)]
    half = size_x // 2

    def body(x, far, at):
        lane = lax.broadcasted_iota(jnp.int32, (size_y, HALF), 1)
        rolled = []
        for z in halves():
            grad = grad_in[x, :, z] + adj4[x, :, z] * extra[x, :, z] + lap1[x, :, z] * extra2[x, :, z]
            rolled.append(pltpu.roll(grad, shift_by, 1))
        high = lane >= shift_by
        first = jnp.where(high, rolled[0], 0.0)
        second = jnp.where(high, rolled[1], rolled[0])
        third = jnp.where(high, 0.0, rolled[1])
        for n, (out, place) in zip(which, ((far, at), (near_a, x), (near_b, x), (own, x))):
            value = jnp.where(n == 0, first, jnp.where(n == 1, second, third))
            out[place] = jnp.where((n >= 0) & (n <= 2), value, 0.0)
        return 0

    lax.fori_loop(0, half, lambda x, _: body(x, far0, x), 0, unroll=4)
    lax.fori_loop(half, size_x, lambda x, _: body(x, far1, x - half), 0, unroll=4)


def adjoint_kernel(adj2_in, extra, adj2):
    adj2[...] = adj2_in[...] + extra[...]


def pass_kernel(first, near_in, far, near):
    planes = pl.ds(first, far.shape[0])
    near[planes] = near_in[planes] + far[...]


def sum_kernel(own, a, b, out):
    out[...] = own[...] + (a[...] + b[...])


def local(model_vel2, offsets, wave_prev, wave_cur, adj_cur, adj_next, src_cell, src_amp, rec_cell, rec_res):
    size_x, size_y, depth = wave_cur.shape[1:]
    wave0, wave1, adj4, adj5 = wave_prev[0], wave_cur[0], adj_cur[0], adj_next[0]
    block = shaped(size_x, size_y, depth)
    edge_y, edge_x = shaped(size_x, 8, depth), shaped(8, size_y, depth)
    tile, half = shaped(size_x, size_y, HALF), shaped(size_x // 2, size_y, HALF)
    whole = pltpu.VMEM((size_x, size_y, depth), F32)
    side = pltpu.VMEM((8, size_y, depth), F32)
    along_z, along_y, outer = difference_tables(size_y, depth, size_x // 2)

    tile_a, tile_b = swap_shot(model_vel2, 0), swap_shot(model_vel2, 1)
    tile_ab = swap_across(model_vel2)
    edges = call(
        edges_kernel, (shaped(size_x // 2, 8, depth),) * 2 + (shaped(4, size_y, depth),) * 2, n_in=1
    )(wave1)
    halos = exchange(edges)
    inject0, inject1 = call(functools.partial(tables_kernel, size_x, size_y), (block, block), n_in=2, room=8)(
        rec_cell, rec_res
    )
    lap1 = call(
        first_kernel, block, (whole, pltpu.VMEM((size_x + 8, size_y, depth), F32)), n_in=8, room=8
    )(wave1, *halos, along_y, along_z, outer)
    vel, wave2, image, *edges = call(
        second_kernel, (block,) * 3 + (edge_y,) * 2 + (edge_x,) * 2,
        (pltpu.VMEM((4, size_x, size_y, HALF), F32),), smem=3, n_in=8, room=8,
    )(offsets, src_cell, src_amp, model_vel2, tile_a, tile_b, tile_ab, lap1, wave0, wave1, adj4)
    halos = exchange(edges)
    inner = call(third_inner_kernel, (block,) * 3, (whole,) * 2, n_in=9, room=10)(
        wave1, wave2, adj4, adj5, vel, image, inject0, along_y, along_z
    )
    lap2, wave3, adj3, image3, *edges = call(
        third_kernel, (block,) * 4 + (edge_y,) * 2 + (edge_x,) * 2, (side, side, whole, whole), smem=2, n_in=9,
        room=10, aliases={6: 0, 7: 1, 8: 2},
    )(src_cell, src_amp, *halos, *inner, vel, outer)
    halos = exchange(edges)
    inner_adj2, inner_grad = call(fourth_inner_kernel, (block,) * 2, (whole,) * 2, n_in=9, room=10)(
        wave3, image3, adj3, adj4, lap1, lap2, inject1, along_y, along_z
    )
    far0, far1, near_a, near_b, own, extra = call(
        fourth_kernel, (half, half, tile, tile, tile, block), (side, side, whole), smem=1, n_in=8, room=10
    )(offsets, *halos, inner_grad, adj4, lap1, outer)
    from_a, from_b = swap_shot(far0, 0), swap_shot(far1, 1)
    near_b = call(functools.partial(pass_kernel, 0), tile, n_in=2, aliases={0: 0})(near_b, from_a)
    near_a = call(functools.partial(pass_kernel, size_x // 2), tile, n_in=2, aliases={0: 0})(near_a, from_b)
    got_b, got_a = swap_shot(near_b, 1), swap_shot(near_a, 0)
    adj2 = call(adjoint_kernel, block, n_in=2)(inner_adj2, extra)
    owned = call(sum_kernel, tile, n_in=3)(own, got_a, got_b)
    return owned, adj2[None]


def solution(mesh):
    return jax.shard_map(
        local,
        mesh=mesh,
        in_specs=(
            P("gx", "gy", "shot"),
            P("shot"),
            P("shot", "gx", "gy", None),
            P("shot", "gx", "gy", None),
            P("shot", "gx", "gy", None),
            P("shot", "gx", "gy", None),
            P("shot", None),
            P("shot", None),
            P("shot", None, None),
            P("shot", None, None),
        ),
        out_specs=(P("gx", "gy", "shot"), P("shot", "gx", "gy", None)),
        check_vma=False,
    )
```

```python
import functools

import jax
import jax.numpy as jnp
from jax import lax
from jax.experimental import pallas as pl
from jax.experimental.pallas import tpu as pltpu
from jax.sharding import PartitionSpec as P

COEF = (-205.0 / 72.0, 8.0 / 5.0, -1.0 / 5.0, 8.0 / 315.0, -1.0 / 560.0)
SCALE = 5040.0
WEIGHT = (0.0, 8064.0, -1008.0, 128.0, -9.0)
F32 = jnp.float32
HALF = 128


def swap(value, axis, odd):
    pairs = []
    for i in range(odd, lax.axis_size(axis) - 1, 2):
        pairs += [(i, i + 1), (i + 1, i)]
    return lax.ppermute(value, axis, pairs)


def swap_shot(value, odd):
    size = lax.axis_size("shot")
    pairs = []
    for i in range(odd, size, 2):
        pairs += [(i, (i + 1) % size), ((i + 1) % size, i)]
    return lax.ppermute(value, "shot", pairs)


def swap_across(value):
    size = lax.axis_size("shot")
    return lax.ppermute(value, "shot", [(i, (i + size // 2) % size) for i in range(size)])


def exchange(payload):
    ya, yb, xa, xb = payload
    return swap(yb, "gy", 1), swap(ya, "gy", 0), swap(xb, "gx", 1), swap(xa, "gx", 0)


def call(body, out_shape, scratch=(), smem=0, n_in=0, room=4, aliases=None, flops=0):
    vmem = pl.BlockSpec(memory_space=pltpu.VMEM)
    scal = pl.BlockSpec(memory_space=pltpu.SMEM)
    return pl.pallas_call(
        body,
        out_shape=out_shape,
        in_specs=[scal] * smem + [vmem] * n_in,
        out_specs=jax.tree.map(lambda _: vmem, out_shape),
        scratch_shapes=list(scratch),
        input_output_aliases=aliases or {},
        cost_estimate=pl.CostEstimate(flops=flops, bytes_accessed=0, transcendentals=0),
        compiler_params=pltpu.CompilerParams(vmem_limit_bytes=room << 20),
    )


def shaped(*dims):
    return jax.ShapeDtypeStruct(dims, F32)


def even(axis):
    return lax.rem(lax.axis_index(axis), 2) == 0


def weight(distance):
    distance = jnp.abs(distance)
    total = jnp.zeros(distance.shape, F32)
    for k in range(1, 5):
        total = jnp.where(distance == k, WEIGHT[k], total)
    return total


def three(value):
    first = value.astype(jnp.bfloat16)
    rest = value - first.astype(F32)
    second = rest.astype(jnp.bfloat16)
    return first, second, (rest - second.astype(F32)).astype(jnp.bfloat16)


def product(a, b):
    return jnp.dot(a, b, preferred_element_type=F32)


def flat_part(field, along_y, along_z, out):
    size_x, size_y, depth = field.shape
    chunk = along_y.shape[0] // size_y
    for at in range(0, size_x, chunk):
        parts = three(field[at : at + chunk].reshape(chunk * size_y, depth))
        total = sum(product(part, along_z[...]) + product(along_y[...], part) for part in parts)
        out[at : at + chunk] = total.reshape(chunk, size_y, depth)


def outer_part(ya, yb, at, outer, field, size_y):
    depth = ya.shape[2]
    chunk = outer.shape[1] // size_y
    a, b = (m[at : at + chunk].reshape(chunk * 8, depth) for m in (ya, yb))
    even_y = even("gy")
    below, above = three(jnp.where(even_y, b, a)), three(jnp.where(even_y, a, b))
    total = sum(product(outer[field], jnp.concatenate(pair, axis=0)) for pair in zip(below, above))
    return total.reshape(chunk, size_y, depth)


def outside_x(xa, xb, plane, out):
    even_x = even("gx")
    low = [jnp.where(even_x, xb[plane + i], xa[plane + i]) for i in range(4)]
    high = [jnp.where(even_x, xa[plane + i], xb[plane + i]) for i in range(4)]
    for i in range(4):
        first, last = 0.0, 0.0
        for k in range(i + 1, 5):
            first = first + COEF[k] * low[4 + i - k]
            last = last + COEF[k] * high[k - i - 1]
        out[i] = first
        out[7 - i] = last


def outer_parts(ya, yb, xa, xb, outer, size_x, size_y, sides, extras):
    chunk = outer.shape[1] // size_y
    for field, (side, extra) in enumerate(zip(sides, extras)):
        outside_x(xa, xb, 4 * field, side)
        for at in range(0, size_x, chunk):
            extra[at : at + chunk] = outer_part(ya, yb, at, outer, field, size_y) * (1.0 / SCALE)
        extra[0:4] = extra[0:4] + side[0:4]
        extra[size_x - 4 : size_x] = extra[size_x - 4 : size_x] + side[4:8]


def across(plane, x, z):
    total = (3.0 * COEF[0]) * plane(x, z)
    for k in range(1, 5):
        near = [p for p in (plane(x - k, z), plane(x + k, z)) if p is not None]
        if near:
            total = total + COEF[k] * sum(near[1:], near[0])
    return total


def within(field):
    size_x = field.shape[0]
    return lambda x, z: field[x, :, z] if 0 <= x < size_x else None


def halves():
    return [slice(h * HALF, (h + 1) * HALF) for h in range(2)]


def put_edges(field, row, ya, yb, xa, xb, plane):
    even_y, even_x = even("gy"), even("gx")
    size_x, size_y = field.shape[0], field.shape[1]
    first, last = field[:, 0:4, :], field[:, size_y - 4 : size_y, :]
    ya[:, row : row + 4, :] = jnp.where(even_y, last, first)
    yb[:, row : row + 4, :] = jnp.where(even_y, first, last)
    top = size_x - 4
    xa[plane : plane + 4] = field[pl.ds(jnp.where(even_x, top, 0), 4)]
    xb[plane : plane + 4] = field[pl.ds(jnp.where(even_x, 0, top), 4)]


def edges_kernel(field, ya, yb, xa, xb):
    even_y, even_x = even("gy"), even("gx")
    size_x, size_y = field.shape[0], field.shape[1]
    half = size_x // 2
    for part in range(2):
        x = slice(part * half, (part + 1) * half)
        first, last = field[x, 0:4, :], field[x, size_y - 4 : size_y, :]
        ya[:, part * 4 : part * 4 + 4, :] = jnp.where(even_y, last, first)
        yb[:, part * 4 : part * 4 + 4, :] = jnp.where(even_y, first, last)
    top = size_x - 4
    xa[...] = field[pl.ds(jnp.where(even_x, top, 0), 4)]
    xb[...] = field[pl.ds(jnp.where(even_x, 0, top), 4)]


def tables_kernel(
    size_x, size_y, cell, amp, cells, res, along_y, along_z, outer, source0, source1, inject0, inject1
):
    depth = inject0.shape[2]
    half = size_x // 2
    rows = half * size_y

    def index(shape, dim):
        return lax.broadcasted_iota(jnp.int32, shape, dim)

    along_z[...] = weight(index((depth, depth), 0) - index((depth, depth), 1)).astype(jnp.bfloat16)
    here, there = index((rows, rows), 0), index((rows, rows), 1)
    near = jnp.where(here // size_y == there // size_y, weight(here - there), 0.0)
    along_y[...] = near.astype(jnp.bfloat16)
    here, there = index((rows, half * 8), 0), index((rows, half * 8), 1)
    y, row = lax.rem(here, size_y), lax.rem(there, 4)
    below, above = weight(y - row + 4), weight(row + size_y - y)
    for field in range(2):
        use = (here // size_y == there // 8) & (lax.rem(there, 8) // 4 == field)
        both = jnp.concatenate([jnp.where(use, below, 0.0), jnp.where(use, above, 0.0)], axis=1)
        outer[field] = both.astype(jnp.bfloat16)

    base_x, base_y = lax.axis_index("gx") * size_x, lax.axis_index("gy") * size_y
    x, y = cell[0, 0] - base_x, cell[0, 1] - base_y
    source0[...] = jnp.zeros_like(source0)
    source1[...] = jnp.zeros_like(source1)

    @pl.when((x >= 0) & (x < size_x) & (y >= 0) & (y < size_y))
    def _():
        at = (index((size_y, depth), 0) == y) & (index((size_y, depth), 1) == cell[0, 2])
        source0[x] = jnp.where(at, amp[0, 0], 0.0)
        source1[x] = jnp.where(at, amp[0, 1], 0.0)

    count = cells.shape[1]
    x, y = cells[0:1, :] - base_x, cells[1:2, :] - base_y
    inside = (x >= 0) & (x < size_x) & (y >= 0) & (y < size_y)
    place = jnp.where(inside, x * size_y + y, -1)
    deep = index((depth, count), 0) == cells[2:3, :]
    parts = [three(jnp.where(deep, res[n : n + 1, :], 0.0)) for n in range(2)]
    for part in range(2):
        at = index((rows, count), 0) + part * rows
        flat = jnp.where(at == place, 1.0, 0.0).astype(jnp.bfloat16)
        for n, out in enumerate((inject0, inject1)):
            done = sum(
                lax.dot_general(flat, p, (((1,), (1,)), ((), ())), preferred_element_type=F32) for p in parts[n]
            )
            out[part * half : (part + 1) * half] = done.reshape(half, size_y, depth)


def first_inner_kernel(wave1, yb, ya, along_y, along_z, outer, lap1, flat):
    size_x, size_y = wave1.shape[0], wave1.shape[1]
    flat_part(wave1, along_y, along_z, flat)
    half = size_x // 2
    for part in range(2):
        x = slice(part * half, (part + 1) * half)
        flat[x] = flat[x] + outer_part(ya, yb, 0, outer, part, size_y)
    for x in range(size_x):
        for z in halves():
            lap1[x, :, z] = across(within(wave1), x, z) + flat[x, :, z] * (1.0 / SCALE)


def first_kernel(inner, xb, xa, lap1, side):
    size_x = lap1.shape[0]
    outside_x(xa, xb, 0, side)
    lap1[0:4] = inner[0:4] + side[0:4]
    lap1[size_x - 4 : size_x] = inner[size_x - 4 : size_x] + side[4:8]


def second_kernel(
    offsets, tile, tile_a, tile_b, tile_ab, lap1, wave0, wave1, adj4, source,
    vel, wave2, image, ya, yb, xa, xb, column,
):
    size_x, size_y = wave1.shape[0], wave1.shape[1]
    me = lax.axis_index("shot")
    turn = jnp.where(even("shot"), 1, 3)
    for part, away in ((tile, 0), (tile_a, turn), (tile_ab, 2), (tile_b, 4 - turn)):
        column[lax.rem(me + away, 4)] = part[...]
    start = offsets[0]
    low = start // HALF
    shift_by = lax.rem(start, HALF)
    back = lax.rem(HALF - shift_by, HALF)
    third = jnp.minimum(low + 2, 3)

    def body(x, _):
        lane = lax.broadcasted_iota(jnp.int32, (size_y, HALF), 1)
        rolled = [pltpu.roll(column[i, x], back, 1) for i in (low, low + 1, third)]
        for h, z in enumerate(halves()):
            v = jnp.where(lane < HALF - shift_by, rolled[h], rolled[h + 1])
            vel[x, :, z] = v
            image[x, :, z] = v * adj4[x, :, z]
            wave2[x, :, z] = 2.0 * wave1[x, :, z] - wave0[x, :, z] + v * lap1[x, :, z] + source[x, :, z]
        return 0

    lax.fori_loop(0, size_x, body, 0, unroll=4)
    put_edges(wave2, 0, ya, yb, xa, xb, 0)
    put_edges(image, 4, ya, yb, xa, xb, 4)


def third_inner_kernel(
    wave1, wave2, adj4, adj5, vel, image, source, inject, along_y, along_z,
    lap2, wave3, adj3, flat, flat2,
):
    flat_part(wave2, along_y, along_z, flat)
    flat_part(image, along_y, along_z, flat2)
    for x in range(wave1.shape[0]):
        for z in halves():
            lap = across(within(wave2), x, z) + flat[x, :, z] * (1.0 / SCALE)
            lap2[x, :, z] = lap
            wave3[x, :, z] = 2.0 * wave2[x, :, z] - wave1[x, :, z] + vel[x, :, z] * lap + source[x, :, z]
            adj = across(within(image), x, z) + flat2[x, :, z] * (1.0 / SCALE)
            adj3[x, :, z] = 2.0 * adj4[x, :, z] - adj5[x, :, z] + adj + inject[x, :, z]


def third_kernel(
    yb, ya, xb, xa, lap2_in, wave3_in, adj3_in, vel, outer,
    lap2, wave3, adj3, image3, pya, pyb, pxa, pxb, side, side2, extra, extra2,
):
    size_x, size_y = vel.shape[0], vel.shape[1]
    outer_parts(ya, yb, xa, xb, outer, size_x, size_y, (side, side2), (extra, extra2))

    def body(x, _):
        v = vel[x]
        lap2[x] = lap2_in[x] + extra[x]
        wave3[x] = wave3_in[x] + v * extra[x]
        adj = adj3_in[x] + extra2[x]
        adj3[x] = adj
        image3[x] = v * adj
        return 0

    lax.fori_loop(0, size_x, body, 0, unroll=4)
    put_edges(wave3, 0, pya, pyb, pxa, pxb, 0)
    put_edges(image3, 4, pya, pyb, pxa, pxb, 4)


def fourth_inner_kernel(
    wave3, image3, adj3, adj4, lap1, lap2, inject, along_y, along_z,
    adj2, grad, flat, flat2,
):
    flat_part(wave3, along_y, along_z, flat)
    flat_part(image3, along_y, along_z, flat2)
    for x in range(wave3.shape[0]):
        for z in halves():
            lap3 = across(within(wave3), x, z) + flat[x, :, z] * (1.0 / SCALE)
            adj = across(within(image3), x, z) + flat2[x, :, z] * (1.0 / SCALE)
            old, mid = adj4[x, :, z], adj3[x, :, z]
            adj = 2.0 * mid - old + adj + inject[x, :, z]
            adj2[x, :, z] = adj
            grad[x, :, z] = old * lap3 + mid * lap2[x, :, z] + adj * lap1[x, :, z]


def fourth_kernel(
    offsets, yb, ya, xb, xa, grad_in, adj4, lap1, outer,
    far0, far1, near_a, near_b, own, extra2, side, side2, extra,
):
    size_x, size_y = adj4.shape[0], adj4.shape[1]
    outer_parts(ya, yb, xa, xb, outer, size_x, size_y, (side, side2), (extra, extra2))
    start = offsets[0]
    low = start // HALF
    shift_by = lax.rem(start, HALF)
    me = lax.axis_index("shot")
    turn = jnp.where(even("shot"), 1, 3)
    which = [lax.rem(me + away, 4) - low for away in (2, turn, 4 - turn, 0)]
    half = size_x // 2

    def body(x, far, at):
        lane = lax.broadcasted_iota(jnp.int32, (size_y, HALF), 1)
        rolled = []
        for z in halves():
            grad = grad_in[x, :, z] + adj4[x, :, z] * extra[x, :, z] + lap1[x, :, z] * extra2[x, :, z]
            rolled.append(pltpu.roll(grad, shift_by, 1))
        high = lane >= shift_by
        first = jnp.where(high, rolled[0], 0.0)
        second = jnp.where(high, rolled[1], rolled[0])
        third = jnp.where(high, 0.0, rolled[1])
        for n, (out, place) in zip(which, ((far, at), (near_a, x), (near_b, x), (own, x))):
            value = jnp.where(n == 0, first, jnp.where(n == 1, second, third))
            out[place] = jnp.where((n >= 0) & (n <= 2), value, 0.0)
        return 0

    lax.fori_loop(0, half, lambda x, _: body(x, far0, x), 0, unroll=4)
    lax.fori_loop(half, size_x, lambda x, _: body(x, far1, x - half), 0, unroll=4)


def adjoint_kernel(adj2_in, extra, adj2):
    adj2[...] = adj2_in[...] + extra[...]


def pass_kernel(first, near_in, far, near):
    planes = pl.ds(first, far.shape[0])
    near[planes] = near_in[planes] + far[...]


def sum_kernel(own, a, b, out):
    out[...] = own[...] + (a[...] + b[...])


def local(model_vel2, offsets, wave_prev, wave_cur, adj_cur, adj_next, src_cell, src_amp, rec_cell, rec_res):
    size_x, size_y, depth = wave_cur.shape[1:]
    wave0, wave1, adj4, adj5 = wave_prev[0], wave_cur[0], adj_cur[0], adj_next[0]
    block = shaped(size_x, size_y, depth)
    edge_y, edge_x = shaped(size_x, 8, depth), shaped(8, size_y, depth)
    tile, half = shaped(size_x, size_y, HALF), shaped(size_x // 2, size_y, HALF)
    whole = pltpu.VMEM((size_x, size_y, depth), F32)
    side = pltpu.VMEM((8, size_y, depth), F32)
    rows, bf16 = size_x // 2 * size_y, jnp.bfloat16
    matrices = [
        jax.ShapeDtypeStruct(dims, bf16)
        for dims in ((rows, rows), (depth, depth), (2, rows, size_x // 2 * 16))
    ]

    tile_a, tile_b = swap_shot(model_vel2, 0), swap_shot(model_vel2, 1)
    tile_ab = swap_across(model_vel2)
    edges = call(
        edges_kernel, (shaped(size_x // 2, 8, depth),) * 2 + (shaped(4, size_y, depth),) * 2, n_in=1
    )(wave1)
    halos = exchange(edges)
    along_y, along_z, outer, source0, source1, inject0, inject1 = call(
        functools.partial(tables_kernel, size_x, size_y), (*matrices, block, block, block, block),
        smem=2, n_in=2, room=8,
    )(src_cell, src_amp, jnp.transpose(rec_cell[0]), jnp.transpose(rec_res[0]))
    yb, ya, xb, xa = halos
    lap1 = call(first_inner_kernel, block, (whole,), n_in=6, room=6)(wave1, yb, ya, along_y, along_z, outer)
    lap1 = call(first_kernel, block, (side,), n_in=3, aliases={0: 0})(lap1, xb, xa)
    vel, wave2, image, *edges = call(
        second_kernel, (block,) * 3 + (edge_y,) * 2 + (edge_x,) * 2,
        (pltpu.VMEM((4, size_x, size_y, HALF), F32),), smem=1, n_in=9, room=8,
    )(offsets, model_vel2, tile_a, tile_b, tile_ab, lap1, wave0, wave1, adj4, source0)
    halos = exchange(edges)
    inner = call(third_inner_kernel, (block,) * 3, (whole,) * 2, n_in=10, room=10)(
        wave1, wave2, adj4, adj5, vel, image, source1, inject0, along_y, along_z
    )
    lap2, wave3, adj3, image3, *edges = call(
        third_kernel, (block,) * 4 + (edge_y,) * 2 + (edge_x,) * 2, (side, side, whole, whole), n_in=9,
        room=10, aliases={4: 0, 5: 1, 6: 2},
    )(*halos, *inner, vel, outer)
    halos = exchange(edges)
    inner_adj2, inner_grad = call(fourth_inner_kernel, (block,) * 2, (whole,) * 2, n_in=9, room=10)(
        wave3, image3, adj3, adj4, lap1, lap2, inject1, along_y, along_z
    )
    far0, far1, near_a, near_b, own, extra = call(
        fourth_kernel, (half, half, tile, tile, tile, block), (side, side, whole), smem=1, n_in=8, room=10
    )(offsets, *halos, inner_grad, adj4, lap1, outer)
    from_a, from_b = swap_shot(far0, 0), swap_shot(far1, 1)
    near_b = call(functools.partial(pass_kernel, 0), tile, n_in=2, aliases={0: 0})(near_b, from_a)
    near_a = call(functools.partial(pass_kernel, size_x // 2), tile, n_in=2, aliases={0: 0})(near_a, from_b)
    got_b, got_a = swap_shot(near_b, 1), swap_shot(near_a, 0)
    adj2 = call(adjoint_kernel, block, n_in=2)(inner_adj2, extra)
    owned = call(sum_kernel, tile, n_in=3)(own, got_a, got_b)
    return owned, adj2[None]


def solution(mesh):
    return jax.shard_map(
        local,
        mesh=mesh,
        in_specs=(
            P("gx", "gy", "shot"),
            P("shot"),
            P("shot", "gx", "gy", None),
            P("shot", "gx", "gy", None),
            P("shot", "gx", "gy", None),
            P("shot", "gx", "gy", None),
            P("shot", None),
            P("shot", None),
            P("shot", None, None),
            P("shot", None, None),
        ),
        out_specs=(P("gx", "gy", "shot"), P("shot", "gx", "gy", None)),
        check_vma=False,
    )
```

```python
import functools

import jax
import jax.numpy as jnp
from jax import lax
from jax.experimental import pallas as pl
from jax.experimental.pallas import tpu as pltpu
from jax.sharding import PartitionSpec as P

COEF = (-205.0 / 72.0, 8.0 / 5.0, -1.0 / 5.0, 8.0 / 315.0, -1.0 / 560.0)
SCALE = 5040.0
WEIGHT = (0.0, 8064.0, -1008.0, 128.0, -9.0)
F32 = jnp.float32
HALF = 128


def swap(value, axis, odd):
    pairs = []
    for i in range(odd, lax.axis_size(axis) - 1, 2):
        pairs += [(i, i + 1), (i + 1, i)]
    return lax.ppermute(value, axis, pairs)


def swap_shot(value, odd):
    size = lax.axis_size("shot")
    pairs = []
    for i in range(odd, size, 2):
        pairs += [(i, (i + 1) % size), ((i + 1) % size, i)]
    return lax.ppermute(value, "shot", pairs)


def exchange(payload):
    ya, yb, xa, xb = payload
    return swap(yb, "gy", 1), swap(ya, "gy", 0), swap(xb, "gx", 1), swap(xa, "gx", 0)


def call(body, out_shape, scratch=(), smem=0, n_in=0, room=4, aliases=None, flops=0):
    vmem = pl.BlockSpec(memory_space=pltpu.VMEM)
    scal = pl.BlockSpec(memory_space=pltpu.SMEM)
    return pl.pallas_call(
        body,
        out_shape=out_shape,
        in_specs=[scal] * smem + [vmem] * n_in,
        out_specs=jax.tree.map(lambda _: vmem, out_shape),
        scratch_shapes=list(scratch),
        input_output_aliases=aliases or {},
        cost_estimate=pl.CostEstimate(flops=flops, bytes_accessed=0, transcendentals=0),
        compiler_params=pltpu.CompilerParams(vmem_limit_bytes=room << 20),
    )


def shaped(*dims):
    return jax.ShapeDtypeStruct(dims, F32)


def even(axis):
    return lax.rem(lax.axis_index(axis), 2) == 0


def weight(distance):
    distance = jnp.abs(distance)
    total = jnp.zeros(distance.shape, F32)
    for k in range(1, 5):
        total = jnp.where(distance == k, WEIGHT[k], total)
    return total


def three(value):
    first = value.astype(jnp.bfloat16)
    rest = value - first.astype(F32)
    second = rest.astype(jnp.bfloat16)
    return first, second, (rest - second.astype(F32)).astype(jnp.bfloat16)


def product(a, b):
    return jnp.dot(a, b, preferred_element_type=F32)


def flat_part(field, along_y, along_z, out):
    size_x, size_y, depth = field.shape
    chunk = along_y.shape[0] // size_y
    for at in range(0, size_x, chunk):
        parts = three(field[at : at + chunk].reshape(chunk * size_y, depth))
        total = sum(product(part, along_z[...]) + product(along_y[...], part) for part in parts)
        out[at : at + chunk] = total.reshape(chunk, size_y, depth)


def outer_part(ya, yb, at, outer, field, size_y):
    depth = ya.shape[2]
    chunk = outer.shape[1] // size_y
    a, b = (m[at : at + chunk].reshape(chunk * 8, depth) for m in (ya, yb))
    even_y = even("gy")
    below, above = three(jnp.where(even_y, b, a)), three(jnp.where(even_y, a, b))
    total = sum(product(outer[field], jnp.concatenate(pair, axis=0)) for pair in zip(below, above))
    return total.reshape(chunk, size_y, depth)


def outside_x(xa, xb, plane, out):
    even_x = even("gx")
    low = [jnp.where(even_x, xb[plane + i], xa[plane + i]) for i in range(4)]
    high = [jnp.where(even_x, xa[plane + i], xb[plane + i]) for i in range(4)]
    for i in range(4):
        first, last = 0.0, 0.0
        for k in range(i + 1, 5):
            first = first + COEF[k] * low[4 + i - k]
            last = last + COEF[k] * high[k - i - 1]
        out[i] = first
        out[7 - i] = last


def outer_parts(ya, yb, xa, xb, outer, size_x, size_y, sides, extras):
    chunk = outer.shape[1] // size_y
    for field, (side, extra) in enumerate(zip(sides, extras)):
        outside_x(xa, xb, 4 * field, side)
        for at in range(0, size_x, chunk):
            extra[at : at + chunk] = outer_part(ya, yb, at, outer, field, size_y) * (1.0 / SCALE)
        extra[0:4] = extra[0:4] + side[0:4]
        extra[size_x - 4 : size_x] = extra[size_x - 4 : size_x] + side[4:8]


def across(plane, x, z):
    total = (3.0 * COEF[0]) * plane(x, z)
    for k in range(1, 5):
        near = [p for p in (plane(x - k, z), plane(x + k, z)) if p is not None]
        if near:
            total = total + COEF[k] * sum(near[1:], near[0])
    return total


def within(field):
    size_x = field.shape[0]
    return lambda x, z: field[x, :, z] if 0 <= x < size_x else None


def halves():
    return [slice(h * HALF, (h + 1) * HALF) for h in range(2)]


def put_edges(field, row, ya, yb, xa, xb, plane):
    even_y, even_x = even("gy"), even("gx")
    size_x, size_y = field.shape[0], field.shape[1]
    first, last = field[:, 0:4, :], field[:, size_y - 4 : size_y, :]
    ya[:, row : row + 4, :] = jnp.where(even_y, last, first)
    yb[:, row : row + 4, :] = jnp.where(even_y, first, last)
    top = size_x - 4
    xa[plane : plane + 4] = field[pl.ds(jnp.where(even_x, top, 0), 4)]
    xb[plane : plane + 4] = field[pl.ds(jnp.where(even_x, 0, top), 4)]


def after_kernel(value, other, out):
    out[...] = value[...]


def edges_kernel(field, ya, yb, xa, xb):
    even_y, even_x = even("gy"), even("gx")
    size_x, size_y = field.shape[0], field.shape[1]
    half = size_x // 2
    for part in range(2):
        x = slice(part * half, (part + 1) * half)
        first, last = field[x, 0:4, :], field[x, size_y - 4 : size_y, :]
        ya[:, part * 4 : part * 4 + 4, :] = jnp.where(even_y, last, first)
        yb[:, part * 4 : part * 4 + 4, :] = jnp.where(even_y, first, last)
    top = size_x - 4
    xa[...] = field[pl.ds(jnp.where(even_x, top, 0), 4)]
    xb[...] = field[pl.ds(jnp.where(even_x, 0, top), 4)]


def tables_kernel(
    size_x, size_y, cell, amp, cells, res, along_y, along_z, outer, source0, source1, inject0, inject1
):
    depth = inject0.shape[2]
    half = size_x // 2
    rows = half * size_y

    def index(shape, dim):
        return lax.broadcasted_iota(jnp.int32, shape, dim)

    along_z[...] = weight(index((depth, depth), 0) - index((depth, depth), 1)).astype(jnp.bfloat16)
    here, there = index((rows, rows), 0), index((rows, rows), 1)
    near = jnp.where(here // size_y == there // size_y, weight(here - there), 0.0)
    along_y[...] = near.astype(jnp.bfloat16)
    here, there = index((rows, half * 8), 0), index((rows, half * 8), 1)
    y, row = lax.rem(here, size_y), lax.rem(there, 4)
    below, above = weight(y - row + 4), weight(row + size_y - y)
    for field in range(2):
        use = (here // size_y == there // 8) & (lax.rem(there, 8) // 4 == field)
        both = jnp.concatenate([jnp.where(use, below, 0.0), jnp.where(use, above, 0.0)], axis=1)
        outer[field] = both.astype(jnp.bfloat16)

    base_x, base_y = lax.axis_index("gx") * size_x, lax.axis_index("gy") * size_y
    x, y = cell[0, 0] - base_x, cell[0, 1] - base_y
    source0[...] = jnp.zeros_like(source0)
    source1[...] = jnp.zeros_like(source1)

    @pl.when((x >= 0) & (x < size_x) & (y >= 0) & (y < size_y))
    def _():
        at = (index((size_y, depth), 0) == y) & (index((size_y, depth), 1) == cell[0, 2])
        source0[x] = jnp.where(at, amp[0, 0], 0.0)
        source1[x] = jnp.where(at, amp[0, 1], 0.0)

    count = cells.shape[1]
    x, y = cells[0:1, :] - base_x, cells[1:2, :] - base_y
    inside = (x >= 0) & (x < size_x) & (y >= 0) & (y < size_y)
    place = jnp.where(inside, x * size_y + y, -1)
    deep = index((depth, count), 0) == cells[2:3, :]
    parts = [three(jnp.where(deep, res[n : n + 1, :], 0.0)) for n in range(2)]
    for part in range(2):
        at = index((rows, count), 0) + part * rows
        flat = jnp.where(at == place, 1.0, 0.0).astype(jnp.bfloat16)
        for n, out in enumerate((inject0, inject1)):
            done = sum(
                lax.dot_general(flat, p, (((1,), (1,)), ((), ())), preferred_element_type=F32) for p in parts[n]
            )
            out[part * half : (part + 1) * half] = done.reshape(half, size_y, depth)


def first_inner_kernel(wave1, yb, ya, along_y, along_z, outer, lap1, flat):
    size_x, size_y = wave1.shape[0], wave1.shape[1]
    flat_part(wave1, along_y, along_z, flat)
    half = size_x // 2
    for part in range(2):
        x = slice(part * half, (part + 1) * half)
        flat[x] = flat[x] + outer_part(ya, yb, 0, outer, part, size_y)
    for x in range(size_x):
        for z in halves():
            lap1[x, :, z] = across(within(wave1), x, z) + flat[x, :, z] * (1.0 / SCALE)


def first_kernel(inner, xb, xa, lap1, side):
    size_x = lap1.shape[0]
    outside_x(xa, xb, 0, side)
    lap1[0:4] = inner[0:4] + side[0:4]
    lap1[size_x - 4 : size_x] = inner[size_x - 4 : size_x] + side[4:8]


def second_kernel(
    offsets, tile, tile_a, tile_b, tile_ab, lap1, wave0, wave1, adj4, source,
    vel, wave2, image, ya, yb, xa, xb, column,
):
    size_x, size_y = wave1.shape[0], wave1.shape[1]
    me = lax.axis_index("shot")
    turn = jnp.where(even("shot"), 1, 3)
    for part, away in ((tile, 0), (tile_a, turn), (tile_ab, 2), (tile_b, 4 - turn)):
        column[lax.rem(me + away, 4)] = part[...]
    start = offsets[0]
    low = start // HALF
    shift_by = lax.rem(start, HALF)
    back = lax.rem(HALF - shift_by, HALF)
    third = jnp.minimum(low + 2, 3)

    def body(x, _):
        lane = lax.broadcasted_iota(jnp.int32, (size_y, HALF), 1)
        rolled = [pltpu.roll(column[i, x], back, 1) for i in (low, low + 1, third)]
        for h, z in enumerate(halves()):
            v = jnp.where(lane < HALF - shift_by, rolled[h], rolled[h + 1])
            vel[x, :, z] = v
            image[x, :, z] = v * adj4[x, :, z]
            wave2[x, :, z] = 2.0 * wave1[x, :, z] - wave0[x, :, z] + v * lap1[x, :, z] + source[x, :, z]
        return 0

    lax.fori_loop(0, size_x, body, 0, unroll=4)
    put_edges(wave2, 0, ya, yb, xa, xb, 0)
    put_edges(image, 4, ya, yb, xa, xb, 4)


def third_inner_kernel(
    wave1, wave2, adj4, adj5, vel, image, source, inject, along_y, along_z,
    lap2, wave3, adj3, flat, flat2,
):
    flat_part(wave2, along_y, along_z, flat)
    flat_part(image, along_y, along_z, flat2)
    for x in range(wave1.shape[0]):
        for z in halves():
            lap = across(within(wave2), x, z) + flat[x, :, z] * (1.0 / SCALE)
            lap2[x, :, z] = lap
            wave3[x, :, z] = 2.0 * wave2[x, :, z] - wave1[x, :, z] + vel[x, :, z] * lap + source[x, :, z]
            adj = across(within(image), x, z) + flat2[x, :, z] * (1.0 / SCALE)
            adj3[x, :, z] = 2.0 * adj4[x, :, z] - adj5[x, :, z] + adj + inject[x, :, z]


def third_kernel(
    yb, ya, xb, xa, lap2_in, wave3_in, adj3_in, vel, outer,
    lap2, wave3, adj3, image3, pya, pyb, pxa, pxb, side, side2, extra, extra2,
):
    size_x, size_y = vel.shape[0], vel.shape[1]
    outer_parts(ya, yb, xa, xb, outer, size_x, size_y, (side, side2), (extra, extra2))

    def body(x, _):
        v = vel[x]
        lap2[x] = lap2_in[x] + extra[x]
        wave3[x] = wave3_in[x] + v * extra[x]
        adj = adj3_in[x] + extra2[x]
        adj3[x] = adj
        image3[x] = v * adj
        return 0

    lax.fori_loop(0, size_x, body, 0, unroll=4)
    put_edges(wave3, 0, pya, pyb, pxa, pxb, 0)
    put_edges(image3, 4, pya, pyb, pxa, pxb, 4)


def fourth_inner_kernel(
    wave3, image3, adj3, adj4, lap1, lap2, inject, along_y, along_z,
    adj2, grad, flat, flat2,
):
    flat_part(wave3, along_y, along_z, flat)
    flat_part(image3, along_y, along_z, flat2)
    for x in range(wave3.shape[0]):
        for z in halves():
            lap3 = across(within(wave3), x, z) + flat[x, :, z] * (1.0 / SCALE)
            adj = across(within(image3), x, z) + flat2[x, :, z] * (1.0 / SCALE)
            old, mid = adj4[x, :, z], adj3[x, :, z]
            adj = 2.0 * mid - old + adj + inject[x, :, z]
            adj2[x, :, z] = adj
            grad[x, :, z] = old * lap3 + mid * lap2[x, :, z] + adj * lap1[x, :, z]


def fourth_kernel(
    offsets, yb, ya, xb, xa, grad_in, adj4, lap1, outer,
    far0, far1, near_a0, near_a1, near_b, own, extra2, side, side2, extra,
):
    size_x, size_y = adj4.shape[0], adj4.shape[1]
    outer_parts(ya, yb, xa, xb, outer, size_x, size_y, (side, side2), (extra, extra2))
    start = offsets[0]
    low = start // HALF
    shift_by = lax.rem(start, HALF)
    me = lax.axis_index("shot")
    turn = jnp.where(even("shot"), 1, 3)
    which = [lax.rem(me + away, 4) - low for away in (2, turn, 4 - turn, 0)]
    half = size_x // 2

    def body(x, far, near_a, at):
        lane = lax.broadcasted_iota(jnp.int32, (size_y, HALF), 1)
        rolled = []
        for z in halves():
            grad = grad_in[x, :, z] + adj4[x, :, z] * extra[x, :, z] + lap1[x, :, z] * extra2[x, :, z]
            rolled.append(pltpu.roll(grad, shift_by, 1))
        high = lane >= shift_by
        first = jnp.where(high, rolled[0], 0.0)
        second = jnp.where(high, rolled[1], rolled[0])
        third = jnp.where(high, 0.0, rolled[1])
        for n, (out, place) in zip(which, ((far, at), (near_a, at), (near_b, x), (own, x))):
            value = jnp.where(n == 0, first, jnp.where(n == 1, second, third))
            out[place] = jnp.where((n >= 0) & (n <= 2), value, 0.0)
        return 0

    lax.fori_loop(0, half, lambda x, _: body(x, far0, near_a0, x), 0, unroll=4)
    lax.fori_loop(half, size_x, lambda x, _: body(x, far1, near_a1, x - half), 0, unroll=4)


def adjoint_kernel(adj2_in, extra, adj2):
    adj2[...] = adj2_in[...] + extra[...]


def pass_lower_kernel(near_in, far, near):
    planes = pl.ds(0, far.shape[0])
    near[planes] = near_in[planes] + far[...]


def pass_kernel(near, far, out):
    out[...] = near[...] + far[...]


def sum_kernel(own, a0, a1, b, out):
    half = a0.shape[0]
    out[0:half] = own[0:half] + (a0[...] + b[0:half])
    out[half:] = own[half:] + (a1[...] + b[half:])


def local(model_vel2, offsets, wave_prev, wave_cur, adj_cur, adj_next, src_cell, src_amp, rec_cell, rec_res):
    size_x, size_y, depth = wave_cur.shape[1:]
    wave0, wave1, adj4, adj5 = wave_prev[0], wave_cur[0], adj_cur[0], adj_next[0]
    block = shaped(size_x, size_y, depth)
    edge_y, edge_x = shaped(size_x, 8, depth), shaped(8, size_y, depth)
    tile, half = shaped(size_x, size_y, HALF), shaped(size_x // 2, size_y, HALF)
    whole = pltpu.VMEM((size_x, size_y, depth), F32)
    side = pltpu.VMEM((8, size_y, depth), F32)
    rows, bf16 = size_x // 2 * size_y, jnp.bfloat16
    matrices = [
        jax.ShapeDtypeStruct(dims, bf16)
        for dims in ((rows, rows), (depth, depth), (2, rows, size_x // 2 * 16))
    ]

    tile_a, tile_b = swap_shot(model_vel2, 0), swap_shot(model_vel2, 1)
    tile_ab = swap_shot(call(after_kernel, tile, n_in=2, room=2)(tile_b, tile_a), 0)
    edges = call(
        edges_kernel, (shaped(size_x // 2, 8, depth),) * 2 + (shaped(4, size_y, depth),) * 2, n_in=1
    )(wave1)
    halos = exchange(edges)
    along_y, along_z, outer, source0, source1, inject0, inject1 = call(
        functools.partial(tables_kernel, size_x, size_y), (*matrices, block, block, block, block),
        smem=2, n_in=2, room=8,
    )(src_cell, src_amp, jnp.transpose(rec_cell[0]), jnp.transpose(rec_res[0]))
    yb, ya, xb, xa = halos
    lap1 = call(first_inner_kernel, block, (whole,), n_in=6, room=6, flops=2000000000)(wave1, yb, ya, along_y, along_z, outer)
    lap1 = call(first_kernel, block, (side,), n_in=3, aliases={0: 0})(lap1, xb, xa)
    vel, wave2, image, *edges = call(
        second_kernel, (block,) * 3 + (edge_y,) * 2 + (edge_x,) * 2,
        (pltpu.VMEM((4, size_x, size_y, HALF), F32),), smem=1, n_in=9, room=8,
    )(offsets, model_vel2, tile_a, tile_b, tile_ab, lap1, wave0, wave1, adj4, source0)
    halos = exchange(edges)
    inner = call(third_inner_kernel, (block,) * 3, (whole,) * 2, n_in=10, room=10)(
        wave1, wave2, adj4, adj5, vel, image, source1, inject0, along_y, along_z
    )
    lap2, wave3, adj3, image3, *edges = call(
        third_kernel, (block,) * 4 + (edge_y,) * 2 + (edge_x,) * 2, (side, side, whole, whole), n_in=9,
        room=10, aliases={4: 0, 5: 1, 6: 2},
    )(*halos, *inner, vel, outer)
    halos = exchange(edges)
    inner_adj2, inner_grad = call(fourth_inner_kernel, (block,) * 2, (whole,) * 2, n_in=9, room=10)(
        wave3, image3, adj3, adj4, lap1, lap2, inject1, along_y, along_z
    )
    far0, far1, near_a0, near_a1, near_b, own, extra = call(
        fourth_kernel, (half, half, half, half, tile, tile, block), (side, side, whole), smem=1, n_in=8, room=10
    )(offsets, *halos, inner_grad, adj4, lap1, outer)
    from_a, from_b = swap_shot(far0, 0), swap_shot(far1, 1)
    got_a0 = swap_shot(near_a0, 0)
    got_b = swap_shot(call(pass_lower_kernel, tile, n_in=2, aliases={0: 0})(near_b, from_a), 1)
    got_a1 = swap_shot(call(pass_kernel, half, n_in=2)(near_a1, from_b), 0)
    adj2 = call(adjoint_kernel, block, n_in=2)(inner_adj2, extra)
    owned = call(sum_kernel, tile, n_in=4)(own, got_a0, got_a1, got_b)
    return owned, adj2[None]


def solution(mesh):
    return jax.shard_map(
        local,
        mesh=mesh,
        in_specs=(
            P("gx", "gy", "shot"),
            P("shot"),
            P("shot", "gx", "gy", None),
            P("shot", "gx", "gy", None),
            P("shot", "gx", "gy", None),
            P("shot", "gx", "gy", None),
            P("shot", None),
            P("shot", None),
            P("shot", None, None),
            P("shot", None, None),
        ),
        out_specs=(P("gx", "gy", "shot"), P("shot", "gx", "gy", None)),
        check_vma=False,
    )
```

```python
import functools

import jax
import jax.numpy as jnp
from jax import lax
from jax.experimental import pallas as pl
from jax.experimental.pallas import tpu as pltpu
from jax.sharding import PartitionSpec as P

COEF = (-205.0 / 72.0, 8.0 / 5.0, -1.0 / 5.0, 8.0 / 315.0, -1.0 / 560.0)
SCALE = 5040.0
WEIGHT = (0.0, 8064.0, -1008.0, 128.0, -9.0)
F32 = jnp.float32
HALF = 128


def swap(value, axis, odd):
    pairs = []
    for i in range(odd, lax.axis_size(axis) - 1, 2):
        pairs += [(i, i + 1), (i + 1, i)]
    return lax.ppermute(value, axis, pairs)


def swap_shot(value, odd):
    size = lax.axis_size("shot")
    pairs = []
    for i in range(odd, size, 2):
        pairs += [(i, (i + 1) % size), ((i + 1) % size, i)]
    return lax.ppermute(value, "shot", pairs)


def exchange(payload):
    ya, yb, xa, xb = payload
    return swap(yb, "gy", 1), swap(ya, "gy", 0), swap(xb, "gx", 1), swap(xa, "gx", 0)


def call(body, out_shape, scratch=(), smem=0, n_in=0, room=4, aliases=None, flops=0):
    vmem = pl.BlockSpec(memory_space=pltpu.VMEM)
    scal = pl.BlockSpec(memory_space=pltpu.SMEM)
    return pl.pallas_call(
        body,
        out_shape=out_shape,
        in_specs=[scal] * smem + [vmem] * n_in,
        out_specs=jax.tree.map(lambda _: vmem, out_shape),
        scratch_shapes=list(scratch),
        input_output_aliases=aliases or {},
        cost_estimate=pl.CostEstimate(flops=flops, bytes_accessed=0, transcendentals=0),
        compiler_params=pltpu.CompilerParams(vmem_limit_bytes=room << 20),
    )


def shaped(*dims):
    return jax.ShapeDtypeStruct(dims, F32)


def even(axis):
    return lax.rem(lax.axis_index(axis), 2) == 0


def weight(distance):
    distance = jnp.abs(distance)
    total = jnp.zeros(distance.shape, F32)
    for k in range(1, 5):
        total = jnp.where(distance == k, WEIGHT[k], total)
    return total


def three(value):
    first = value.astype(jnp.bfloat16)
    rest = value - first.astype(F32)
    second = rest.astype(jnp.bfloat16)
    return first, second, (rest - second.astype(F32)).astype(jnp.bfloat16)


def product(a, b):
    return jnp.dot(a, b, preferred_element_type=F32)


def flat_part(field, along_y, along_z, out):
    size_x, size_y, depth = field.shape
    chunk = along_y.shape[0] // size_y
    for at in range(0, size_x, chunk):
        parts = three(field[at : at + chunk].reshape(chunk * size_y, depth))
        total = sum(product(part, along_z[...]) + product(along_y[...], part) for part in parts)
        out[at : at + chunk] = total.reshape(chunk, size_y, depth)


def outer_part(ya, yb, at, outer, field, size_y):
    depth = ya.shape[2]
    chunk = outer.shape[1] // size_y
    a, b = (m[at : at + chunk].reshape(chunk * 8, depth) for m in (ya, yb))
    even_y = even("gy")
    below, above = three(jnp.where(even_y, b, a)), three(jnp.where(even_y, a, b))
    total = sum(product(outer[field], jnp.concatenate(pair, axis=0)) for pair in zip(below, above))
    return total.reshape(chunk, size_y, depth)


def outside_x(xa, xb, plane, out):
    even_x = even("gx")
    low = [jnp.where(even_x, xb[plane + i], xa[plane + i]) for i in range(4)]
    high = [jnp.where(even_x, xa[plane + i], xb[plane + i]) for i in range(4)]
    for i in range(4):
        first, last = 0.0, 0.0
        for k in range(i + 1, 5):
            first = first + COEF[k] * low[4 + i - k]
            last = last + COEF[k] * high[k - i - 1]
        out[i] = first
        out[7 - i] = last


def outer_parts(ya, yb, xa, xb, outer, size_x, size_y, sides, extras):
    chunk = outer.shape[1] // size_y
    for field, (side, extra) in enumerate(zip(sides, extras)):
        outside_x(xa, xb, 4 * field, side)
        for at in range(0, size_x, chunk):
            extra[at : at + chunk] = outer_part(ya, yb, at, outer, field, size_y) * (1.0 / SCALE)
        extra[0:4] = extra[0:4] + side[0:4]
        extra[size_x - 4 : size_x] = extra[size_x - 4 : size_x] + side[4:8]


def across(plane, x, z):
    total = (3.0 * COEF[0]) * plane(x, z)
    for k in range(1, 5):
        near = [p for p in (plane(x - k, z), plane(x + k, z)) if p is not None]
        if near:
            total = total + COEF[k] * sum(near[1:], near[0])
    return total


def within(field):
    size_x = field.shape[0]
    return lambda x, z: field[x, :, z] if 0 <= x < size_x else None


def halves():
    return [slice(h * HALF, (h + 1) * HALF) for h in range(2)]


def put_edges(field, row, ya, yb, xa, xb, plane):
    even_y, even_x = even("gy"), even("gx")
    size_x, size_y = field.shape[0], field.shape[1]
    first, last = field[:, 0:4, :], field[:, size_y - 4 : size_y, :]
    ya[:, row : row + 4, :] = jnp.where(even_y, last, first)
    yb[:, row : row + 4, :] = jnp.where(even_y, first, last)
    top = size_x - 4
    xa[plane : plane + 4] = field[pl.ds(jnp.where(even_x, top, 0), 4)]
    xb[plane : plane + 4] = field[pl.ds(jnp.where(even_x, 0, top), 4)]


def pair_kernel(first, second, out):
    half = first.shape[0]
    out[0:half] = first[...]
    out[half:] = second[...]


def edges_kernel(field, ya, yb, xa, xb):
    even_y, even_x = even("gy"), even("gx")
    size_x, size_y = field.shape[0], field.shape[1]
    half = size_x // 2
    for part in range(2):
        x = slice(part * half, (part + 1) * half)
        first, last = field[x, 0:4, :], field[x, size_y - 4 : size_y, :]
        ya[:, part * 4 : part * 4 + 4, :] = jnp.where(even_y, last, first)
        yb[:, part * 4 : part * 4 + 4, :] = jnp.where(even_y, first, last)
    top = size_x - 4
    xa[...] = field[pl.ds(jnp.where(even_x, top, 0), 4)]
    xb[...] = field[pl.ds(jnp.where(even_x, 0, top), 4)]


def tables_kernel(
    size_x, size_y, cell, amp, cells, res, along_y, along_z, outer, source0, source1, inject0, inject1
):
    depth = inject0.shape[2]
    half = size_x // 2
    rows = half * size_y

    def index(shape, dim):
        return lax.broadcasted_iota(jnp.int32, shape, dim)

    along_z[...] = weight(index((depth, depth), 0) - index((depth, depth), 1)).astype(jnp.bfloat16)
    here, there = index((rows, rows), 0), index((rows, rows), 1)
    near = jnp.where(here // size_y == there // size_y, weight(here - there), 0.0)
    along_y[...] = near.astype(jnp.bfloat16)
    here, there = index((rows, half * 8), 0), index((rows, half * 8), 1)
    y, row = lax.rem(here, size_y), lax.rem(there, 4)
    below, above = weight(y - row + 4), weight(row + size_y - y)
    for field in range(2):
        use = (here // size_y == there // 8) & (lax.rem(there, 8) // 4 == field)
        both = jnp.concatenate([jnp.where(use, below, 0.0), jnp.where(use, above, 0.0)], axis=1)
        outer[field] = both.astype(jnp.bfloat16)

    base_x, base_y = lax.axis_index("gx") * size_x, lax.axis_index("gy") * size_y
    x, y = cell[0, 0] - base_x, cell[0, 1] - base_y
    source0[...] = jnp.zeros_like(source0)
    source1[...] = jnp.zeros_like(source1)

    @pl.when((x >= 0) & (x < size_x) & (y >= 0) & (y < size_y))
    def _():
        at = (index((size_y, depth), 0) == y) & (index((size_y, depth), 1) == cell[0, 2])
        source0[x] = jnp.where(at, amp[0, 0], 0.0)
        source1[x] = jnp.where(at, amp[0, 1], 0.0)

    count = cells.shape[1]
    x, y = cells[0:1, :] - base_x, cells[1:2, :] - base_y
    inside = (x >= 0) & (x < size_x) & (y >= 0) & (y < size_y)
    place = jnp.where(inside, x * size_y + y, -1)
    deep = index((depth, count), 0) == cells[2:3, :]
    parts = [three(jnp.where(deep, res[n : n + 1, :], 0.0)) for n in range(2)]
    for part in range(2):
        at = index((rows, count), 0) + part * rows
        flat = jnp.where(at == place, 1.0, 0.0).astype(jnp.bfloat16)
        for n, out in enumerate((inject0, inject1)):
            done = sum(
                lax.dot_general(flat, p, (((1,), (1,)), ((), ())), preferred_element_type=F32) for p in parts[n]
            )
            out[part * half : (part + 1) * half] = done.reshape(half, size_y, depth)


def first_inner_kernel(wave1, yb, ya, along_y, along_z, outer, lap1, flat):
    size_x, size_y = wave1.shape[0], wave1.shape[1]
    flat_part(wave1, along_y, along_z, flat)
    half = size_x // 2
    for part in range(2):
        x = slice(part * half, (part + 1) * half)
        flat[x] = flat[x] + outer_part(ya, yb, 0, outer, part, size_y)
    for x in range(size_x):
        for z in halves():
            lap1[x, :, z] = across(within(wave1), x, z) + flat[x, :, z] * (1.0 / SCALE)


def first_kernel(inner, xb, xa, lap1, side):
    size_x = lap1.shape[0]
    outside_x(xa, xb, 0, side)
    lap1[0:4] = inner[0:4] + side[0:4]
    lap1[size_x - 4 : size_x] = inner[size_x - 4 : size_x] + side[4:8]


def second_kernel(
    offsets, tile, tile_a, pair, lap1, wave0, wave1, adj4, source,
    vel, wave2, image, ya, yb, xa, xb, column,
):
    size_x, size_y = wave1.shape[0], wave1.shape[1]
    me = lax.axis_index("shot")
    turn = jnp.where(even("shot"), 1, 3)
    column[me] = tile[...]
    column[lax.rem(me + turn, 4)] = tile_a[...]
    column[lax.rem(me + 4 - turn, 4)] = pair[0:size_x]
    column[lax.rem(me + 2, 4)] = pair[size_x:]
    start = offsets[0]
    low = start // HALF
    shift_by = lax.rem(start, HALF)
    back = lax.rem(HALF - shift_by, HALF)
    third = jnp.minimum(low + 2, 3)

    def body(x, _):
        lane = lax.broadcasted_iota(jnp.int32, (size_y, HALF), 1)
        rolled = [pltpu.roll(column[i, x], back, 1) for i in (low, low + 1, third)]
        for h, z in enumerate(halves()):
            v = jnp.where(lane < HALF - shift_by, rolled[h], rolled[h + 1])
            vel[x, :, z] = v
            image[x, :, z] = v * adj4[x, :, z]
            wave2[x, :, z] = 2.0 * wave1[x, :, z] - wave0[x, :, z] + v * lap1[x, :, z] + source[x, :, z]
        return 0

    lax.fori_loop(0, size_x, body, 0, unroll=4)
    put_edges(wave2, 0, ya, yb, xa, xb, 0)
    put_edges(image, 4, ya, yb, xa, xb, 4)


def third_inner_kernel(
    wave1, wave2, adj4, adj5, vel, image, source, inject, along_y, along_z,
    lap2, wave3, adj3, flat, flat2,
):
    flat_part(wave2, along_y, along_z, flat)
    flat_part(image, along_y, along_z, flat2)
    for x in range(wave1.shape[0]):
        for z in halves():
            lap = across(within(wave2), x, z) + flat[x, :, z] * (1.0 / SCALE)
            lap2[x, :, z] = lap
            wave3[x, :, z] = 2.0 * wave2[x, :, z] - wave1[x, :, z] + vel[x, :, z] * lap + source[x, :, z]
            adj = across(within(image), x, z) + flat2[x, :, z] * (1.0 / SCALE)
            adj3[x, :, z] = 2.0 * adj4[x, :, z] - adj5[x, :, z] + adj + inject[x, :, z]


def third_kernel(
    yb, ya, xb, xa, lap2_in, wave3_in, adj3_in, vel, outer,
    lap2, wave3, adj3, image3, pya, pyb, pxa, pxb, side, side2, extra, extra2,
):
    size_x, size_y = vel.shape[0], vel.shape[1]
    outer_parts(ya, yb, xa, xb, outer, size_x, size_y, (side, side2), (extra, extra2))

    def body(x, _):
        v = vel[x]
        lap2[x] = lap2_in[x] + extra[x]
        wave3[x] = wave3_in[x] + v * extra[x]
        adj = adj3_in[x] + extra2[x]
        adj3[x] = adj
        image3[x] = v * adj
        return 0

    lax.fori_loop(0, size_x, body, 0, unroll=4)
    put_edges(wave3, 0, pya, pyb, pxa, pxb, 0)
    put_edges(image3, 4, pya, pyb, pxa, pxb, 4)


def fourth_inner_kernel(
    wave3, image3, adj3, adj4, lap1, lap2, inject, along_y, along_z,
    adj2, grad, flat, flat2,
):
    flat_part(wave3, along_y, along_z, flat)
    flat_part(image3, along_y, along_z, flat2)
    for x in range(wave3.shape[0]):
        for z in halves():
            lap3 = across(within(wave3), x, z) + flat[x, :, z] * (1.0 / SCALE)
            adj = across(within(image3), x, z) + flat2[x, :, z] * (1.0 / SCALE)
            old, mid = adj4[x, :, z], adj3[x, :, z]
            adj = 2.0 * mid - old + adj + inject[x, :, z]
            adj2[x, :, z] = adj
            grad[x, :, z] = old * lap3 + mid * lap2[x, :, z] + adj * lap1[x, :, z]


def fourth_kernel(
    offsets, yb, ya, xb, xa, grad_in, adj4, lap1, outer,
    placed, extra2, side, side2, extra,
):
    size_x, size_y = adj4.shape[0], adj4.shape[1]
    outer_parts(ya, yb, xa, xb, outer, size_x, size_y, (side, side2), (extra, extra2))
    start = offsets[0]
    low = start // HALF
    shift_by = lax.rem(start, HALF)

    def body(x, _):
        lane = lax.broadcasted_iota(jnp.int32, (size_y, HALF), 1)
        rolled = []
        for z in halves():
            grad = grad_in[x, :, z] + adj4[x, :, z] * extra[x, :, z] + lap1[x, :, z] * extra2[x, :, z]
            rolled.append(pltpu.roll(grad, shift_by, 1))
        high = lane >= shift_by
        first = jnp.where(high, rolled[0], 0.0)
        second = jnp.where(high, rolled[1], rolled[0])
        third = jnp.where(high, 0.0, rolled[1])
        for n in range(4):
            value = jnp.where(low == n, first, jnp.where(low + 1 == n, second, third))
            placed[n, x] = jnp.where((low <= n) & (n <= low + 2), value, 0.0)
        return 0

    lax.fori_loop(0, size_x, body, 0, unroll=4)


def last_kernel(parts, adj2_in, extra, out, adj2):
    out[...] = (parts[0] + parts[1]) + (parts[2] + parts[3])
    adj2[...] = adj2_in[...] + extra[...]


def local(model_vel2, offsets, wave_prev, wave_cur, adj_cur, adj_next, src_cell, src_amp, rec_cell, rec_res):
    size_x, size_y, depth = wave_cur.shape[1:]
    wave0, wave1, adj4, adj5 = wave_prev[0], wave_cur[0], adj_cur[0], adj_next[0]
    block = shaped(size_x, size_y, depth)
    edge_y, edge_x = shaped(size_x, 8, depth), shaped(8, size_y, depth)
    tile = shaped(size_x, size_y, HALF)
    whole = pltpu.VMEM((size_x, size_y, depth), F32)
    side = pltpu.VMEM((8, size_y, depth), F32)
    rows, bf16 = size_x // 2 * size_y, jnp.bfloat16
    matrices = [
        jax.ShapeDtypeStruct(dims, bf16)
        for dims in ((rows, rows), (depth, depth), (2, rows, size_x // 2 * 16))
    ]

    tile_a = swap_shot(model_vel2, 0)
    pair = swap_shot(call(pair_kernel, shaped(2 * size_x, size_y, HALF), n_in=2)(model_vel2, tile_a), 1)
    edges = call(
        edges_kernel, (shaped(size_x // 2, 8, depth),) * 2 + (shaped(4, size_y, depth),) * 2, n_in=1
    )(wave1)
    halos = exchange(edges)
    along_y, along_z, outer, source0, source1, inject0, inject1 = call(
        functools.partial(tables_kernel, size_x, size_y), (*matrices, block, block, block, block),
        smem=2, n_in=2, room=8,
    )(src_cell, src_amp, jnp.transpose(rec_cell[0]), jnp.transpose(rec_res[0]))
    yb, ya, xb, xa = halos
    lap1 = call(first_inner_kernel, block, (whole,), n_in=6, room=6, flops=5000000000)(wave1, yb, ya, along_y, along_z, outer)
    lap1 = call(first_kernel, block, (side,), n_in=3, aliases={0: 0})(lap1, xb, xa)
    vel, wave2, image, *edges = call(
        second_kernel, (block,) * 3 + (edge_y,) * 2 + (edge_x,) * 2,
        (pltpu.VMEM((4, size_x, size_y, HALF), F32),), smem=1, n_in=8, room=8,
    )(offsets, model_vel2, tile_a, pair, lap1, wave0, wave1, adj4, source0)
    halos = exchange(edges)
    inner = call(third_inner_kernel, (block,) * 3, (whole,) * 2, n_in=10, room=10)(
        wave1, wave2, adj4, adj5, vel, image, source1, inject0, along_y, along_z
    )
    lap2, wave3, adj3, image3, *edges = call(
        third_kernel, (block,) * 4 + (edge_y,) * 2 + (edge_x,) * 2, (side, side, whole, whole), n_in=9,
        room=10, aliases={4: 0, 5: 1, 6: 2},
    )(*halos, *inner, vel, outer)
    halos = exchange(edges)
    inner_adj2, inner_grad = call(fourth_inner_kernel, (block,) * 2, (whole,) * 2, n_in=9, room=10)(
        wave3, image3, adj3, adj4, lap1, lap2, inject1, along_y, along_z
    )
    placed, extra = call(
        fourth_kernel, (shaped(4, size_x, size_y, HALF), block), (side, side, whole), smem=1, n_in=8, room=10
    )(offsets, *halos, inner_grad, adj4, lap1, outer)
    parts = lax.all_to_all(placed, "shot", 0, 0)
    owned, adj2 = call(last_kernel, (tile, block), n_in=3)(parts, inner_adj2, extra)
    return owned, adj2[None]


def solution(mesh):
    return jax.shard_map(
        local,
        mesh=mesh,
        in_specs=(
            P("gx", "gy", "shot"),
            P("shot"),
            P("shot", "gx", "gy", None),
            P("shot", "gx", "gy", None),
            P("shot", "gx", "gy", None),
            P("shot", "gx", "gy", None),
            P("shot", None),
            P("shot", None),
            P("shot", None, None),
            P("shot", None, None),
        ),
        out_specs=(P("gx", "gy", "shot"), P("shot", "gx", "gy", None)),
        check_vma=False,
    )
```

```python
import functools

import jax
import jax.numpy as jnp
from jax import lax
from jax.experimental import pallas as pl
from jax.experimental.pallas import tpu as pltpu
from jax.sharding import PartitionSpec as P

COEF = (-205.0 / 72.0, 8.0 / 5.0, -1.0 / 5.0, 8.0 / 315.0, -1.0 / 560.0)
SCALE = 5040.0
WEIGHT = (0.0, 8064.0, -1008.0, 128.0, -9.0)
F32 = jnp.float32
HALF = 128


def swap(value, axis, odd):
    pairs = []
    for i in range(odd, lax.axis_size(axis) - 1, 2):
        pairs += [(i, i + 1), (i + 1, i)]
    return lax.ppermute(value, axis, pairs)


def swap_shot(value, odd):
    size = lax.axis_size("shot")
    pairs = []
    for i in range(odd, size, 2):
        pairs += [(i, (i + 1) % size), ((i + 1) % size, i)]
    return lax.ppermute(value, "shot", pairs)


def swap_across(value):
    size = lax.axis_size("shot")
    return lax.ppermute(value, "shot", [(i, (i + size // 2) % size) for i in range(size)])


def exchange(payload):
    ya, yb, xa, xb = payload
    return swap(yb, "gy", 1), swap(ya, "gy", 0), swap(xb, "gx", 1), swap(xa, "gx", 0)


def call(body, out_shape, scratch=(), smem=0, n_in=0, room=4, aliases=None, flops=0):
    vmem = pl.BlockSpec(memory_space=pltpu.VMEM)
    scal = pl.BlockSpec(memory_space=pltpu.SMEM)
    return pl.pallas_call(
        body,
        out_shape=out_shape,
        in_specs=[scal] * smem + [vmem] * n_in,
        out_specs=jax.tree.map(lambda _: vmem, out_shape),
        scratch_shapes=list(scratch),
        input_output_aliases=aliases or {},
        cost_estimate=pl.CostEstimate(flops=flops, bytes_accessed=0, transcendentals=0),
        compiler_params=pltpu.CompilerParams(vmem_limit_bytes=room << 20),
    )


def shaped(*dims):
    return jax.ShapeDtypeStruct(dims, F32)


def even(axis):
    return lax.rem(lax.axis_index(axis), 2) == 0


def weight(distance):
    distance = jnp.abs(distance)
    total = jnp.zeros(distance.shape, F32)
    for k in range(1, 5):
        total = jnp.where(distance == k, WEIGHT[k], total)
    return total


def three(value):
    first = value.astype(jnp.bfloat16)
    rest = value - first.astype(F32)
    second = rest.astype(jnp.bfloat16)
    return first, second, (rest - second.astype(F32)).astype(jnp.bfloat16)


def product(a, b):
    return jnp.dot(a, b, preferred_element_type=F32)


def flat_part(field, along_y, along_z, out):
    size_x, size_y, depth = field.shape
    chunk = along_y.shape[0] // size_y
    for at in range(0, size_x, chunk):
        parts = three(field[at : at + chunk].reshape(chunk * size_y, depth))
        total = sum(product(part, along_z[...]) + product(along_y[...], part) for part in parts)
        out[at : at + chunk] = total.reshape(chunk, size_y, depth)


def outer_part(ya, yb, at, outer, field, size_y):
    depth = ya.shape[2]
    chunk = outer.shape[1] // size_y
    a, b = (m[at : at + chunk].reshape(chunk * 8, depth) for m in (ya, yb))
    even_y = even("gy")
    below, above = three(jnp.where(even_y, b, a)), three(jnp.where(even_y, a, b))
    total = sum(product(outer[field], jnp.concatenate(pair, axis=0)) for pair in zip(below, above))
    return total.reshape(chunk, size_y, depth)


def outside_x(xa, xb, plane, out):
    even_x = even("gx")
    low = [jnp.where(even_x, xb[plane + i], xa[plane + i]) for i in range(4)]
    high = [jnp.where(even_x, xa[plane + i], xb[plane + i]) for i in range(4)]
    for i in range(4):
        first, last = 0.0, 0.0
        for k in range(i + 1, 5):
            first = first + COEF[k] * low[4 + i - k]
            last = last + COEF[k] * high[k - i - 1]
        out[i] = first
        out[7 - i] = last


def outer_parts(ya, yb, xa, xb, outer, size_x, size_y, sides, extras):
    chunk = outer.shape[1] // size_y
    for field, (side, extra) in enumerate(zip(sides, extras)):
        outside_x(xa, xb, 4 * field, side)
        for at in range(0, size_x, chunk):
            extra[at : at + chunk] = outer_part(ya, yb, at, outer, field, size_y) * (1.0 / SCALE)
        extra[0:4] = extra[0:4] + side[0:4]
        extra[size_x - 4 : size_x] = extra[size_x - 4 : size_x] + side[4:8]


def across(plane, x, z):
    total = (3.0 * COEF[0]) * plane(x, z)
    for k in range(1, 5):
        near = [p for p in (plane(x - k, z), plane(x + k, z)) if p is not None]
        if near:
            total = total + COEF[k] * sum(near[1:], near[0])
    return total


def within(field):
    size_x = field.shape[0]
    return lambda x, z: field[x, :, z] if 0 <= x < size_x else None


def halves():
    return [slice(h * HALF, (h + 1) * HALF) for h in range(2)]


def put_edges(field, row, ya, yb, xa, xb, plane):
    even_y, even_x = even("gy"), even("gx")
    size_x, size_y = field.shape[0], field.shape[1]
    first, last = field[:, 0:4, :], field[:, size_y - 4 : size_y, :]
    ya[:, row : row + 4, :] = jnp.where(even_y, last, first)
    yb[:, row : row + 4, :] = jnp.where(even_y, first, last)
    top = size_x - 4
    xa[plane : plane + 4] = field[pl.ds(jnp.where(even_x, top, 0), 4)]
    xb[plane : plane + 4] = field[pl.ds(jnp.where(even_x, 0, top), 4)]


def copies_kernel(tile, out, sems):
    moves = [pltpu.make_async_copy(tile, out.at[n], sems.at[n]) for n in range(4)]
    for move in moves:
        move.start()
    for move in moves:
        move.wait()


def edges_kernel(field, ya, yb, xa, xb):
    even_y, even_x = even("gy"), even("gx")
    size_x, size_y = field.shape[0], field.shape[1]
    half = size_x // 2
    for part in range(2):
        x = slice(part * half, (part + 1) * half)
        first, last = field[x, 0:4, :], field[x, size_y - 4 : size_y, :]
        ya[:, part * 4 : part * 4 + 4, :] = jnp.where(even_y, last, first)
        yb[:, part * 4 : part * 4 + 4, :] = jnp.where(even_y, first, last)
    top = size_x - 4
    xa[...] = field[pl.ds(jnp.where(even_x, top, 0), 4)]
    xb[...] = field[pl.ds(jnp.where(even_x, 0, top), 4)]


def index(shape, dim):
    return lax.broadcasted_iota(jnp.int32, shape, dim)


def matrices_kernel(size_x, size_y, along_y, along_z, outer):
    depth = along_z.shape[0]
    half = size_x // 2
    rows = half * size_y
    along_z[...] = weight(index((depth, depth), 0) - index((depth, depth), 1)).astype(jnp.bfloat16)
    here, there = index((rows, rows), 0), index((rows, rows), 1)
    near = jnp.where(here // size_y == there // size_y, weight(here - there), 0.0)
    along_y[...] = near.astype(jnp.bfloat16)
    here, there = index((rows, half * 8), 0), index((rows, half * 8), 1)
    y, row = lax.rem(here, size_y), lax.rem(there, 4)
    below, above = weight(y - row + 4), weight(row + size_y - y)
    for field in range(2):
        use = (here // size_y == there // 8) & (lax.rem(there, 8) // 4 == field)
        both = jnp.concatenate([jnp.where(use, below, 0.0), jnp.where(use, above, 0.0)], axis=1)
        outer[field] = both.astype(jnp.bfloat16)


def inject_kernel(size_x, size_y, cell, amp, cells, res, other, source0, source1, inject0, inject1):
    depth = inject0.shape[2]
    half = size_x // 2
    rows = half * size_y
    base_x, base_y = lax.axis_index("gx") * size_x, lax.axis_index("gy") * size_y
    x, y = cell[0, 0] - base_x, cell[0, 1] - base_y
    source0[...] = jnp.zeros_like(source0)
    source1[...] = jnp.zeros_like(source1)

    @pl.when((x >= 0) & (x < size_x) & (y >= 0) & (y < size_y))
    def _():
        at = (index((size_y, depth), 0) == y) & (index((size_y, depth), 1) == cell[0, 2])
        source0[x] = jnp.where(at, amp[0, 0], 0.0)
        source1[x] = jnp.where(at, amp[0, 1], 0.0)

    count = cells.shape[1]
    x, y = cells[0:1, :] - base_x, cells[1:2, :] - base_y
    inside = (x >= 0) & (x < size_x) & (y >= 0) & (y < size_y)
    place = jnp.where(inside, x * size_y + y, -1)
    deep = index((depth, count), 0) == cells[2:3, :]
    parts = [three(jnp.where(deep, res[n : n + 1, :], 0.0)) for n in range(2)]
    for part in range(2):
        at = index((rows, count), 0) + part * rows
        flat = jnp.where(at == place, 1.0, 0.0).astype(jnp.bfloat16)
        for n, out in enumerate((inject0, inject1)):
            done = sum(
                lax.dot_general(flat, p, (((1,), (1,)), ((), ())), preferred_element_type=F32) for p in parts[n]
            )
            out[part * half : (part + 1) * half] = done.reshape(half, size_y, depth)


def first_inner_kernel(wave1, yb, ya, along_y, along_z, outer, lap1, flat):
    size_x, size_y = wave1.shape[0], wave1.shape[1]
    flat_part(wave1, along_y, along_z, flat)
    half = size_x // 2
    for part in range(2):
        x = slice(part * half, (part + 1) * half)
        flat[x] = flat[x] + outer_part(ya, yb, 0, outer, part, size_y)
    for x in range(size_x):
        for z in halves():
            lap1[x, :, z] = across(within(wave1), x, z) + flat[x, :, z] * (1.0 / SCALE)


def first_kernel(inner, xb, xa, lap1, side):
    size_x = lap1.shape[0]
    outside_x(xa, xb, 0, side)
    lap1[0:4] = inner[0:4] + side[0:4]
    lap1[size_x - 4 : size_x] = inner[size_x - 4 : size_x] + side[4:8]


def second_kernel(
    offsets, column, lap1, wave0, wave1, adj4, source, vel, wave2, image, ya, yb, xa, xb
):
    size_x, size_y = wave1.shape[0], wave1.shape[1]
    start = offsets[0]
    low = start // HALF
    shift_by = lax.rem(start, HALF)
    back = lax.rem(HALF - shift_by, HALF)
    third = jnp.minimum(low + 2, 3)

    def body(x, _):
        lane = lax.broadcasted_iota(jnp.int32, (size_y, HALF), 1)
        rolled = [pltpu.roll(column[i, x], back, 1) for i in (low, low + 1, third)]
        for h, z in enumerate(halves()):
            v = jnp.where(lane < HALF - shift_by, rolled[h], rolled[h + 1])
            vel[x, :, z] = v
            image[x, :, z] = v * adj4[x, :, z]
            wave2[x, :, z] = 2.0 * wave1[x, :, z] - wave0[x, :, z] + v * lap1[x, :, z] + source[x, :, z]
        return 0

    lax.fori_loop(0, size_x, body, 0, unroll=4)
    put_edges(wave2, 0, ya, yb, xa, xb, 0)
    put_edges(image, 4, ya, yb, xa, xb, 4)


def third_inner_kernel(
    wave1, wave2, adj4, adj5, vel, image, source, inject, along_y, along_z,
    lap2, wave3, adj3, flat, flat2,
):
    flat_part(wave2, along_y, along_z, flat)
    flat_part(image, along_y, along_z, flat2)
    for x in range(wave1.shape[0]):
        for z in halves():
            lap = across(within(wave2), x, z) + flat[x, :, z] * (1.0 / SCALE)
            lap2[x, :, z] = lap
            wave3[x, :, z] = 2.0 * wave2[x, :, z] - wave1[x, :, z] + vel[x, :, z] * lap + source[x, :, z]
            adj = across(within(image), x, z) + flat2[x, :, z] * (1.0 / SCALE)
            adj3[x, :, z] = 2.0 * adj4[x, :, z] - adj5[x, :, z] + adj + inject[x, :, z]


def third_kernel(
    yb, ya, xb, xa, lap2_in, wave3_in, adj3_in, vel, outer,
    lap2, wave3, adj3, image3, pya, pyb, pxa, pxb, side, side2, extra, extra2,
):
    size_x, size_y = vel.shape[0], vel.shape[1]
    outer_parts(ya, yb, xa, xb, outer, size_x, size_y, (side, side2), (extra, extra2))

    def body(x, _):
        v = vel[x]
        lap2[x] = lap2_in[x] + extra[x]
        wave3[x] = wave3_in[x] + v * extra[x]
        adj = adj3_in[x] + extra2[x]
        adj3[x] = adj
        image3[x] = v * adj
        return 0

    lax.fori_loop(0, size_x, body, 0, unroll=4)
    put_edges(wave3, 0, pya, pyb, pxa, pxb, 0)
    put_edges(image3, 4, pya, pyb, pxa, pxb, 4)


def fourth_inner_kernel(
    wave3, image3, adj3, adj4, lap1, lap2, inject, along_y, along_z,
    adj2, grad, flat, flat2,
):
    flat_part(wave3, along_y, along_z, flat)
    flat_part(image3, along_y, along_z, flat2)
    for x in range(wave3.shape[0]):
        for z in halves():
            lap3 = across(within(wave3), x, z) + flat[x, :, z] * (1.0 / SCALE)
            adj = across(within(image3), x, z) + flat2[x, :, z] * (1.0 / SCALE)
            old, mid = adj4[x, :, z], adj3[x, :, z]
            adj = 2.0 * mid - old + adj + inject[x, :, z]
            adj2[x, :, z] = adj
            grad[x, :, z] = old * lap3 + mid * lap2[x, :, z] + adj * lap1[x, :, z]


def fourth_kernel(
    offsets, yb, ya, xb, xa, grad_in, adj4, lap1, outer,
    far, near_b, near_a, own, extra2, side, side2, extra,
):
    size_x, size_y = adj4.shape[0], adj4.shape[1]
    outer_parts(ya, yb, xa, xb, outer, size_x, size_y, (side, side2), (extra, extra2))
    start = offsets[0]
    low = start // HALF
    shift_by = lax.rem(start, HALF)

    me = lax.axis_index("shot")
    turn = jnp.where(even("shot"), 1, 3)
    which = [(lax.rem(me + away, 4) - low, tile) for away, tile in ((2, far), (turn, near_a), (4 - turn, near_b), (0, own))]

    def body(x, _):
        lane = lax.broadcasted_iota(jnp.int32, (size_y, HALF), 1)
        rolled = []
        for z in halves():
            grad = grad_in[x, :, z] + adj4[x, :, z] * extra[x, :, z] + lap1[x, :, z] * extra2[x, :, z]
            rolled.append(pltpu.roll(grad, shift_by, 1))
        high = lane >= shift_by
        first = jnp.where(high, rolled[0], 0.0)
        second = jnp.where(high, rolled[1], rolled[0])
        third = jnp.where(high, 0.0, rolled[1])
        for n, tile in which:
            value = jnp.where(n == 0, first, jnp.where(n == 1, second, third))
            tile[x] = jnp.where((n >= 0) & (n <= 2), value, 0.0)
        return 0

    lax.fori_loop(0, size_x, body, 0, unroll=4)


def last_kernel(own, far, b, a, adj2_in, extra, out, adj2):
    out[...] = (own[...] + far[...]) + (a[...] + b[...])
    adj2[...] = adj2_in[...] + extra[...]


def local(model_vel2, offsets, wave_prev, wave_cur, adj_cur, adj_next, src_cell, src_amp, rec_cell, rec_res):
    size_x, size_y, depth = wave_cur.shape[1:]
    wave0, wave1, adj4, adj5 = wave_prev[0], wave_cur[0], adj_cur[0], adj_next[0]
    block = shaped(size_x, size_y, depth)
    edge_y, edge_x = shaped(size_x, 8, depth), shaped(8, size_y, depth)
    tile = shaped(size_x, size_y, HALF)
    whole = pltpu.VMEM((size_x, size_y, depth), F32)
    side = pltpu.VMEM((8, size_y, depth), F32)
    rows, bf16 = size_x // 2 * size_y, jnp.bfloat16
    matrices = [
        jax.ShapeDtypeStruct(dims, bf16)
        for dims in ((rows, rows), (depth, depth), (2, rows, size_x // 2 * 16))
    ]

    copies = pl.pallas_call(
        copies_kernel,
        out_shape=shaped(4, size_x, size_y, HALF),
        in_specs=[pl.BlockSpec(memory_space=pltpu.HBM)],
        out_specs=pl.BlockSpec(memory_space=pltpu.HBM),
        scratch_shapes=[pltpu.SemaphoreType.DMA((4,))],
        compiler_params=pltpu.CompilerParams(vmem_limit_bytes=1 << 20),
    )(model_vel2)
    column = lax.all_to_all(copies, "shot", 0, 0)
    edges = call(
        edges_kernel, (shaped(size_x // 2, 8, depth),) * 2 + (shaped(4, size_y, depth),) * 2, n_in=1, room=1
    )(wave1)
    halos = exchange(edges)
    along_y, along_z, outer = call(
        functools.partial(matrices_kernel, size_x, size_y), tuple(matrices), n_in=0, room=1
    )()
    yb, ya, xb, xa = halos
    lap1 = call(first_inner_kernel, block, (whole,), n_in=6, room=2, flops=0)(wave1, yb, ya, along_y, along_z, outer)
    lap1 = call(first_kernel, block, (side,), n_in=3, room=1, aliases={0: 0})(lap1, xb, xa)
    source0, source1, inject0, inject1 = pl.pallas_call(
        functools.partial(inject_kernel, size_x, size_y),
        out_shape=(block,) * 4,
        in_specs=[pl.BlockSpec(memory_space=pltpu.SMEM)] * 2 + [pl.BlockSpec(memory_space=pltpu.VMEM)] * 2
        + [pl.BlockSpec(memory_space=pl.ANY)],
        out_specs=(pl.BlockSpec(memory_space=pltpu.VMEM),) * 4,
        compiler_params=pltpu.CompilerParams(vmem_limit_bytes=4 << 20),
    )(src_cell, src_amp, jnp.transpose(rec_cell[0]), jnp.transpose(rec_res[0]), column)
    vel, wave2, image, *edges = call(
        second_kernel, (block,) * 3 + (edge_y,) * 2 + (edge_x,) * 2,
        smem=1, n_in=6, room=4,
    )(offsets, column, lap1, wave0, wave1, adj4, source0)
    halos = exchange(edges)
    inner = call(third_inner_kernel, (block,) * 3, (whole,) * 2, n_in=10, room=10)(
        wave1, wave2, adj4, adj5, vel, image, source1, inject0, along_y, along_z
    )
    lap2, wave3, adj3, image3, *edges = call(
        third_kernel, (block,) * 4 + (edge_y,) * 2 + (edge_x,) * 2, (side, side, whole, whole), n_in=9,
        room=10, aliases={4: 0, 5: 1, 6: 2},
    )(*halos, *inner, vel, outer)
    halos = exchange(edges)
    inner_adj2, inner_grad = call(fourth_inner_kernel, (block,) * 2, (whole,) * 2, n_in=9, room=10)(
        wave3, image3, adj3, adj4, lap1, lap2, inject1, along_y, along_z
    )
    far, near_b, near_a, own, extra = call(
        fourth_kernel, (tile, tile, tile, tile, block), (side, side, whole), smem=1, n_in=8, room=10
    )(offsets, *halos, inner_grad, adj4, lap1, outer)
    far, b, a = swap_across(far), swap_shot(near_b, 1), swap_shot(near_a, 0)
    owned, adj2 = call(last_kernel, (tile, block), n_in=6)(own, far, b, a, inner_adj2, extra)
    return owned, adj2[None]


def solution(mesh):
    return jax.shard_map(
        local,
        mesh=mesh,
        in_specs=(
            P("gx", "gy", "shot"),
            P("shot"),
            P("shot", "gx", "gy", None),
            P("shot", "gx", "gy", None),
            P("shot", "gx", "gy", None),
            P("shot", "gx", "gy", None),
            P("shot", None),
            P("shot", None),
            P("shot", None, None),
            P("shot", None, None),
        ),
        out_specs=(P("gx", "gy", "shot"), P("shot", "gx", "gy", None)),
        check_vma=False,
    )
```

```python
import functools

import jax
import jax.numpy as jnp
from jax import lax
from jax.experimental import pallas as pl
from jax.experimental.pallas import tpu as pltpu
from jax.sharding import PartitionSpec as P

COEF = (-205.0 / 72.0, 8.0 / 5.0, -1.0 / 5.0, 8.0 / 315.0, -1.0 / 560.0)
SCALE = 5040.0
WEIGHT = (0.0, 8064.0, -1008.0, 128.0, -9.0)
F32 = jnp.float32
HALF = 128


def swap(value, axis, odd):
    pairs = []
    for i in range(odd, lax.axis_size(axis) - 1, 2):
        pairs += [(i, i + 1), (i + 1, i)]
    return lax.ppermute(value, axis, pairs)


def swap_shot(value, odd):
    size = lax.axis_size("shot")
    pairs = []
    for i in range(odd, size, 2):
        pairs += [(i, (i + 1) % size), ((i + 1) % size, i)]
    return lax.ppermute(value, "shot", pairs)


def swap_across(value):
    size = lax.axis_size("shot")
    return lax.ppermute(value, "shot", [(i, (i + size // 2) % size) for i in range(size)])


def exchange(payload):
    ya, yb, xa, xb = payload
    return swap(yb, "gy", 1), swap(ya, "gy", 0), swap(xb, "gx", 1), swap(xa, "gx", 0)


def call(body, out_shape, scratch=(), smem=0, n_in=0, room=4, aliases=None, flops=0):
    vmem = pl.BlockSpec(memory_space=pltpu.VMEM)
    scal = pl.BlockSpec(memory_space=pltpu.SMEM)
    return pl.pallas_call(
        body,
        out_shape=out_shape,
        in_specs=[scal] * smem + [vmem] * n_in,
        out_specs=jax.tree.map(lambda _: vmem, out_shape),
        scratch_shapes=list(scratch),
        input_output_aliases=aliases or {},
        cost_estimate=pl.CostEstimate(flops=flops, bytes_accessed=0, transcendentals=0),
        compiler_params=pltpu.CompilerParams(vmem_limit_bytes=room << 20),
    )


def shaped(*dims):
    return jax.ShapeDtypeStruct(dims, F32)


def even(axis):
    return lax.rem(lax.axis_index(axis), 2) == 0


def weight(distance):
    distance = jnp.abs(distance)
    total = jnp.zeros(distance.shape, F32)
    for k in range(1, 5):
        total = jnp.where(distance == k, WEIGHT[k], total)
    return total


def three(value):
    first = value.astype(jnp.bfloat16)
    rest = value - first.astype(F32)
    second = rest.astype(jnp.bfloat16)
    return first, second, (rest - second.astype(F32)).astype(jnp.bfloat16)


def product(a, b):
    return jnp.dot(a, b, preferred_element_type=F32)


def flat_part(field, along_y, along_z, out):
    size_x, size_y, depth = field.shape
    chunk = along_y.shape[0] // size_y
    for at in range(0, size_x, chunk):
        parts = three(field[at : at + chunk].reshape(chunk * size_y, depth))
        total = sum(product(part, along_z[...]) + product(along_y[...], part) for part in parts)
        out[at : at + chunk] = total.reshape(chunk, size_y, depth)


def outer_part(ya, yb, at, outer, field):
    depth = ya.shape[2]
    chunk = outer.shape[1] // 8
    a, b = (m[at : at + chunk].reshape(chunk * 8, depth) for m in (ya, yb))
    even_y = even("gy")
    below, above = three(jnp.where(even_y, b, a)), three(jnp.where(even_y, a, b))
    total = sum(product(outer[field], jnp.concatenate(pair, axis=0)) for pair in zip(below, above))
    return total.reshape(chunk, 8, depth) * (1.0 / SCALE)


def spread(rows, size_y):
    first = lax.broadcasted_iota(jnp.int32, rows.shape, 0) < 4
    middle = [jnp.zeros((size_y - 16, rows.shape[1]), F32)] if size_y > 16 else []
    return jnp.concatenate([jnp.where(first, rows, 0.0)] + middle + [jnp.where(first, 0.0, rows)], axis=0)


def outside_x(xa, xb, plane, out):
    even_x = even("gx")
    low = [jnp.where(even_x, xb[plane + i], xa[plane + i]) for i in range(4)]
    high = [jnp.where(even_x, xa[plane + i], xb[plane + i]) for i in range(4)]
    for i in range(4):
        first, last = 0.0, 0.0
        for k in range(i + 1, 5):
            first = first + COEF[k] * low[4 + i - k]
            last = last + COEF[k] * high[k - i - 1]
        out[i] = first
        out[7 - i] = last


def outer_parts(ya, yb, xa, xb, outer, sides, rows):
    chunk = outer.shape[1] // 8
    for field, (side, row) in enumerate(zip(sides, rows)):
        outside_x(xa, xb, 4 * field, side)
        for at in range(0, row.shape[0], chunk):
            row[at : at + chunk] = outer_part(ya, yb, at, outer, field)


def outer_of(side, row, x, z):
    size_x, size_y = row.shape[0], side.shape[1]
    extra = spread(row[x, :, z], size_y)
    if x < 4:
        extra = extra + side[x, :, z]
    if x >= size_x - 4:
        extra = extra + side[x - (size_x - 8), :, z]
    return extra


def across(plane, x, z):
    total = (3.0 * COEF[0]) * plane(x, z)
    for k in range(1, 5):
        near = [p for p in (plane(x - k, z), plane(x + k, z)) if p is not None]
        if near:
            total = total + COEF[k] * sum(near[1:], near[0])
    return total


def within(field):
    size_x = field.shape[0]
    return lambda x, z: field[x, :, z] if 0 <= x < size_x else None


def halves():
    return [slice(h * HALF, (h + 1) * HALF) for h in range(2)]


def put_edges(field, row, ya, yb, xa, xb, plane):
    even_y, even_x = even("gy"), even("gx")
    size_x, size_y = field.shape[0], field.shape[1]
    first, last = field[:, 0:4, :], field[:, size_y - 4 : size_y, :]
    ya[:, row : row + 4, :] = jnp.where(even_y, last, first)
    yb[:, row : row + 4, :] = jnp.where(even_y, first, last)
    top = size_x - 4
    xa[plane : plane + 4] = field[pl.ds(jnp.where(even_x, top, 0), 4)]
    xb[plane : plane + 4] = field[pl.ds(jnp.where(even_x, 0, top), 4)]


def copies_kernel(tile, out, sems):
    moves = [pltpu.make_async_copy(tile, out.at[n], sems.at[n]) for n in range(4)]
    for move in moves:
        move.start()
    for move in moves:
        move.wait()


def edges_kernel(field, ya, yb, xa, xb):
    even_y, even_x = even("gy"), even("gx")
    size_x, size_y = field.shape[0], field.shape[1]
    half = size_x // 2
    for part in range(2):
        x = slice(part * half, (part + 1) * half)
        first, last = field[x, 0:4, :], field[x, size_y - 4 : size_y, :]
        ya[:, part * 4 : part * 4 + 4, :] = jnp.where(even_y, last, first)
        yb[:, part * 4 : part * 4 + 4, :] = jnp.where(even_y, first, last)
    top = size_x - 4
    xa[...] = field[pl.ds(jnp.where(even_x, top, 0), 4)]
    xb[...] = field[pl.ds(jnp.where(even_x, 0, top), 4)]


def source_of(cell, amp, step, size_x, size_y):
    shape = (size_y, HALF)

    def one(array, n):
        return jnp.broadcast_to(array[0:1, n : n + 1], shape)

    x = one(cell, 0) - lax.axis_index("gx") * size_x
    y = one(cell, 1) - lax.axis_index("gy") * size_y
    at_y = lax.broadcasted_iota(jnp.int32, shape, 0) == y
    z = lax.broadcasted_iota(jnp.int32, shape, 1)
    return x, [jnp.where(at_y & (z + h * HALF == one(cell, 2)), one(amp, step), 0.0) for h in range(2)]


def index(shape, dim):
    return lax.broadcasted_iota(jnp.int32, shape, dim)


def matrices_kernel(size_x, size_y, along_y, along_z):
    depth = along_z.shape[0]
    rows = size_x // 2 * size_y
    along_z[...] = weight(index((depth, depth), 0) - index((depth, depth), 1)).astype(jnp.bfloat16)
    here, there = index((rows, rows), 0), index((rows, rows), 1)
    near = jnp.where(here // size_y == there // size_y, weight(here - there), 0.0)
    along_y[...] = near.astype(jnp.bfloat16)


def outer_matrices(size_x, size_y, outer):
    half = size_x // 2
    shape = (half * 8, half * 8)
    here, there = index(shape, 0), index(shape, 1)
    y, row = lax.rem(here, 8), lax.rem(there, 4)
    y = jnp.where(y < 4, y, y + size_y - 8)
    below, above = weight(y - row + 4), weight(row + size_y - y)
    for field in range(2):
        use = (here // 8 == there // 8) & (lax.rem(there, 8) // 4 == field)
        both = jnp.concatenate([jnp.where(use, below, 0.0), jnp.where(use, above, 0.0)], axis=1)
        outer[field] = both.astype(jnp.bfloat16)


def inject_kernel(size_x, size_y, cells, res, other, inject0, inject1, outer):
    outer_matrices(size_x, size_y, outer)
    depth = inject0.shape[2]
    half = size_x // 2
    rows = half * size_y
    count = cells.shape[1]
    x = cells[0:1, :] - lax.axis_index("gx") * size_x
    y = cells[1:2, :] - lax.axis_index("gy") * size_y
    inside = (x >= 0) & (x < size_x) & (y >= 0) & (y < size_y)
    place = jnp.where(inside, x * size_y + y, -1)
    deep = index((depth, count), 0) == cells[2:3, :]
    parts = [three(jnp.where(deep, res[n : n + 1, :], 0.0)) for n in range(2)]
    for part in range(2):
        at = index((rows, count), 0) + part * rows
        flat = jnp.where(at == place, 1.0, 0.0).astype(jnp.bfloat16)
        for n, out in enumerate((inject0, inject1)):
            done = sum(
                lax.dot_general(flat, p, (((1,), (1,)), ((), ())), preferred_element_type=F32) for p in parts[n]
            )
            out[part * half : (part + 1) * half] = done.reshape(half, size_y, depth)


def first_inner_kernel(wave1, yb, ya, along_y, along_z, lap1, flat, outer, row):
    size_x, size_y = wave1.shape[0], wave1.shape[1]
    outer_matrices(size_x, size_y, outer)
    flat_part(wave1, along_y, along_z, flat)
    half = size_x // 2
    for part in range(2):
        row[part * half : (part + 1) * half] = outer_part(ya, yb, 0, outer, part)
    for x in range(size_x):
        for z in halves():
            lap = across(within(wave1), x, z) + flat[x, :, z] * (1.0 / SCALE)
            lap1[x, :, z] = lap + spread(row[x, :, z], size_y)


def first_kernel(inner, xb, xa, lap1, side):
    size_x = lap1.shape[0]
    outside_x(xa, xb, 0, side)
    lap1[0:4] = inner[0:4] + side[0:4]
    lap1[size_x - 4 : size_x] = inner[size_x - 4 : size_x] + side[4:8]


def second_kernel(
    offsets, column, lap1, wave0, wave1, adj4, cell, amp, vel, wave2, image, ya, yb, xa, xb
):
    size_x, size_y = wave1.shape[0], wave1.shape[1]
    start = offsets[0]
    low = start // HALF
    shift_by = lax.rem(start, HALF)
    back = lax.rem(HALF - shift_by, HALF)
    third = jnp.minimum(low + 2, 3)

    plane, amounts = source_of(cell, amp, 0, size_x, size_y)

    def body(x, _):
        lane = lax.broadcasted_iota(jnp.int32, (size_y, HALF), 1)
        rolled = [pltpu.roll(column[i, x], back, 1) for i in (low, low + 1, third)]
        for h, z in enumerate(halves()):
            v = jnp.where(lane < HALF - shift_by, rolled[h], rolled[h + 1])
            vel[x, :, z] = v
            image[x, :, z] = v * adj4[x, :, z]
            wave = 2.0 * wave1[x, :, z] - wave0[x, :, z] + v * lap1[x, :, z]
            wave2[x, :, z] = wave + jnp.where(plane == x, amounts[h], 0.0)
        return 0

    lax.fori_loop(0, size_x, body, 0, unroll=4)
    put_edges(wave2, 0, ya, yb, xa, xb, 0)
    put_edges(image, 4, ya, yb, xa, xb, 4)


def third_inner_kernel(
    wave1, wave2, adj4, adj5, vel, image, cell, amp, inject, along_y, along_z,
    lap2, wave3, adj3, flat, flat2,
):
    flat_part(wave2, along_y, along_z, flat)
    flat_part(image, along_y, along_z, flat2)
    plane, amounts = source_of(cell, amp, 1, wave1.shape[0], wave1.shape[1])
    for x in range(wave1.shape[0]):
        for h, z in enumerate(halves()):
            lap = across(within(wave2), x, z) + flat[x, :, z] * (1.0 / SCALE)
            lap2[x, :, z] = lap
            wave = 2.0 * wave2[x, :, z] - wave1[x, :, z] + vel[x, :, z] * lap
            wave3[x, :, z] = wave + jnp.where(plane == x, amounts[h], 0.0)
            adj = across(within(image), x, z) + flat2[x, :, z] * (1.0 / SCALE)
            adj3[x, :, z] = 2.0 * adj4[x, :, z] - adj5[x, :, z] + adj + inject[x, :, z]


def third_kernel(
    yb, ya, xb, xa, lap2_in, wave3_in, adj3_in, vel, outer,
    lap2, wave3, adj3, image3, pya, pyb, pxa, pxb, side, side2, row, row2,
):
    outer_parts(ya, yb, xa, xb, outer, (side, side2), (row, row2))
    for x in range(vel.shape[0]):
        for z in halves():
            v = vel[x, :, z]
            extra = outer_of(side, row, x, z)
            lap2[x, :, z] = lap2_in[x, :, z] + extra
            wave3[x, :, z] = wave3_in[x, :, z] + v * extra
            adj = adj3_in[x, :, z] + outer_of(side2, row2, x, z)
            adj3[x, :, z] = adj
            image3[x, :, z] = v * adj
    put_edges(wave3, 0, pya, pyb, pxa, pxb, 0)
    put_edges(image3, 4, pya, pyb, pxa, pxb, 4)


def fourth_inner_kernel(
    wave3, image3, adj3, adj4, lap1, lap2, inject, along_y, along_z,
    adj2, grad, flat, flat2,
):
    flat_part(wave3, along_y, along_z, flat)
    flat_part(image3, along_y, along_z, flat2)
    for x in range(wave3.shape[0]):
        for z in halves():
            lap3 = across(within(wave3), x, z) + flat[x, :, z] * (1.0 / SCALE)
            adj = across(within(image3), x, z) + flat2[x, :, z] * (1.0 / SCALE)
            old, mid = adj4[x, :, z], adj3[x, :, z]
            adj = 2.0 * mid - old + adj + inject[x, :, z]
            adj2[x, :, z] = adj
            grad[x, :, z] = old * lap3 + mid * lap2[x, :, z] + adj * lap1[x, :, z]


def fourth_kernel(
    offsets, yb, ya, xb, xa, grad_in, adj4, lap1, outer,
    far, near_b, near_a, own, extra2, side, side2, row, row2,
):
    size_x, size_y = adj4.shape[0], adj4.shape[1]
    outer_parts(ya, yb, xa, xb, outer, (side, side2), (row, row2))
    start = offsets[0]
    low = start // HALF
    shift_by = lax.rem(start, HALF)

    me = lax.axis_index("shot")
    turn = jnp.where(even("shot"), 1, 3)
    which = [(lax.rem(me + away, 4) - low, tile) for away, tile in ((2, far), (turn, near_a), (4 - turn, near_b), (0, own))]

    lane = lax.broadcasted_iota(jnp.int32, (size_y, HALF), 1)
    high = lane >= shift_by
    for x in range(size_x):
        rolled = []
        for z in halves():
            more = outer_of(side2, row2, x, z)
            extra2[x, :, z] = more
            grad = grad_in[x, :, z] + adj4[x, :, z] * outer_of(side, row, x, z) + lap1[x, :, z] * more
            rolled.append(pltpu.roll(grad, shift_by, 1))
        first = jnp.where(high, rolled[0], 0.0)
        second = jnp.where(high, rolled[1], rolled[0])
        third = jnp.where(high, 0.0, rolled[1])
        for n, tile in which:
            value = jnp.where(n == 0, first, jnp.where(n == 1, second, third))
            tile[x] = jnp.where((n >= 0) & (n <= 2), value, 0.0)


def adjoint_kernel(adj2_in, extra, adj2):
    adj2[...] = adj2_in[...] + extra[...]


def sum_kernel(own, far, b, a, out):
    out[...] = (own[...] + far[...]) + (a[...] + b[...])


def local(model_vel2, offsets, wave_prev, wave_cur, adj_cur, adj_next, src_cell, src_amp, rec_cell, rec_res):
    size_x, size_y, depth = wave_cur.shape[1:]
    wave0, wave1, adj4, adj5 = wave_prev[0], wave_cur[0], adj_cur[0], adj_next[0]
    block = shaped(size_x, size_y, depth)
    edge_y, edge_x = shaped(size_x, 8, depth), shaped(8, size_y, depth)
    tile = shaped(size_x, size_y, HALF)
    whole = pltpu.VMEM((size_x, size_y, depth), F32)
    side = pltpu.VMEM((8, size_y, depth), F32)
    rows, bf16 = size_x // 2 * size_y, jnp.bfloat16
    outer_dims = (2, size_x // 2 * 8, size_x // 2 * 16)
    rows8 = pltpu.VMEM((size_x, 8, depth), F32)

    copies = pl.pallas_call(
        copies_kernel,
        out_shape=shaped(4, size_x, size_y, HALF),
        in_specs=[pl.BlockSpec(memory_space=pltpu.HBM)],
        out_specs=pl.BlockSpec(memory_space=pltpu.HBM),
        scratch_shapes=[pltpu.SemaphoreType.DMA((4,))],
        compiler_params=pltpu.CompilerParams(vmem_limit_bytes=1 << 20),
    )(model_vel2)
    column = lax.all_to_all(copies, "shot", 0, 0)
    edges = call(
        edges_kernel, (shaped(size_x // 2, 8, depth),) * 2 + (shaped(4, size_y, depth),) * 2, n_in=1, room=1
    )(wave1)
    halos = exchange(edges)
    along_y, along_z = call(
        functools.partial(matrices_kernel, size_x, size_y),
        (jax.ShapeDtypeStruct((rows, rows), bf16), jax.ShapeDtypeStruct((depth, depth), bf16)), room=1,
    )()
    yb, ya, xb, xa = halos
    lap1 = call(first_inner_kernel, block, (whole, pltpu.VMEM(outer_dims, bf16), rows8), n_in=5, room=2)(
        wave1, yb, ya, along_y, along_z
    )
    lap1 = call(first_kernel, block, (side,), n_in=3, room=1, aliases={0: 0})(lap1, xb, xa)
    vel, wave2, image, *edges = call(
        second_kernel, (block,) * 3 + (edge_y,) * 2 + (edge_x,) * 2,
        smem=1, n_in=7, room=4,
    )(offsets, column, lap1, wave0, wave1, adj4, src_cell, src_amp)
    inject0, inject1, outer = pl.pallas_call(
        functools.partial(inject_kernel, size_x, size_y),
        out_shape=(block, block, jax.ShapeDtypeStruct(outer_dims, bf16)),
        in_specs=[pl.BlockSpec(memory_space=pltpu.VMEM)] * 2 + [pl.BlockSpec(memory_space=pl.ANY)],
        out_specs=(pl.BlockSpec(memory_space=pltpu.VMEM),) * 3,
        compiler_params=pltpu.CompilerParams(vmem_limit_bytes=4 << 20),
    )(jnp.transpose(rec_cell[0]), jnp.transpose(rec_res[0]), vel)
    halos = exchange(edges)
    inner = call(third_inner_kernel, (block,) * 3, (whole,) * 2, n_in=11, room=10)(
        wave1, wave2, adj4, adj5, vel, image, src_cell, src_amp, inject0, along_y, along_z
    )
    lap2, wave3, adj3, image3, *edges = call(
        third_kernel, (block,) * 4 + (edge_y,) * 2 + (edge_x,) * 2, (side, side, rows8, rows8), n_in=9,
        room=10, aliases={4: 0, 5: 1, 6: 2},
    )(*halos, *inner, vel, outer)
    halos = exchange(edges)
    inner_adj2, inner_grad = call(fourth_inner_kernel, (block,) * 2, (whole,) * 2, n_in=9, room=10)(
        wave3, image3, adj3, adj4, lap1, lap2, inject1, along_y, along_z
    )
    far, near_b, near_a, own, extra = call(
        fourth_kernel, (tile, tile, tile, tile, block), (side, side, rows8, rows8), smem=1, n_in=8, room=10
    )(offsets, *halos, inner_grad, adj4, lap1, outer)
    far, b, a = swap_across(far), swap_shot(near_b, 1), swap_shot(near_a, 0)
    adj2 = call(adjoint_kernel, block, n_in=2)(inner_adj2, extra)
    owned = call(sum_kernel, tile, n_in=4)(own, far, b, a)
    return owned, adj2[None]


def solution(mesh):
    return jax.shard_map(
        local,
        mesh=mesh,
        in_specs=(
            P("gx", "gy", "shot"),
            P("shot"),
            P("shot", "gx", "gy", None),
            P("shot", "gx", "gy", None),
            P("shot", "gx", "gy", None),
            P("shot", "gx", "gy", None),
            P("shot", None),
            P("shot", None),
            P("shot", None, None),
            P("shot", None, None),
        ),
        out_specs=(P("gx", "gy", "shot"), P("shot", "gx", "gy", None)),
        check_vma=False,
    )
```

```python
import functools

import jax
import jax.numpy as jnp
from jax import lax
from jax.experimental import pallas as pl
from jax.experimental.pallas import tpu as pltpu
from jax.sharding import PartitionSpec as P

COEF = (-205.0 / 72.0, 8.0 / 5.0, -1.0 / 5.0, 8.0 / 315.0, -1.0 / 560.0)
SCALE = 5040.0
WEIGHT = (0.0, 8064.0, -1008.0, 128.0, -9.0)
F32 = jnp.float32
HALF = 128


def swap(value, axis, odd):
    pairs = []
    for i in range(odd, lax.axis_size(axis) - 1, 2):
        pairs += [(i, i + 1), (i + 1, i)]
    return lax.ppermute(value, axis, pairs)


def swap_shot(value, odd):
    size = lax.axis_size("shot")
    pairs = []
    for i in range(odd, size, 2):
        pairs += [(i, (i + 1) % size), ((i + 1) % size, i)]
    return lax.ppermute(value, "shot", pairs)


def swap_across(value):
    size = lax.axis_size("shot")
    return lax.ppermute(value, "shot", [(i, (i + size // 2) % size) for i in range(size)])


def exchange(payload):
    ya, yb, xa, xb = payload
    return swap(yb, "gy", 1), swap(ya, "gy", 0), swap(xb, "gx", 1), swap(xa, "gx", 0)


def call(body, out_shape, scratch=(), smem=0, n_in=0, room=4, aliases=None, flops=0):
    vmem = pl.BlockSpec(memory_space=pltpu.VMEM)
    scal = pl.BlockSpec(memory_space=pltpu.SMEM)
    return pl.pallas_call(
        body,
        out_shape=out_shape,
        in_specs=[scal] * smem + [vmem] * n_in,
        out_specs=jax.tree.map(lambda _: vmem, out_shape),
        scratch_shapes=list(scratch),
        input_output_aliases=aliases or {},
        cost_estimate=pl.CostEstimate(flops=flops, bytes_accessed=0, transcendentals=0),
        compiler_params=pltpu.CompilerParams(vmem_limit_bytes=room << 20),
    )


def shaped(*dims):
    return jax.ShapeDtypeStruct(dims, F32)


def even(axis):
    return lax.rem(lax.axis_index(axis), 2) == 0


def weight(distance):
    distance = jnp.abs(distance)
    total = jnp.zeros(distance.shape, F32)
    for k in range(1, 5):
        total = jnp.where(distance == k, WEIGHT[k], total)
    return total


def three(value):
    first = value.astype(jnp.bfloat16)
    rest = value - first.astype(F32)
    second = rest.astype(jnp.bfloat16)
    return first, second, (rest - second.astype(F32)).astype(jnp.bfloat16)


def product(a, b):
    return jnp.dot(a, b, preferred_element_type=F32)


def flat_part(field, along_y, along_z, out):
    size_x, size_y, depth = field.shape
    chunk = along_y.shape[0] // size_y
    for at in range(0, size_x, chunk):
        parts = three(field[at : at + chunk].reshape(chunk * size_y, depth))
        total = sum(product(part, along_z[...]) + product(along_y[...], part) for part in parts)
        out[at : at + chunk] = total.reshape(chunk, size_y, depth)


def outer_part(ya, yb, at, outer, field):
    depth = ya.shape[2]
    chunk = outer.shape[1] // 8
    a, b = (m[at : at + chunk].reshape(chunk * 8, depth) for m in (ya, yb))
    even_y = even("gy")
    below, above = three(jnp.where(even_y, b, a)), three(jnp.where(even_y, a, b))
    total = sum(product(outer[field], jnp.concatenate(pair, axis=0)) for pair in zip(below, above))
    return total.reshape(chunk, 8, depth) * (1.0 / SCALE)


def spread(rows, size_y):
    first = lax.broadcasted_iota(jnp.int32, rows.shape, 0) < 4
    middle = [jnp.zeros((size_y - 16, rows.shape[1]), F32)] if size_y > 16 else []
    return jnp.concatenate([jnp.where(first, rows, 0.0)] + middle + [jnp.where(first, 0.0, rows)], axis=0)


def outside_x(xa, xb, plane, out):
    even_x = even("gx")
    low = [jnp.where(even_x, xb[plane + i], xa[plane + i]) for i in range(4)]
    high = [jnp.where(even_x, xa[plane + i], xb[plane + i]) for i in range(4)]
    for i in range(4):
        first, last = 0.0, 0.0
        for k in range(i + 1, 5):
            first = first + COEF[k] * low[4 + i - k]
            last = last + COEF[k] * high[k - i - 1]
        out[i] = first
        out[7 - i] = last


def outer_parts(ya, yb, xa, xb, outer, sides, rows):
    chunk = outer.shape[1] // 8
    for field, (side, row) in enumerate(zip(sides, rows)):
        outside_x(xa, xb, 4 * field, side)
        for at in range(0, row.shape[0], chunk):
            row[at : at + chunk] = outer_part(ya, yb, at, outer, field)


def outer_of(side, row, x, z):
    size_x, size_y = row.shape[0], side.shape[1]
    extra = spread(row[x, :, z], size_y)
    if x < 4:
        extra = extra + side[x, :, z]
    if x >= size_x - 4:
        extra = extra + side[x - (size_x - 8), :, z]
    return extra


def across(plane, x, z):
    total = (3.0 * COEF[0]) * plane(x, z)
    for k in range(1, 5):
        near = [p for p in (plane(x - k, z), plane(x + k, z)) if p is not None]
        if near:
            total = total + COEF[k] * sum(near[1:], near[0])
    return total


def within(field):
    size_x, held = field.shape[0], {}

    def plane(x, z):
        if not 0 <= x < size_x:
            return None
        if (x, z.start) not in held:
            held[x, z.start] = field[x, :, z]
        return held[x, z.start]

    return plane


def halves():
    return [slice(h * HALF, (h + 1) * HALF) for h in range(2)]


def put_edges(field, row, ya, yb, xa, xb, plane):
    even_y, even_x = even("gy"), even("gx")
    size_x, size_y = field.shape[0], field.shape[1]
    first, last = field[:, 0:4, :], field[:, size_y - 4 : size_y, :]
    ya[:, row : row + 4, :] = jnp.where(even_y, last, first)
    yb[:, row : row + 4, :] = jnp.where(even_y, first, last)
    top = size_x - 4
    xa[plane : plane + 4] = field[pl.ds(jnp.where(even_x, top, 0), 4)]
    xb[plane : plane + 4] = field[pl.ds(jnp.where(even_x, 0, top), 4)]


def copies_kernel(tile, out, sems):
    moves = [pltpu.make_async_copy(tile, out.at[n], sems.at[n]) for n in range(4)]
    for move in moves:
        move.start()
    for move in moves:
        move.wait()


def edges_kernel(field, ya, yb, xa, xb):
    even_y, even_x = even("gy"), even("gx")
    size_x, size_y = field.shape[0], field.shape[1]
    half = size_x // 2
    for part in range(2):
        x = slice(part * half, (part + 1) * half)
        first, last = field[x, 0:4, :], field[x, size_y - 4 : size_y, :]
        ya[:, part * 4 : part * 4 + 4, :] = jnp.where(even_y, last, first)
        yb[:, part * 4 : part * 4 + 4, :] = jnp.where(even_y, first, last)
    top = size_x - 4
    xa[...] = field[pl.ds(jnp.where(even_x, top, 0), 4)]
    xb[...] = field[pl.ds(jnp.where(even_x, 0, top), 4)]


def source_of(cell, amp, step, size_x, size_y):
    shape = (size_y, HALF)

    def one(array, n):
        return jnp.broadcast_to(array[0:1, n : n + 1], shape)

    x = one(cell, 0) - lax.axis_index("gx") * size_x
    y = one(cell, 1) - lax.axis_index("gy") * size_y
    at_y = lax.broadcasted_iota(jnp.int32, shape, 0) == y
    z = lax.broadcasted_iota(jnp.int32, shape, 1)
    return x, [jnp.where(at_y & (z + h * HALF == one(cell, 2)), one(amp, step), 0.0) for h in range(2)]


def index(shape, dim):
    return lax.broadcasted_iota(jnp.int32, shape, dim)


def difference_matrices(size_y, along_y, along_z):
    shape = along_z.shape
    along_z[...] = weight(index(shape, 0) - index(shape, 1)).astype(jnp.bfloat16)
    here, there = index(along_y.shape, 0), index(along_y.shape, 1)
    near = jnp.where(here // size_y == there // size_y, weight(here - there), 0.0)
    along_y[...] = near.astype(jnp.bfloat16)


def outer_matrices(size_x, size_y, outer):
    half = size_x // 2
    shape = (half * 8, half * 8)
    here, there = index(shape, 0), index(shape, 1)
    y, row = lax.rem(here, 8), lax.rem(there, 4)
    y = jnp.where(y < 4, y, y + size_y - 8)
    below, above = weight(y - row + 4), weight(row + size_y - y)
    for field in range(2):
        use = (here // 8 == there // 8) & (lax.rem(there, 8) // 4 == field)
        both = jnp.concatenate([jnp.where(use, below, 0.0), jnp.where(use, above, 0.0)], axis=1)
        outer[field] = both.astype(jnp.bfloat16)


def tables_kernel(size_x, size_y, cells, res, other, inject0, inject1, along_y, along_z, outer):
    difference_matrices(size_y, along_y, along_z)
    outer_matrices(size_x, size_y, outer)
    depth = inject0.shape[2]
    half = size_x // 2
    rows = half * size_y
    count = cells.shape[1]
    x = cells[0:1, :] - lax.axis_index("gx") * size_x
    y = cells[1:2, :] - lax.axis_index("gy") * size_y
    inside = (x >= 0) & (x < size_x) & (y >= 0) & (y < size_y)
    place = jnp.where(inside, x * size_y + y, -1)
    deep = index((depth, count), 0) == cells[2:3, :]
    parts = [three(jnp.where(deep, res[n : n + 1, :], 0.0)) for n in range(2)]
    for part in range(2):
        at = index((rows, count), 0) + part * rows
        flat = jnp.where(at == place, 1.0, 0.0).astype(jnp.bfloat16)
        for n, out in enumerate((inject0, inject1)):
            done = sum(
                lax.dot_general(flat, p, (((1,), (1,)), ((), ())), preferred_element_type=F32) for p in parts[n]
            )
            out[part * half : (part + 1) * half] = done.reshape(half, size_y, depth)


def first_inner_kernel(wave1, yb, ya, next0, next1, cell, amp, lap1, flat, along_y, along_z, outer, row):
    size_x, size_y = wave1.shape[0], wave1.shape[1]
    difference_matrices(size_y, along_y, along_z)
    outer_matrices(size_x, size_y, outer)
    flat_part(wave1, along_y, along_z, flat)
    half = size_x // 2
    for part in range(2):
        row[part * half : (part + 1) * half] = outer_part(ya, yb, 0, outer, part)
    planes = within(wave1)
    for z in halves():
        for x in range(size_x):
            lap = across(planes, x, z) + flat[x, :, z] * (1.0 / SCALE)
            lap1[x, :, z] = lap + spread(row[x, :, z], size_y)


def first_kernel(inner, xb, xa, lap1, side):
    size_x = lap1.shape[0]
    outside_x(xa, xb, 0, side)
    lap1[0:4] = inner[0:4] + side[0:4]
    lap1[size_x - 4 : size_x] = inner[size_x - 4 : size_x] + side[4:8]


def second_kernel(
    offsets, column, lap1, wave0, wave1, adj4, cell, amp, vel, wave2, image, ya, yb, xa, xb
):
    size_x, size_y = wave1.shape[0], wave1.shape[1]
    start = offsets[0]
    low = start // HALF
    shift_by = lax.rem(start, HALF)
    back = lax.rem(HALF - shift_by, HALF)
    third = jnp.minimum(low + 2, 3)

    plane, amounts = source_of(cell, amp, 0, size_x, size_y)

    def body(x, _):
        lane = lax.broadcasted_iota(jnp.int32, (size_y, HALF), 1)
        rolled = [pltpu.roll(column[i, x], back, 1) for i in (low, low + 1, third)]
        for h, z in enumerate(halves()):
            v = jnp.where(lane < HALF - shift_by, rolled[h], rolled[h + 1])
            vel[x, :, z] = v
            image[x, :, z] = v * adj4[x, :, z]
            wave = 2.0 * wave1[x, :, z] - wave0[x, :, z] + v * lap1[x, :, z]
            wave2[x, :, z] = wave + jnp.where(plane == x, amounts[h], 0.0)
        return 0

    lax.fori_loop(0, size_x, body, 0, unroll=4)
    put_edges(wave2, 0, ya, yb, xa, xb, 0)
    put_edges(image, 4, ya, yb, xa, xb, 4)


def third_inner_kernel(
    wave1, wave2, adj4, adj5, vel, image, cell, amp, inject, along_y, along_z,
    lap2, wave3, adj3, flat, flat2,
):
    flat_part(wave2, along_y, along_z, flat)
    flat_part(image, along_y, along_z, flat2)
    plane, amounts = source_of(cell, amp, 1, wave1.shape[0], wave1.shape[1])
    waves, images = within(wave2), within(image)
    for h, z in enumerate(halves()):
        for x in range(wave1.shape[0]):
            lap = across(waves, x, z) + flat[x, :, z] * (1.0 / SCALE)
            lap2[x, :, z] = lap
            wave = 2.0 * waves(x, z) - wave1[x, :, z] + vel[x, :, z] * lap
            wave3[x, :, z] = wave + jnp.where(plane == x, amounts[h], 0.0)
            adj = across(images, x, z) + flat2[x, :, z] * (1.0 / SCALE)
            adj3[x, :, z] = 2.0 * adj4[x, :, z] - adj5[x, :, z] + adj + inject[x, :, z]


def third_kernel(
    yb, ya, xb, xa, lap2_in, wave3_in, adj3_in, vel, outer,
    lap2, wave3, adj3, image3, pya, pyb, pxa, pxb, side, side2, row, row2,
):
    outer_parts(ya, yb, xa, xb, outer, (side, side2), (row, row2))
    for x in range(vel.shape[0]):
        for z in halves():
            v = vel[x, :, z]
            extra = outer_of(side, row, x, z)
            lap2[x, :, z] = lap2_in[x, :, z] + extra
            wave3[x, :, z] = wave3_in[x, :, z] + v * extra
            adj = adj3_in[x, :, z] + outer_of(side2, row2, x, z)
            adj3[x, :, z] = adj
            image3[x, :, z] = v * adj
    put_edges(wave3, 0, pya, pyb, pxa, pxb, 0)
    put_edges(image3, 4, pya, pyb, pxa, pxb, 4)


def fourth_inner_kernel(
    wave3, image3, adj3, adj4, lap1, lap2, inject, along_y, along_z,
    adj2, grad, flat, flat2,
):
    flat_part(wave3, along_y, along_z, flat)
    flat_part(image3, along_y, along_z, flat2)
    waves, images = within(wave3), within(image3)
    for z in halves():
        for x in range(wave3.shape[0]):
            lap3 = across(waves, x, z) + flat[x, :, z] * (1.0 / SCALE)
            adj = across(images, x, z) + flat2[x, :, z] * (1.0 / SCALE)
            old, mid = adj4[x, :, z], adj3[x, :, z]
            adj = 2.0 * mid - old + adj + inject[x, :, z]
            adj2[x, :, z] = adj
            grad[x, :, z] = old * lap3 + mid * lap2[x, :, z] + adj * lap1[x, :, z]


def fourth_kernel(
    offsets, yb, ya, xb, xa, grad_in, adj4, lap1, outer,
    far, near_b, near_a, own, extra2, side, side2, row, row2,
):
    size_x, size_y = adj4.shape[0], adj4.shape[1]
    outer_parts(ya, yb, xa, xb, outer, (side, side2), (row, row2))
    start = offsets[0]
    low = start // HALF
    shift_by = lax.rem(start, HALF)

    me = lax.axis_index("shot")
    turn = jnp.where(even("shot"), 1, 3)
    which = [(lax.rem(me + away, 4) - low, tile) for away, tile in ((2, far), (turn, near_a), (4 - turn, near_b), (0, own))]

    lane = lax.broadcasted_iota(jnp.int32, (size_y, HALF), 1)
    high = lane >= shift_by
    for x in range(size_x):
        rolled = []
        for z in halves():
            more = outer_of(side2, row2, x, z)
            extra2[x, :, z] = more
            grad = grad_in[x, :, z] + adj4[x, :, z] * outer_of(side, row, x, z) + lap1[x, :, z] * more
            rolled.append(pltpu.roll(grad, shift_by, 1))
        first = jnp.where(high, rolled[0], 0.0)
        second = jnp.where(high, rolled[1], rolled[0])
        third = jnp.where(high, 0.0, rolled[1])
        for n, tile in which:
            value = jnp.where(n == 0, first, jnp.where(n == 1, second, third))
            tile[x] = jnp.where((n >= 0) & (n <= 2), value, 0.0)


def adjoint_kernel(adj2_in, extra, adj2):
    adj2[...] = adj2_in[...] + extra[...]


def sum_kernel(own, far, b, a, out):
    out[...] = (own[...] + far[...]) + (a[...] + b[...])


def local(model_vel2, offsets, wave_prev, wave_cur, adj_cur, adj_next, src_cell, src_amp, rec_cell, rec_res):
    size_x, size_y, depth = wave_cur.shape[1:]
    wave0, wave1, adj4, adj5 = wave_prev[0], wave_cur[0], adj_cur[0], adj_next[0]
    block = shaped(size_x, size_y, depth)
    edge_y, edge_x = shaped(size_x, 8, depth), shaped(8, size_y, depth)
    tile = shaped(size_x, size_y, HALF)
    whole = pltpu.VMEM((size_x, size_y, depth), F32)
    side = pltpu.VMEM((8, size_y, depth), F32)
    rows, bf16 = size_x // 2 * size_y, jnp.bfloat16
    rows8 = pltpu.VMEM((size_x, 8, depth), F32)

    copies = pl.pallas_call(
        copies_kernel,
        out_shape=shaped(4, size_x, size_y, HALF),
        in_specs=[pl.BlockSpec(memory_space=pltpu.HBM)],
        out_specs=pl.BlockSpec(memory_space=pltpu.HBM),
        scratch_shapes=[pltpu.SemaphoreType.DMA((4,))],
        compiler_params=pltpu.CompilerParams(vmem_limit_bytes=1 << 20),
    )(model_vel2)
    column = lax.all_to_all(copies, "shot", 0, 0)
    edges = call(
        edges_kernel, (shaped(size_x // 2, 8, depth),) * 2 + (shaped(4, size_y, depth),) * 2, n_in=1, room=1
    )(wave1)
    halos = exchange(edges)
    yb, ya, xb, xa = halos
    matrices = ((rows, rows), (depth, depth), (2, size_x // 2 * 8, size_x // 2 * 16))
    own = tuple(pltpu.VMEM(dims, bf16) for dims in matrices)
    lap1 = call(first_inner_kernel, block, (whole, *own, rows8), n_in=7, room=2)(
        wave1, yb, ya, wave0, adj4, src_cell, src_amp
    )
    lap1 = call(first_kernel, block, (side,), n_in=3, room=1, aliases={0: 0})(lap1, xb, xa)
    vel, wave2, image, *edges = call(
        second_kernel, (block,) * 3 + (edge_y,) * 2 + (edge_x,) * 2,
        smem=1, n_in=7, room=4,
    )(offsets, column, lap1, wave0, wave1, adj4, src_cell, src_amp)
    inject0, inject1, along_y, along_z, outer = pl.pallas_call(
        functools.partial(tables_kernel, size_x, size_y),
        out_shape=(block, block, *(jax.ShapeDtypeStruct(dims, bf16) for dims in matrices)),
        in_specs=[pl.BlockSpec(memory_space=pltpu.VMEM)] * 2 + [pl.BlockSpec(memory_space=pl.ANY)],
        out_specs=(pl.BlockSpec(memory_space=pltpu.VMEM),) * 5,
        compiler_params=pltpu.CompilerParams(vmem_limit_bytes=4 << 20),
    )(jnp.transpose(rec_cell[0]), jnp.transpose(rec_res[0]), vel)
    halos = exchange(edges)
    inner = call(third_inner_kernel, (block,) * 3, (whole,) * 2, n_in=11, room=10)(
        wave1, wave2, adj4, adj5, vel, image, src_cell, src_amp, inject0, along_y, along_z
    )
    lap2, wave3, adj3, image3, *edges = call(
        third_kernel, (block,) * 4 + (edge_y,) * 2 + (edge_x,) * 2, (side, side, rows8, rows8), n_in=9,
        room=10, aliases={4: 0, 5: 1, 6: 2},
    )(*halos, *inner, vel, outer)
    halos = exchange(edges)
    inner_adj2, inner_grad = call(fourth_inner_kernel, (block,) * 2, (whole,) * 2, n_in=9, room=10)(
        wave3, image3, adj3, adj4, lap1, lap2, inject1, along_y, along_z
    )
    far, near_b, near_a, own, extra = call(
        fourth_kernel, (tile, tile, tile, tile, block), (side, side, rows8, rows8), smem=1, n_in=8, room=10
    )(offsets, *halos, inner_grad, adj4, lap1, outer)
    far, b, a = swap_across(far), swap_shot(near_b, 1), swap_shot(near_a, 0)
    adj2 = call(adjoint_kernel, block, n_in=2)(inner_adj2, extra)
    owned = call(sum_kernel, tile, n_in=4)(own, far, b, a)
    return owned, adj2[None]


def solution(mesh):
    return jax.shard_map(
        local,
        mesh=mesh,
        in_specs=(
            P("gx", "gy", "shot"),
            P("shot"),
            P("shot", "gx", "gy", None),
            P("shot", "gx", "gy", None),
            P("shot", "gx", "gy", None),
            P("shot", "gx", "gy", None),
            P("shot", None),
            P("shot", None),
            P("shot", None, None),
            P("shot", None, None),
        ),
        out_specs=(P("gx", "gy", "shot"), P("shot", "gx", "gy", None)),
        check_vma=False,
    )
```

```python
import functools

import jax
import jax.numpy as jnp
from jax import lax
from jax.experimental import pallas as pl
from jax.experimental.pallas import tpu as pltpu
from jax.sharding import PartitionSpec as P

COEF = (-205.0 / 72.0, 8.0 / 5.0, -1.0 / 5.0, 8.0 / 315.0, -1.0 / 560.0)
SCALE = 5040.0
WEIGHT = (0.0, 8064.0, -1008.0, 128.0, -9.0)
F32 = jnp.float32
HALF = 128


def swap(value, axis, odd):
    pairs = []
    for i in range(odd, lax.axis_size(axis) - 1, 2):
        pairs += [(i, i + 1), (i + 1, i)]
    return lax.ppermute(value, axis, pairs)


def swap_shot(value, odd):
    size = lax.axis_size("shot")
    pairs = []
    for i in range(odd, size, 2):
        pairs += [(i, (i + 1) % size), ((i + 1) % size, i)]
    return lax.ppermute(value, "shot", pairs)


def swap_across(value):
    size = lax.axis_size("shot")
    return lax.ppermute(value, "shot", [(i, (i + size // 2) % size) for i in range(size)])


def exchange(payload):
    ya, yb, xa, xb = payload
    return swap(yb, "gy", 1), swap(ya, "gy", 0), swap(xb, "gx", 1), swap(xa, "gx", 0)


def call(body, out_shape, scratch=(), smem=0, n_in=0, room=4, aliases=None, flops=0):
    vmem = pl.BlockSpec(memory_space=pltpu.VMEM)
    scal = pl.BlockSpec(memory_space=pltpu.SMEM)
    return pl.pallas_call(
        body,
        out_shape=out_shape,
        in_specs=[scal] * smem + [vmem] * n_in,
        out_specs=jax.tree.map(lambda _: vmem, out_shape),
        scratch_shapes=list(scratch),
        input_output_aliases=aliases or {},
        cost_estimate=pl.CostEstimate(flops=flops, bytes_accessed=0, transcendentals=0),
        compiler_params=pltpu.CompilerParams(vmem_limit_bytes=room << 20),
    )


def shaped(*dims):
    return jax.ShapeDtypeStruct(dims, F32)


def even(axis):
    return lax.rem(lax.axis_index(axis), 2) == 0


def weight(distance):
    distance = jnp.abs(distance)
    total = jnp.zeros(distance.shape, F32)
    for k in range(1, 5):
        total = jnp.where(distance == k, WEIGHT[k], total)
    return total


def three(value):
    first = value.astype(jnp.bfloat16)
    rest = value - first.astype(F32)
    second = rest.astype(jnp.bfloat16)
    return first, second, (rest - second.astype(F32)).astype(jnp.bfloat16)


def product(a, b):
    return jnp.dot(a, b, preferred_element_type=F32)


def flat_part(field, along_y, along_z, out):
    size_x, size_y, depth = field.shape
    chunk = along_y.shape[0] // size_y
    for at in range(0, size_x, chunk):
        parts = three(field[at : at + chunk].reshape(chunk * size_y, depth))
        total = sum(product(part, along_z[...]) + product(along_y[...], part) for part in parts)
        out[at : at + chunk] = total.reshape(chunk, size_y, depth)


def outer_part(ya, yb, at, outer):
    depth = ya.shape[2]
    fields, rows = outer.shape[0], outer.shape[1]
    chunk = rows // 8
    a, b = (m[at : at + chunk].reshape(chunk * 8, depth) for m in (ya, yb))
    even_y = even("gy")
    below, above = three(jnp.where(even_y, b, a)), three(jnp.where(even_y, a, b))
    matrix = outer[...].reshape(fields * rows, outer.shape[2])
    total = sum(product(matrix, jnp.concatenate(pair, axis=0)) for pair in zip(below, above))
    return total.reshape(fields, chunk, 8, depth) * (1.0 / SCALE)


def spread(rows, size_y):
    first = lax.broadcasted_iota(jnp.int32, rows.shape, 0) < 4
    middle = [jnp.zeros((size_y - 16, rows.shape[1]), F32)] if size_y > 16 else []
    return jnp.concatenate([jnp.where(first, rows, 0.0)] + middle + [jnp.where(first, 0.0, rows)], axis=0)


def outside_x(xa, xb, plane, out):
    even_x = even("gx")
    low = [jnp.where(even_x, xb[plane + i], xa[plane + i]) for i in range(4)]
    high = [jnp.where(even_x, xa[plane + i], xb[plane + i]) for i in range(4)]
    for i in range(4):
        first, last = 0.0, 0.0
        for k in range(i + 1, 5):
            first = first + COEF[k] * low[4 + i - k]
            last = last + COEF[k] * high[k - i - 1]
        out[i] = first
        out[7 - i] = last


def outer_parts(ya, yb, xa, xb, outer, sides, rows):
    chunk = outer.shape[1] // 8
    for at in range(0, rows[0].shape[0], chunk):
        both = outer_part(ya, yb, at, outer)
        for field, row in enumerate(rows):
            row[at : at + chunk] = both[field]
    for field, side in enumerate(sides):
        outside_x(xa, xb, 4 * field, side)


def outer_of(side, row, x, z):
    size_x, size_y = row.shape[0], side.shape[1]
    extra = spread(row[x, :, z], size_y)
    if x < 4:
        extra = extra + side[x, :, z]
    if x >= size_x - 4:
        extra = extra + side[x - (size_x - 8), :, z]
    return extra


def across(plane, x, z):
    total = (3.0 * COEF[0]) * plane(x, z)
    for k in range(1, 5):
        near = [p for p in (plane(x - k, z), plane(x + k, z)) if p is not None]
        if near:
            total = total + COEF[k] * sum(near[1:], near[0])
    return total


def within(field):
    size_x, held = field.shape[0], {}

    def plane(x, z):
        if not 0 <= x < size_x:
            return None
        if (x, z.start) not in held:
            held[x, z.start] = field[x, :, z]
        return held[x, z.start]

    return plane


def halves():
    return [slice(h * HALF, (h + 1) * HALF) for h in range(2)]


def put_edges(field, row, ya, yb, xa, xb, plane):
    even_y, even_x = even("gy"), even("gx")
    size_x, size_y = field.shape[0], field.shape[1]
    first, last = field[:, 0:4, :], field[:, size_y - 4 : size_y, :]
    ya[:, row : row + 4, :] = jnp.where(even_y, last, first)
    yb[:, row : row + 4, :] = jnp.where(even_y, first, last)
    top = size_x - 4
    xa[plane : plane + 4] = field[pl.ds(jnp.where(even_x, top, 0), 4)]
    xb[plane : plane + 4] = field[pl.ds(jnp.where(even_x, 0, top), 4)]


def copies_kernel(tile, out, sems):
    moves = [pltpu.make_async_copy(tile, out.at[n], sems.at[n]) for n in range(4)]
    for move in moves:
        move.start()
    for move in moves:
        move.wait()


def edges_kernel(field, ya, yb, xa, xb):
    even_y, even_x = even("gy"), even("gx")
    size_x, size_y = field.shape[0], field.shape[1]
    half = size_x // 2
    for part in range(2):
        x = slice(part * half, (part + 1) * half)
        first, last = field[x, 0:4, :], field[x, size_y - 4 : size_y, :]
        ya[:, part * 4 : part * 4 + 4, :] = jnp.where(even_y, last, first)
        yb[:, part * 4 : part * 4 + 4, :] = jnp.where(even_y, first, last)
    top = size_x - 4
    xa[...] = field[pl.ds(jnp.where(even_x, top, 0), 4)]
    xb[...] = field[pl.ds(jnp.where(even_x, 0, top), 4)]


def source_of(cell, amp, step, size_x, size_y):
    shape = (size_y, HALF)

    def one(array, n):
        return jnp.broadcast_to(array[0:1, n : n + 1], shape)

    x = one(cell, 0) - lax.axis_index("gx") * size_x
    y = one(cell, 1) - lax.axis_index("gy") * size_y
    at_y = lax.broadcasted_iota(jnp.int32, shape, 0) == y
    z = lax.broadcasted_iota(jnp.int32, shape, 1)
    return x, [jnp.where(at_y & (z + h * HALF == one(cell, 2)), one(amp, step), 0.0) for h in range(2)]


def index(shape, dim):
    return lax.broadcasted_iota(jnp.int32, shape, dim)


def difference_matrices(size_y, along_y, along_z):
    shape = along_z.shape
    along_z[...] = weight(index(shape, 0) - index(shape, 1)).astype(jnp.bfloat16)
    here, there = index(along_y.shape, 0), index(along_y.shape, 1)
    near = jnp.where(here // size_y == there // size_y, weight(here - there), 0.0)
    along_y[...] = near.astype(jnp.bfloat16)


def outer_matrices(size_x, size_y, outer):
    half = size_x // 2
    shape = (half * 8, half * 8)
    here, there = index(shape, 0), index(shape, 1)
    y, row = lax.rem(here, 8), lax.rem(there, 4)
    y = jnp.where(y < 4, y, y + size_y - 8)
    below, above = weight(y - row + 4), weight(row + size_y - y)
    for field in range(2):
        use = (here // 8 == there // 8) & (lax.rem(there, 8) // 4 == field)
        both = jnp.concatenate([jnp.where(use, below, 0.0), jnp.where(use, above, 0.0)], axis=1)
        outer[field] = both.astype(jnp.bfloat16)


def tables_kernel(size_x, size_y, cells, res, other, inject0, inject1, along_y, along_z, outer):
    difference_matrices(size_y, along_y, along_z)
    outer_matrices(size_x, size_y, outer)
    depth = inject0.shape[2]
    half = size_x // 2
    rows = half * size_y
    count = cells.shape[1]
    x = cells[0:1, :] - lax.axis_index("gx") * size_x
    y = cells[1:2, :] - lax.axis_index("gy") * size_y
    inside = (x >= 0) & (x < size_x) & (y >= 0) & (y < size_y)
    place = jnp.where(inside, x * size_y + y, -1)
    deep = index((depth, count), 0) == cells[2:3, :]
    parts = [three(jnp.where(deep, res[n : n + 1, :], 0.0)) for n in range(2)]
    for part in range(2):
        at = index((rows, count), 0) + part * rows
        flat = jnp.where(at == place, 1.0, 0.0).astype(jnp.bfloat16)
        for n, out in enumerate((inject0, inject1)):
            done = sum(
                lax.dot_general(flat, p, (((1,), (1,)), ((), ())), preferred_element_type=F32) for p in parts[n]
            )
            out[part * half : (part + 1) * half] = done.reshape(half, size_y, depth)


def first_inner_kernel(wave1, yb, ya, next0, next1, cell, amp, lap1, flat, along_y, along_z, outer, row):
    size_x, size_y = wave1.shape[0], wave1.shape[1]
    difference_matrices(size_y, along_y, along_z)
    outer_matrices(size_x, size_y, outer)
    flat_part(wave1, along_y, along_z, flat)
    both = outer_part(ya, yb, 0, outer)
    row[...] = both.reshape(size_x, 8, both.shape[3])
    planes = within(wave1)
    for z in halves():
        for x in range(size_x):
            lap = across(planes, x, z) + flat[x, :, z] * (1.0 / SCALE)
            lap1[x, :, z] = lap + spread(row[x, :, z], size_y)


def first_kernel(inner, xb, xa, lap1, side):
    size_x = lap1.shape[0]
    outside_x(xa, xb, 0, side)
    lap1[0:4] = inner[0:4] + side[0:4]
    lap1[size_x - 4 : size_x] = inner[size_x - 4 : size_x] + side[4:8]


def second_kernel(
    offsets, column, lap1, wave0, wave1, adj4, cell, amp, vel, wave2, image, ya, yb, xa, xb
):
    size_x, size_y = wave1.shape[0], wave1.shape[1]
    start = offsets[0]
    low = start // HALF
    shift_by = lax.rem(start, HALF)
    back = lax.rem(HALF - shift_by, HALF)
    third = jnp.minimum(low + 2, 3)

    plane, amounts = source_of(cell, amp, 0, size_x, size_y)

    def body(x, _):
        lane = lax.broadcasted_iota(jnp.int32, (size_y, HALF), 1)
        rolled = [pltpu.roll(column[i, x], back, 1) for i in (low, low + 1, third)]
        for h, z in enumerate(halves()):
            v = jnp.where(lane < HALF - shift_by, rolled[h], rolled[h + 1])
            vel[x, :, z] = v
            image[x, :, z] = v * adj4[x, :, z]
            wave = 2.0 * wave1[x, :, z] - wave0[x, :, z] + v * lap1[x, :, z]
            wave2[x, :, z] = wave + jnp.where(plane == x, amounts[h], 0.0)
        return 0

    lax.fori_loop(0, size_x, body, 0, unroll=4)
    put_edges(wave2, 0, ya, yb, xa, xb, 0)
    put_edges(image, 4, ya, yb, xa, xb, 4)


def third_inner_kernel(
    wave1, wave2, adj4, adj5, vel, image, cell, amp, inject, along_y, along_z,
    lap2, wave3, adj3, flat, flat2,
):
    flat_part(wave2, along_y, along_z, flat)
    flat_part(image, along_y, along_z, flat2)
    plane, amounts = source_of(cell, amp, 1, wave1.shape[0], wave1.shape[1])
    waves, images = within(wave2), within(image)
    for h, z in enumerate(halves()):
        for x in range(wave1.shape[0]):
            lap = across(waves, x, z) + flat[x, :, z] * (1.0 / SCALE)
            lap2[x, :, z] = lap
            wave = 2.0 * waves(x, z) - wave1[x, :, z] + vel[x, :, z] * lap
            wave3[x, :, z] = wave + jnp.where(plane == x, amounts[h], 0.0)
            adj = across(images, x, z) + flat2[x, :, z] * (1.0 / SCALE)
            adj3[x, :, z] = 2.0 * adj4[x, :, z] - adj5[x, :, z] + adj + inject[x, :, z]


def third_kernel(
    yb, ya, xb, xa, lap2_in, wave3_in, adj3_in, vel, outer,
    lap2, wave3, adj3, image3, pya, pyb, pxa, pxb, side, side2, row, row2,
):
    outer_parts(ya, yb, xa, xb, outer, (side, side2), (row, row2))
    for x in range(vel.shape[0]):
        for z in halves():
            v = vel[x, :, z]
            extra = outer_of(side, row, x, z)
            lap2[x, :, z] = lap2_in[x, :, z] + extra
            wave3[x, :, z] = wave3_in[x, :, z] + v * extra
            adj = adj3_in[x, :, z] + outer_of(side2, row2, x, z)
            adj3[x, :, z] = adj
            image3[x, :, z] = v * adj
    put_edges(wave3, 0, pya, pyb, pxa, pxb, 0)
    put_edges(image3, 4, pya, pyb, pxa, pxb, 4)


def fourth_inner_kernel(
    wave3, image3, adj3, adj4, lap1, lap2, inject, along_y, along_z,
    adj2, grad, flat, flat2,
):
    flat_part(wave3, along_y, along_z, flat)
    flat_part(image3, along_y, along_z, flat2)
    waves, images = within(wave3), within(image3)
    for z in halves():
        for x in range(wave3.shape[0]):
            lap3 = across(waves, x, z) + flat[x, :, z] * (1.0 / SCALE)
            adj = across(images, x, z) + flat2[x, :, z] * (1.0 / SCALE)
            old, mid = adj4[x, :, z], adj3[x, :, z]
            adj = 2.0 * mid - old + adj + inject[x, :, z]
            adj2[x, :, z] = adj
            grad[x, :, z] = old * lap3 + mid * lap2[x, :, z] + adj * lap1[x, :, z]


def fourth_kernel(
    offsets, yb, ya, xb, xa, grad_in, adj4, lap1, outer,
    far, near_b, near_a, own, extra2, side, side2, row, row2,
):
    size_x, size_y = adj4.shape[0], adj4.shape[1]
    outer_parts(ya, yb, xa, xb, outer, (side, side2), (row, row2))
    start = offsets[0]
    low = start // HALF
    shift_by = lax.rem(start, HALF)

    me = lax.axis_index("shot")
    turn = jnp.where(even("shot"), 1, 3)
    which = [(lax.rem(me + away, 4) - low, tile) for away, tile in ((2, far), (turn, near_a), (4 - turn, near_b), (0, own))]

    lane = lax.broadcasted_iota(jnp.int32, (size_y, HALF), 1)
    high = lane >= shift_by
    for x in range(size_x):
        rolled = []
        for z in halves():
            more = outer_of(side2, row2, x, z)
            extra2[x, :, z] = more
            grad = grad_in[x, :, z] + adj4[x, :, z] * outer_of(side, row, x, z) + lap1[x, :, z] * more
            rolled.append(pltpu.roll(grad, shift_by, 1))
        first = jnp.where(high, rolled[0], 0.0)
        second = jnp.where(high, rolled[1], rolled[0])
        third = jnp.where(high, 0.0, rolled[1])
        for n, tile in which:
            value = jnp.where(n == 0, first, jnp.where(n == 1, second, third))
            tile[x] = jnp.where((n >= 0) & (n <= 2), value, 0.0)


def adjoint_kernel(adj2_in, extra, adj2):
    adj2[...] = adj2_in[...] + extra[...]


def sum_kernel(own, far, b, a, out):
    out[...] = (own[...] + far[...]) + (a[...] + b[...])


def local(model_vel2, offsets, wave_prev, wave_cur, adj_cur, adj_next, src_cell, src_amp, rec_cell, rec_res):
    size_x, size_y, depth = wave_cur.shape[1:]
    wave0, wave1, adj4, adj5 = wave_prev[0], wave_cur[0], adj_cur[0], adj_next[0]
    block = shaped(size_x, size_y, depth)
    edge_y, edge_x = shaped(size_x, 8, depth), shaped(8, size_y, depth)
    tile = shaped(size_x, size_y, HALF)
    whole = pltpu.VMEM((size_x, size_y, depth), F32)
    side = pltpu.VMEM((8, size_y, depth), F32)
    rows, bf16 = size_x // 2 * size_y, jnp.bfloat16
    rows8 = pltpu.VMEM((size_x, 8, depth), F32)

    copies = pl.pallas_call(
        copies_kernel,
        out_shape=shaped(4, size_x, size_y, HALF),
        in_specs=[pl.BlockSpec(memory_space=pltpu.HBM)],
        out_specs=pl.BlockSpec(memory_space=pltpu.HBM),
        scratch_shapes=[pltpu.SemaphoreType.DMA((4,))],
        compiler_params=pltpu.CompilerParams(vmem_limit_bytes=1 << 20),
    )(model_vel2)
    column = lax.all_to_all(copies, "shot", 0, 0)
    edges = call(
        edges_kernel, (shaped(size_x // 2, 8, depth),) * 2 + (shaped(4, size_y, depth),) * 2, n_in=1, room=1
    )(wave1)
    halos = exchange(edges)
    yb, ya, xb, xa = halos
    matrices = ((rows, rows), (depth, depth), (2, size_x // 2 * 8, size_x // 2 * 16))
    own = tuple(pltpu.VMEM(dims, bf16) for dims in matrices)
    lap1 = call(first_inner_kernel, block, (whole, *own, rows8), n_in=7, room=2)(
        wave1, yb, ya, wave0, adj4, src_cell, src_amp
    )
    lap1 = call(first_kernel, block, (side,), n_in=3, room=1, aliases={0: 0})(lap1, xb, xa)
    vel, wave2, image, *edges = call(
        second_kernel, (block,) * 3 + (edge_y,) * 2 + (edge_x,) * 2,
        smem=1, n_in=7, room=4,
    )(offsets, column, lap1, wave0, wave1, adj4, src_cell, src_amp)
    inject0, inject1, along_y, along_z, outer = pl.pallas_call(
        functools.partial(tables_kernel, size_x, size_y),
        out_shape=(block, block, *(jax.ShapeDtypeStruct(dims, bf16) for dims in matrices)),
        in_specs=[pl.BlockSpec(memory_space=pltpu.VMEM)] * 2 + [pl.BlockSpec(memory_space=pl.ANY)],
        out_specs=(pl.BlockSpec(memory_space=pltpu.VMEM),) * 5,
        compiler_params=pltpu.CompilerParams(vmem_limit_bytes=4 << 20),
    )(jnp.transpose(rec_cell[0]), jnp.transpose(rec_res[0]), vel)
    halos = exchange(edges)
    inner = call(third_inner_kernel, (block,) * 3, (whole,) * 2, n_in=11, room=10)(
        wave1, wave2, adj4, adj5, vel, image, src_cell, src_amp, inject0, along_y, along_z
    )
    lap2, wave3, adj3, image3, *edges = call(
        third_kernel, (block,) * 4 + (edge_y,) * 2 + (edge_x,) * 2, (side, side, rows8, rows8), n_in=9,
        room=10, aliases={4: 0, 5: 1, 6: 2},
    )(*halos, *inner, vel, outer)
    halos = exchange(edges)
    inner_adj2, inner_grad = call(fourth_inner_kernel, (block,) * 2, (whole,) * 2, n_in=9, room=10)(
        wave3, image3, adj3, adj4, lap1, lap2, inject1, along_y, along_z
    )
    far, near_b, near_a, own, extra = call(
        fourth_kernel, (tile, tile, tile, tile, block), (side, side, rows8, rows8), smem=1, n_in=8, room=10
    )(offsets, *halos, inner_grad, adj4, lap1, outer)
    far, b, a = swap_across(far), swap_shot(near_b, 1), swap_shot(near_a, 0)
    adj2 = call(adjoint_kernel, block, n_in=2)(inner_adj2, extra)
    owned = call(sum_kernel, tile, n_in=4)(own, far, b, a)
    return owned, adj2[None]


def solution(mesh):
    return jax.shard_map(
        local,
        mesh=mesh,
        in_specs=(
            P("gx", "gy", "shot"),
            P("shot"),
            P("shot", "gx", "gy", None),
            P("shot", "gx", "gy", None),
            P("shot", "gx", "gy", None),
            P("shot", "gx", "gy", None),
            P("shot", None),
            P("shot", None),
            P("shot", None, None),
            P("shot", None, None),
        ),
        out_specs=(P("gx", "gy", "shot"), P("shot", "gx", "gy", None)),
        check_vma=False,
    )
```

```python
import functools

import jax
import jax.numpy as jnp
from jax import lax
from jax.experimental import pallas as pl
from jax.experimental.pallas import tpu as pltpu
from jax.sharding import PartitionSpec as P

COEF = (-205.0 / 72.0, 8.0 / 5.0, -1.0 / 5.0, 8.0 / 315.0, -1.0 / 560.0)
SCALE = 5040.0
WEIGHT = (0.0, 8064.0, -1008.0, 128.0, -9.0)
F32 = jnp.float32
HALF = 128


def swap(value, axis, odd):
    pairs = []
    for i in range(odd, lax.axis_size(axis) - 1, 2):
        pairs += [(i, i + 1), (i + 1, i)]
    return lax.ppermute(value, axis, pairs)


def swap_shot(value, odd):
    size = lax.axis_size("shot")
    pairs = []
    for i in range(odd, size, 2):
        pairs += [(i, (i + 1) % size), ((i + 1) % size, i)]
    return lax.ppermute(value, "shot", pairs)


def swap_across(value):
    size = lax.axis_size("shot")
    return lax.ppermute(value, "shot", [(i, (i + size // 2) % size) for i in range(size)])


def exchange(payload):
    ya, yb, xa, xb = payload
    return swap(yb, "gy", 1), swap(ya, "gy", 0), swap(xb, "gx", 1), swap(xa, "gx", 0)


def call(body, out_shape, scratch=(), smem=0, n_in=0, room=4, aliases=None, flops=0):
    vmem = pl.BlockSpec(memory_space=pltpu.VMEM)
    scal = pl.BlockSpec(memory_space=pltpu.SMEM)
    return pl.pallas_call(
        body,
        out_shape=out_shape,
        in_specs=[scal] * smem + [vmem] * n_in,
        out_specs=jax.tree.map(lambda _: vmem, out_shape),
        scratch_shapes=list(scratch),
        input_output_aliases=aliases or {},
        cost_estimate=pl.CostEstimate(flops=flops, bytes_accessed=0, transcendentals=0),
        compiler_params=pltpu.CompilerParams(vmem_limit_bytes=room << 20),
    )


def shaped(*dims):
    return jax.ShapeDtypeStruct(dims, F32)


def even(axis):
    return lax.rem(lax.axis_index(axis), 2) == 0


def weight(distance):
    distance = jnp.abs(distance)
    total = jnp.zeros(distance.shape, F32)
    for k in range(1, 5):
        total = jnp.where(distance == k, WEIGHT[k], total)
    return total


def three(value):
    first = value.astype(jnp.bfloat16)
    rest = value - first.astype(F32)
    second = rest.astype(jnp.bfloat16)
    return first, second, (rest - second.astype(F32)).astype(jnp.bfloat16)


def product(a, b):
    return jnp.dot(a, b, preferred_element_type=F32)


def flat_part(field, along_y, along_z, out):
    size_x, size_y, depth = field.shape
    chunk = along_y.shape[0] // size_y
    for at in range(0, size_x, chunk):
        parts = three(field[at : at + chunk].reshape(chunk * size_y, depth))
        total = sum(product(part, along_z[...]) + product(along_y[...], part) for part in parts)
        out[at : at + chunk] = total.reshape(chunk, size_y, depth)


def outer_part(ya, yb, at, outer):
    depth = ya.shape[2]
    fields, rows = outer.shape[0], outer.shape[1]
    chunk = rows // 8
    a, b = (m[at : at + chunk].reshape(chunk * 8, depth) for m in (ya, yb))
    even_y = even("gy")
    below, above = three(jnp.where(even_y, b, a)), three(jnp.where(even_y, a, b))
    matrix = outer[...].reshape(fields * rows, outer.shape[2])
    total = sum(product(matrix, jnp.concatenate(pair, axis=0)) for pair in zip(below, above))
    return total.reshape(fields, chunk, 8, depth) * (1.0 / SCALE)


def spread(rows, size_y):
    first = lax.broadcasted_iota(jnp.int32, rows.shape, 0) < 4
    middle = [jnp.zeros((size_y - 16, rows.shape[1]), F32)] if size_y > 16 else []
    return jnp.concatenate([jnp.where(first, rows, 0.0)] + middle + [jnp.where(first, 0.0, rows)], axis=0)


def outside_x(xa, xb, plane, out):
    even_x = even("gx")
    low = [jnp.where(even_x, xb[plane + i], xa[plane + i]) for i in range(4)]
    high = [jnp.where(even_x, xa[plane + i], xb[plane + i]) for i in range(4)]
    for i in range(4):
        first, last = 0.0, 0.0
        for k in range(i + 1, 5):
            first = first + COEF[k] * low[4 + i - k]
            last = last + COEF[k] * high[k - i - 1]
        out[i] = first
        out[7 - i] = last


def outer_parts(ya, yb, xa, xb, outer, sides, rows):
    chunk = outer.shape[1] // 8
    for at in range(0, rows[0].shape[0], chunk):
        both = outer_part(ya, yb, at, outer)
        for field, row in enumerate(rows):
            row[at : at + chunk] = both[field]
    for field, side in enumerate(sides):
        outside_x(xa, xb, 4 * field, side)


def outer_of(side, row, x, z):
    size_x, size_y = row.shape[0], side.shape[1]
    extra = spread(row[x, :, z], size_y)
    if x < 4:
        extra = extra + side[x, :, z]
    if x >= size_x - 4:
        extra = extra + side[x - (size_x - 8), :, z]
    return extra


def across(plane, x, z):
    total = (3.0 * COEF[0]) * plane(x, z)
    for k in range(1, 5):
        near = [p for p in (plane(x - k, z), plane(x + k, z)) if p is not None]
        if near:
            total = total + COEF[k] * sum(near[1:], near[0])
    return total


def within(field):
    size_x, held = field.shape[0], {}

    def plane(x, z):
        if not 0 <= x < size_x:
            return None
        if (x, z.start) not in held:
            held[x, z.start] = field[x, :, z]
        return held[x, z.start]

    return plane


def halves():
    return [slice(h * HALF, (h + 1) * HALF) for h in range(2)]


def put_rows(one, two, ya, yb, x, z):
    size_y = one.shape[0]
    upper = lax.broadcasted_iota(jnp.int32, (8, HALF), 0) < 4
    first = jnp.where(upper, one[0:8], pltpu.roll(two[0:8], 4, 0))
    last = jnp.where(upper, pltpu.roll(one[size_y - 8 :], 4, 0), two[size_y - 8 :])
    even_y = even("gy")
    ya[x, :, z] = jnp.where(even_y, last, first)
    yb[x, :, z] = jnp.where(even_y, first, last)


def put_planes(field, xa, xb, plane):
    even_x = even("gx")
    top = field.shape[0] - 4
    xa[plane : plane + 4] = field[pl.ds(jnp.where(even_x, top, 0), 4)]
    xb[plane : plane + 4] = field[pl.ds(jnp.where(even_x, 0, top), 4)]


def copies_kernel(tile, out, sems):
    moves = [pltpu.make_async_copy(tile, out.at[n], sems.at[n]) for n in range(4)]
    for move in moves:
        move.start()
    for move in moves:
        move.wait()


def edges_kernel(field, ya, yb, xa, xb):
    even_y, even_x = even("gy"), even("gx")
    size_x, size_y = field.shape[0], field.shape[1]
    half = size_x // 2
    for part in range(2):
        x = slice(part * half, (part + 1) * half)
        first, last = field[x, 0:4, :], field[x, size_y - 4 : size_y, :]
        ya[:, part * 4 : part * 4 + 4, :] = jnp.where(even_y, last, first)
        yb[:, part * 4 : part * 4 + 4, :] = jnp.where(even_y, first, last)
    top = size_x - 4
    xa[...] = field[pl.ds(jnp.where(even_x, top, 0), 4)]
    xb[...] = field[pl.ds(jnp.where(even_x, 0, top), 4)]


def source_of(cell, amp, step, size_x, size_y):
    shape = (size_y, HALF)

    def one(array, n):
        return jnp.broadcast_to(array[0:1, n : n + 1], shape)

    x = one(cell, 0) - lax.axis_index("gx") * size_x
    y = one(cell, 1) - lax.axis_index("gy") * size_y
    at_y = lax.broadcasted_iota(jnp.int32, shape, 0) == y
    z = lax.broadcasted_iota(jnp.int32, shape, 1)
    return x, [jnp.where(at_y & (z + h * HALF == one(cell, 2)), one(amp, step), 0.0) for h in range(2)]


def index(shape, dim):
    return lax.broadcasted_iota(jnp.int32, shape, dim)


def difference_matrices(size_y, along_y, along_z):
    shape = along_z.shape
    along_z[...] = weight(index(shape, 0) - index(shape, 1)).astype(jnp.bfloat16)
    here, there = index(along_y.shape, 0), index(along_y.shape, 1)
    near = jnp.where(here // size_y == there // size_y, weight(here - there), 0.0)
    along_y[...] = near.astype(jnp.bfloat16)


def outer_matrices(size_x, size_y, outer):
    half = size_x // 2
    shape = (half * 8, half * 8)
    here, there = index(shape, 0), index(shape, 1)
    y, row = lax.rem(here, 8), lax.rem(there, 4)
    y = jnp.where(y < 4, y, y + size_y - 8)
    below, above = weight(y - row + 4), weight(row + size_y - y)
    for field in range(2):
        use = (here // 8 == there // 8) & (lax.rem(there, 8) // 4 == field)
        both = jnp.concatenate([jnp.where(use, below, 0.0), jnp.where(use, above, 0.0)], axis=1)
        outer[field] = both.astype(jnp.bfloat16)


def tables_kernel(size_x, size_y, cells, res, other, inject0, inject1, along_y, along_z, outer):
    difference_matrices(size_y, along_y, along_z)
    outer_matrices(size_x, size_y, outer)
    depth = inject0.shape[2]
    half = size_x // 2
    rows = half * size_y
    count = cells.shape[1]
    x = cells[0:1, :] - lax.axis_index("gx") * size_x
    y = cells[1:2, :] - lax.axis_index("gy") * size_y
    inside = (x >= 0) & (x < size_x) & (y >= 0) & (y < size_y)
    place = jnp.where(inside, x * size_y + y, -1)
    deep = index((depth, count), 0) == cells[2:3, :]
    parts = [three(jnp.where(deep, res[n : n + 1, :], 0.0)) for n in range(2)]
    for part in range(2):
        at = index((rows, count), 0) + part * rows
        flat = jnp.where(at == place, 1.0, 0.0).astype(jnp.bfloat16)
        for n, out in enumerate((inject0, inject1)):
            done = sum(
                lax.dot_general(flat, p, (((1,), (1,)), ((), ())), preferred_element_type=F32) for p in parts[n]
            )
            out[part * half : (part + 1) * half] = done.reshape(half, size_y, depth)


def first_inner_kernel(wave1, yb, ya, next0, next1, cell, amp, lap1, flat, along_y, along_z, outer, row):
    size_x, size_y = wave1.shape[0], wave1.shape[1]
    difference_matrices(size_y, along_y, along_z)
    outer_matrices(size_x, size_y, outer)
    flat_part(wave1, along_y, along_z, flat)
    both = outer_part(ya, yb, 0, outer)
    row[...] = both.reshape(size_x, 8, both.shape[3])
    planes = within(wave1)
    for z in halves():
        for x in range(size_x):
            lap = across(planes, x, z) + flat[x, :, z] * (1.0 / SCALE)
            lap1[x, :, z] = lap + spread(row[x, :, z], size_y)


def first_kernel(inner, xb, xa, lap1, side):
    size_x = lap1.shape[0]
    outside_x(xa, xb, 0, side)
    lap1[0:4] = inner[0:4] + side[0:4]
    lap1[size_x - 4 : size_x] = inner[size_x - 4 : size_x] + side[4:8]


def second_kernel(
    offsets, column, lap1, wave0, wave1, adj4, cell, amp, vel, wave2, image, ya, yb, xa, xb
):
    size_x, size_y = wave1.shape[0], wave1.shape[1]
    start = offsets[0]
    low = start // HALF
    shift_by = lax.rem(start, HALF)
    back = lax.rem(HALF - shift_by, HALF)
    third = jnp.minimum(low + 2, 3)

    plane, amounts = source_of(cell, amp, 0, size_x, size_y)

    def body(x, _):
        lane = lax.broadcasted_iota(jnp.int32, (size_y, HALF), 1)
        rolled = [pltpu.roll(column[i, x], back, 1) for i in (low, low + 1, third)]
        for h, z in enumerate(halves()):
            v = jnp.where(lane < HALF - shift_by, rolled[h], rolled[h + 1])
            vel[x, :, z] = v
            wave = 2.0 * wave1[x, :, z] - wave0[x, :, z] + v * lap1[x, :, z]
            wave = wave + jnp.where(plane == x, amounts[h], 0.0)
            product4 = v * adj4[x, :, z]
            wave2[x, :, z] = wave
            image[x, :, z] = product4
            put_rows(wave, product4, ya, yb, x, z)
        return 0

    lax.fori_loop(0, size_x, body, 0, unroll=4)
    put_planes(wave2, xa, xb, 0)
    put_planes(image, xa, xb, 4)


def third_inner_kernel(
    wave1, wave2, adj4, adj5, vel, image, cell, amp, inject, along_y, along_z,
    lap2, wave3, adj3, flat, flat2,
):
    flat_part(wave2, along_y, along_z, flat)
    flat_part(image, along_y, along_z, flat2)
    plane, amounts = source_of(cell, amp, 1, wave1.shape[0], wave1.shape[1])
    waves, images = within(wave2), within(image)
    for h, z in enumerate(halves()):
        for x in range(wave1.shape[0]):
            lap = across(waves, x, z) + flat[x, :, z] * (1.0 / SCALE)
            lap2[x, :, z] = lap
            wave = 2.0 * waves(x, z) - wave1[x, :, z] + vel[x, :, z] * lap
            wave3[x, :, z] = wave + jnp.where(plane == x, amounts[h], 0.0)
            adj = across(images, x, z) + flat2[x, :, z] * (1.0 / SCALE)
            adj3[x, :, z] = 2.0 * adj4[x, :, z] - adj5[x, :, z] + adj + inject[x, :, z]


def third_kernel(
    yb, ya, xb, xa, lap2_in, wave3_in, adj3_in, vel, outer,
    lap2, wave3, adj3, image3, pya, pyb, pxa, pxb, side, side2, row, row2,
):
    outer_parts(ya, yb, xa, xb, outer, (side, side2), (row, row2))
    for x in range(vel.shape[0]):
        for z in halves():
            v = vel[x, :, z]
            extra = outer_of(side, row, x, z)
            lap2[x, :, z] = lap2_in[x, :, z] + extra
            wave = wave3_in[x, :, z] + v * extra
            wave3[x, :, z] = wave
            adj = adj3_in[x, :, z] + outer_of(side2, row2, x, z)
            adj3[x, :, z] = adj
            image3[x, :, z] = v * adj
            put_rows(wave, v * adj, pya, pyb, x, z)
    put_planes(wave3, pxa, pxb, 0)
    put_planes(image3, pxa, pxb, 4)


def fourth_inner_kernel(
    wave3, image3, adj3, adj4, lap1, lap2, inject, along_y, along_z,
    adj2, grad, flat, flat2,
):
    flat_part(wave3, along_y, along_z, flat)
    flat_part(image3, along_y, along_z, flat2)
    waves, images = within(wave3), within(image3)
    for z in halves():
        for x in range(wave3.shape[0]):
            lap3 = across(waves, x, z) + flat[x, :, z] * (1.0 / SCALE)
            adj = across(images, x, z) + flat2[x, :, z] * (1.0 / SCALE)
            old, mid = adj4[x, :, z], adj3[x, :, z]
            adj = 2.0 * mid - old + adj + inject[x, :, z]
            adj2[x, :, z] = adj
            grad[x, :, z] = old * lap3 + mid * lap2[x, :, z] + adj * lap1[x, :, z]


def fourth_kernel(
    offsets, yb, ya, xb, xa, grad_in, adj4, lap1, outer,
    far, near_b, near_a, own, extra2, side, side2, row, row2,
):
    size_x, size_y = adj4.shape[0], adj4.shape[1]
    outer_parts(ya, yb, xa, xb, outer, (side, side2), (row, row2))
    start = offsets[0]
    low = start // HALF
    shift_by = lax.rem(start, HALF)

    me = lax.axis_index("shot")
    turn = jnp.where(even("shot"), 1, 3)
    which = [(lax.rem(me + away, 4) - low, tile) for away, tile in ((2, far), (turn, near_a), (4 - turn, near_b), (0, own))]

    lane = lax.broadcasted_iota(jnp.int32, (size_y, HALF), 1)
    high = lane >= shift_by
    for x in range(size_x):
        rolled = []
        for z in halves():
            more = outer_of(side2, row2, x, z)
            extra2[x, :, z] = more
            grad = grad_in[x, :, z] + adj4[x, :, z] * outer_of(side, row, x, z) + lap1[x, :, z] * more
            rolled.append(pltpu.roll(grad, shift_by, 1))
        first = jnp.where(high, rolled[0], 0.0)
        second = jnp.where(high, rolled[1], rolled[0])
        third = jnp.where(high, 0.0, rolled[1])
        for n, tile in which:
            value = jnp.where(n == 0, first, jnp.where(n == 1, second, third))
            tile[x] = jnp.where((n >= 0) & (n <= 2), value, 0.0)


def adjoint_kernel(adj2_in, extra, adj2):
    adj2[...] = adj2_in[...] + extra[...]


def sum_kernel(own, far, b, a, out):
    out[...] = (own[...] + far[...]) + (a[...] + b[...])


def local(model_vel2, offsets, wave_prev, wave_cur, adj_cur, adj_next, src_cell, src_amp, rec_cell, rec_res):
    size_x, size_y, depth = wave_cur.shape[1:]
    wave0, wave1, adj4, adj5 = wave_prev[0], wave_cur[0], adj_cur[0], adj_next[0]
    block = shaped(size_x, size_y, depth)
    edge_y, edge_x = shaped(size_x, 8, depth), shaped(8, size_y, depth)
    tile = shaped(size_x, size_y, HALF)
    whole = pltpu.VMEM((size_x, size_y, depth), F32)
    side = pltpu.VMEM((8, size_y, depth), F32)
    rows, bf16 = size_x // 2 * size_y, jnp.bfloat16
    rows8 = pltpu.VMEM((size_x, 8, depth), F32)

    copies = pl.pallas_call(
        copies_kernel,
        out_shape=shaped(4, size_x, size_y, HALF),
        in_specs=[pl.BlockSpec(memory_space=pltpu.HBM)],
        out_specs=pl.BlockSpec(memory_space=pltpu.HBM),
        scratch_shapes=[pltpu.SemaphoreType.DMA((4,))],
        compiler_params=pltpu.CompilerParams(vmem_limit_bytes=1 << 20),
    )(model_vel2)
    column = lax.all_to_all(copies, "shot", 0, 0)
    edges = call(
        edges_kernel, (shaped(size_x // 2, 8, depth),) * 2 + (shaped(4, size_y, depth),) * 2, n_in=1, room=1
    )(wave1)
    halos = exchange(edges)
    yb, ya, xb, xa = halos
    matrices = ((rows, rows), (depth, depth), (2, size_x // 2 * 8, size_x // 2 * 16))
    own = tuple(pltpu.VMEM(dims, bf16) for dims in matrices)
    lap1 = call(first_inner_kernel, block, (whole, *own, rows8), n_in=7, room=2)(
        wave1, yb, ya, wave0, adj4, src_cell, src_amp
    )
    lap1 = call(first_kernel, block, (side,), n_in=3, room=1, aliases={0: 0})(lap1, xb, xa)
    vel, wave2, image, *edges = call(
        second_kernel, (block,) * 3 + (edge_y,) * 2 + (edge_x,) * 2,
        smem=1, n_in=7, room=4,
    )(offsets, column, lap1, wave0, wave1, adj4, src_cell, src_amp)
    inject0, inject1, along_y, along_z, outer = pl.pallas_call(
        functools.partial(tables_kernel, size_x, size_y),
        out_shape=(block, block, *(jax.ShapeDtypeStruct(dims, bf16) for dims in matrices)),
        in_specs=[pl.BlockSpec(memory_space=pltpu.VMEM)] * 2 + [pl.BlockSpec(memory_space=pl.ANY)],
        out_specs=(pl.BlockSpec(memory_space=pltpu.VMEM),) * 5,
        compiler_params=pltpu.CompilerParams(vmem_limit_bytes=4 << 20),
    )(jnp.transpose(rec_cell[0]), jnp.transpose(rec_res[0]), vel)
    halos = exchange(edges)
    inner = call(third_inner_kernel, (block,) * 3, (whole,) * 2, n_in=11, room=10)(
        wave1, wave2, adj4, adj5, vel, image, src_cell, src_amp, inject0, along_y, along_z
    )
    lap2, wave3, adj3, image3, *edges = call(
        third_kernel, (block,) * 4 + (edge_y,) * 2 + (edge_x,) * 2, (side, side, rows8, rows8), n_in=9,
        room=10, aliases={4: 0, 5: 1, 6: 2},
    )(*halos, *inner, vel, outer)
    halos = exchange(edges)
    inner_adj2, inner_grad = call(fourth_inner_kernel, (block,) * 2, (whole,) * 2, n_in=9, room=10)(
        wave3, image3, adj3, adj4, lap1, lap2, inject1, along_y, along_z
    )
    far, near_b, near_a, own, extra = call(
        fourth_kernel, (tile, tile, tile, tile, block), (side, side, rows8, rows8), smem=1, n_in=8, room=10
    )(offsets, *halos, inner_grad, adj4, lap1, outer)
    far, b, a = swap_across(far), swap_shot(near_b, 1), swap_shot(near_a, 0)
    adj2 = call(adjoint_kernel, block, n_in=2)(inner_adj2, extra)
    owned = call(sum_kernel, tile, n_in=4)(own, far, b, a)
    return owned, adj2[None]


def solution(mesh):
    return jax.shard_map(
        local,
        mesh=mesh,
        in_specs=(
            P("gx", "gy", "shot"),
            P("shot"),
            P("shot", "gx", "gy", None),
            P("shot", "gx", "gy", None),
            P("shot", "gx", "gy", None),
            P("shot", "gx", "gy", None),
            P("shot", None),
            P("shot", None),
            P("shot", None, None),
            P("shot", None, None),
        ),
        out_specs=(P("gx", "gy", "shot"), P("shot", "gx", "gy", None)),
        check_vma=False,
    )
```

```python
import functools

import jax
import jax.numpy as jnp
from jax import lax
from jax.experimental import pallas as pl
from jax.experimental.pallas import tpu as pltpu
from jax.sharding import PartitionSpec as P

COEF = (-205.0 / 72.0, 8.0 / 5.0, -1.0 / 5.0, 8.0 / 315.0, -1.0 / 560.0)
SCALE = 5040.0
WEIGHT = (0.0, 8064.0, -1008.0, 128.0, -9.0)
F32 = jnp.float32
HALF = 128


def swap(value, axis, odd):
    pairs = []
    for i in range(odd, lax.axis_size(axis) - 1, 2):
        pairs += [(i, i + 1), (i + 1, i)]
    return lax.ppermute(value, axis, pairs)


def swap_shot(value, odd):
    size = lax.axis_size("shot")
    pairs = []
    for i in range(odd, size, 2):
        pairs += [(i, (i + 1) % size), ((i + 1) % size, i)]
    return lax.ppermute(value, "shot", pairs)


def swap_across(value):
    size = lax.axis_size("shot")
    return lax.ppermute(value, "shot", [(i, (i + size // 2) % size) for i in range(size)])


def exchange(payload):
    ya, yb, xa, xb = payload
    return swap(yb, "gy", 1), swap(ya, "gy", 0), swap(xb, "gx", 1), swap(xa, "gx", 0)


def call(body, out_shape, scratch=(), smem=0, n_in=0, room=4, aliases=None, flops=0):
    vmem = pl.BlockSpec(memory_space=pltpu.VMEM)
    scal = pl.BlockSpec(memory_space=pltpu.SMEM)
    return pl.pallas_call(
        body,
        out_shape=out_shape,
        in_specs=[scal] * smem + [vmem] * n_in,
        out_specs=jax.tree.map(lambda _: vmem, out_shape),
        scratch_shapes=list(scratch),
        input_output_aliases=aliases or {},
        cost_estimate=pl.CostEstimate(flops=flops, bytes_accessed=0, transcendentals=0),
        compiler_params=pltpu.CompilerParams(vmem_limit_bytes=room << 20),
    )


def shaped(*dims):
    return jax.ShapeDtypeStruct(dims, F32)


def even(axis):
    return lax.rem(lax.axis_index(axis), 2) == 0


def weight(distance):
    distance = jnp.abs(distance)
    total = jnp.zeros(distance.shape, F32)
    for k in range(1, 5):
        total = jnp.where(distance == k, WEIGHT[k], total)
    return total


def three(value):
    first = value.astype(jnp.bfloat16)
    rest = value - first.astype(F32)
    second = rest.astype(jnp.bfloat16)
    return first, second, (rest - second.astype(F32)).astype(jnp.bfloat16)


def product(a, b):
    return jnp.dot(a, b, preferred_element_type=F32)


def flat_part(field, along_y, along_z, out):
    size_x, size_y, depth = field.shape
    chunk = along_y.shape[0] // size_y
    for at in range(0, size_x, chunk):
        parts = three(field[at : at + chunk].reshape(chunk * size_y, depth))
        total = sum(product(part, along_z[...]) + product(along_y[...], part) for part in parts)
        out[at : at + chunk] = total.reshape(chunk, size_y, depth)


def outer_part(ya, yb, at, outer):
    depth = ya.shape[2]
    fields, rows = outer.shape[0], outer.shape[1]
    chunk = rows // 8
    a, b = (m[at : at + chunk].reshape(chunk * 8, depth) for m in (ya, yb))
    even_y = even("gy")
    below, above = three(jnp.where(even_y, b, a)), three(jnp.where(even_y, a, b))
    matrix = outer[...].reshape(fields * rows, outer.shape[2])
    total = sum(product(matrix, jnp.concatenate(pair, axis=0)) for pair in zip(below, above))
    return total.reshape(fields, chunk, 8, depth) * (1.0 / SCALE)


def spread(rows, size_y):
    first = lax.broadcasted_iota(jnp.int32, rows.shape, 0) < 4
    middle = [jnp.zeros((size_y - 16, rows.shape[1]), F32)] if size_y > 16 else []
    return jnp.concatenate([jnp.where(first, rows, 0.0)] + middle + [jnp.where(first, 0.0, rows)], axis=0)


def outside_x(xa, xb, plane, out):
    even_x = even("gx")
    low = [jnp.where(even_x, xb[plane + i], xa[plane + i]) for i in range(4)]
    high = [jnp.where(even_x, xa[plane + i], xb[plane + i]) for i in range(4)]
    for i in range(4):
        first, last = 0.0, 0.0
        for k in range(i + 1, 5):
            first = first + COEF[k] * low[4 + i - k]
            last = last + COEF[k] * high[k - i - 1]
        out[i] = first
        out[7 - i] = last


def outer_parts(ya, yb, xa, xb, outer, sides, rows):
    chunk = outer.shape[1] // 8
    for at in range(0, rows[0].shape[0], chunk):
        both = outer_part(ya, yb, at, outer)
        for field, row in enumerate(rows):
            row[at : at + chunk] = both[field]
    for field, side in enumerate(sides):
        outside_x(xa, xb, 4 * field, side)


def outer_of(side, row, x, z):
    size_x, size_y = row.shape[0], side.shape[1]
    extra = spread(row[x, :, z], size_y)
    if x < 4:
        extra = extra + side[x, :, z]
    if x >= size_x - 4:
        extra = extra + side[x - (size_x - 8), :, z]
    return extra


def across(plane, x, z):
    total = (3.0 * COEF[0]) * plane(x, z)
    for k in range(1, 5):
        near = [p for p in (plane(x - k, z), plane(x + k, z)) if p is not None]
        if near:
            total = total + COEF[k] * sum(near[1:], near[0])
    return total


def within(field):
    size_x, held = field.shape[0], {}

    def plane(x, z):
        if not 0 <= x < size_x:
            return None
        if (x, z.start) not in held:
            held[x, z.start] = field[x, :, z]
        return held[x, z.start]

    return plane


def halves():
    return [slice(h * HALF, (h + 1) * HALF) for h in range(2)]


def put_rows(one, two, ya, yb, x, z):
    size_y = one.shape[0]
    upper = lax.broadcasted_iota(jnp.int32, (8, HALF), 0) < 4
    first = jnp.where(upper, one[0:8], pltpu.roll(two[0:8], 4, 0))
    last = jnp.where(upper, pltpu.roll(one[size_y - 8 :], 4, 0), two[size_y - 8 :])
    even_y = even("gy")
    ya[x, :, z] = jnp.where(even_y, last, first)
    yb[x, :, z] = jnp.where(even_y, first, last)


def put_planes(field, xa, xb, plane):
    even_x = even("gx")
    top = field.shape[0] - 4
    xa[plane : plane + 4] = field[pl.ds(jnp.where(even_x, top, 0), 4)]
    xb[plane : plane + 4] = field[pl.ds(jnp.where(even_x, 0, top), 4)]


def copies_kernel(tile, out, sems):
    moves = [pltpu.make_async_copy(tile, out.at[n], sems.at[n]) for n in range(4)]
    for move in moves:
        move.start()
    for move in moves:
        move.wait()


def edges_kernel(field, ya, yb, xa, xb):
    even_y, even_x = even("gy"), even("gx")
    size_x, size_y = field.shape[0], field.shape[1]
    half = size_x // 2
    for part in range(2):
        x = slice(part * half, (part + 1) * half)
        first, last = field[x, 0:4, :], field[x, size_y - 4 : size_y, :]
        ya[:, part * 4 : part * 4 + 4, :] = jnp.where(even_y, last, first)
        yb[:, part * 4 : part * 4 + 4, :] = jnp.where(even_y, first, last)
    top = size_x - 4
    xa[...] = field[pl.ds(jnp.where(even_x, top, 0), 4)]
    xb[...] = field[pl.ds(jnp.where(even_x, 0, top), 4)]


def source_of(cell, amp, step, size_x, size_y):
    shape = (size_y, HALF)

    def one(array, n):
        return jnp.broadcast_to(array[0:1, n : n + 1], shape)

    x = one(cell, 0) - lax.axis_index("gx") * size_x
    y = one(cell, 1) - lax.axis_index("gy") * size_y
    at_y = lax.broadcasted_iota(jnp.int32, shape, 0) == y
    z = lax.broadcasted_iota(jnp.int32, shape, 1)
    return x, [jnp.where(at_y & (z + h * HALF == one(cell, 2)), one(amp, step), 0.0) for h in range(2)]


def index(shape, dim):
    return lax.broadcasted_iota(jnp.int32, shape, dim)


def difference_matrices(size_y, along_y, along_z):
    shape = along_z.shape
    along_z[...] = weight(index(shape, 0) - index(shape, 1)).astype(jnp.bfloat16)
    here, there = index(along_y.shape, 0), index(along_y.shape, 1)
    near = jnp.where(here // size_y == there // size_y, weight(here - there), 0.0)
    along_y[...] = near.astype(jnp.bfloat16)


def outer_matrices(size_x, size_y, outer):
    half = size_x // 2
    shape = (half * 8, half * 8)
    here, there = index(shape, 0), index(shape, 1)
    y, row = lax.rem(here, 8), lax.rem(there, 4)
    y = jnp.where(y < 4, y, y + size_y - 8)
    below, above = weight(y - row + 4), weight(row + size_y - y)
    for field in range(2):
        use = (here // 8 == there // 8) & (lax.rem(there, 8) // 4 == field)
        both = jnp.concatenate([jnp.where(use, below, 0.0), jnp.where(use, above, 0.0)], axis=1)
        outer[field] = both.astype(jnp.bfloat16)


def tables_kernel(size_x, size_y, cells, res, other, inject, along_y, along_z, outer):
    difference_matrices(size_y, along_y, along_z)
    outer_matrices(size_x, size_y, outer)
    inject_kernel(size_x, size_y, 0, cells, res, other, inject)


def inject_kernel(size_x, size_y, step, cells, res, other, inject):
    depth = inject.shape[2]
    half = size_x // 2
    rows = half * size_y
    count = cells.shape[1]
    x = cells[0:1, :] - lax.axis_index("gx") * size_x
    y = cells[1:2, :] - lax.axis_index("gy") * size_y
    inside = (x >= 0) & (x < size_x) & (y >= 0) & (y < size_y)
    place = jnp.where(inside, x * size_y + y, -1)
    deep = index((depth, count), 0) == cells[2:3, :]
    parts = three(jnp.where(deep, res[step : step + 1, :], 0.0))
    for part in range(2):
        at = index((rows, count), 0) + part * rows
        flat = jnp.where(at == place, 1.0, 0.0).astype(jnp.bfloat16)
        done = sum(lax.dot_general(flat, p, (((1,), (1,)), ((), ())), preferred_element_type=F32) for p in parts)
        inject[part * half : (part + 1) * half] = done.reshape(half, size_y, depth)


def first_inner_kernel(wave1, yb, ya, next0, next1, cell, amp, lap1, flat, along_y, along_z, outer, row):
    size_x, size_y = wave1.shape[0], wave1.shape[1]
    difference_matrices(size_y, along_y, along_z)
    outer_matrices(size_x, size_y, outer)
    flat_part(wave1, along_y, along_z, flat)
    both = outer_part(ya, yb, 0, outer)
    row[...] = both.reshape(size_x, 8, both.shape[3])
    planes = within(wave1)
    for z in halves():
        for x in range(size_x):
            lap = across(planes, x, z) + flat[x, :, z] * (1.0 / SCALE)
            lap1[x, :, z] = lap + spread(row[x, :, z], size_y)


def first_kernel(inner, xb, xa, lap1, side):
    size_x = lap1.shape[0]
    outside_x(xa, xb, 0, side)
    lap1[0:4] = inner[0:4] + side[0:4]
    lap1[size_x - 4 : size_x] = inner[size_x - 4 : size_x] + side[4:8]


def second_kernel(
    offsets, column, lap1, wave0, wave1, adj4, cell, amp, vel, wave2, image, ya, yb, xa, xb
):
    size_x, size_y = wave1.shape[0], wave1.shape[1]
    start = offsets[0]
    low = start // HALF
    shift_by = lax.rem(start, HALF)
    back = lax.rem(HALF - shift_by, HALF)
    third = jnp.minimum(low + 2, 3)

    plane, amounts = source_of(cell, amp, 0, size_x, size_y)

    def body(x, _):
        lane = lax.broadcasted_iota(jnp.int32, (size_y, HALF), 1)
        rolled = [pltpu.roll(column[i, x], back, 1) for i in (low, low + 1, third)]
        for h, z in enumerate(halves()):
            v = jnp.where(lane < HALF - shift_by, rolled[h], rolled[h + 1])
            vel[x, :, z] = v
            wave = 2.0 * wave1[x, :, z] - wave0[x, :, z] + v * lap1[x, :, z]
            wave = wave + jnp.where(plane == x, amounts[h], 0.0)
            product4 = v * adj4[x, :, z]
            wave2[x, :, z] = wave
            image[x, :, z] = product4
            put_rows(wave, product4, ya, yb, x, z)
        return 0

    lax.fori_loop(0, size_x, body, 0, unroll=4)
    put_planes(wave2, xa, xb, 0)
    put_planes(image, xa, xb, 4)


def third_inner_kernel(
    wave1, wave2, adj4, adj5, vel, image, cell, amp, inject, along_y, along_z,
    lap2, wave3, adj3, flat, flat2,
):
    flat_part(wave2, along_y, along_z, flat)
    flat_part(image, along_y, along_z, flat2)
    plane, amounts = source_of(cell, amp, 1, wave1.shape[0], wave1.shape[1])
    waves, images = within(wave2), within(image)
    for h, z in enumerate(halves()):
        for x in range(wave1.shape[0]):
            lap = across(waves, x, z) + flat[x, :, z] * (1.0 / SCALE)
            lap2[x, :, z] = lap
            wave = 2.0 * waves(x, z) - wave1[x, :, z] + vel[x, :, z] * lap
            wave3[x, :, z] = wave + jnp.where(plane == x, amounts[h], 0.0)
            adj = across(images, x, z) + flat2[x, :, z] * (1.0 / SCALE)
            adj3[x, :, z] = 2.0 * adj4[x, :, z] - adj5[x, :, z] + adj + inject[x, :, z]


def third_kernel(
    yb, ya, xb, xa, lap2_in, wave3_in, adj3_in, vel, outer,
    lap2, wave3, adj3, image3, pya, pyb, pxa, pxb, side, side2, row, row2,
):
    outer_parts(ya, yb, xa, xb, outer, (side, side2), (row, row2))
    for x in range(vel.shape[0]):
        for z in halves():
            v = vel[x, :, z]
            extra = outer_of(side, row, x, z)
            lap2[x, :, z] = lap2_in[x, :, z] + extra
            wave = wave3_in[x, :, z] + v * extra
            wave3[x, :, z] = wave
            adj = adj3_in[x, :, z] + outer_of(side2, row2, x, z)
            adj3[x, :, z] = adj
            image3[x, :, z] = v * adj
            put_rows(wave, v * adj, pya, pyb, x, z)
    put_planes(wave3, pxa, pxb, 0)
    put_planes(image3, pxa, pxb, 4)


def fourth_inner_kernel(
    wave3, image3, adj3, adj4, lap1, lap2, inject, along_y, along_z,
    adj2, grad, flat, flat2,
):
    flat_part(wave3, along_y, along_z, flat)
    flat_part(image3, along_y, along_z, flat2)
    waves, images = within(wave3), within(image3)
    for z in halves():
        for x in range(wave3.shape[0]):
            lap3 = across(waves, x, z) + flat[x, :, z] * (1.0 / SCALE)
            adj = across(images, x, z) + flat2[x, :, z] * (1.0 / SCALE)
            old, mid = adj4[x, :, z], adj3[x, :, z]
            adj = 2.0 * mid - old + adj + inject[x, :, z]
            adj2[x, :, z] = adj
            grad[x, :, z] = old * lap3 + mid * lap2[x, :, z] + adj * lap1[x, :, z]


def fourth_kernel(
    offsets, yb, ya, xb, xa, grad_in, adj4, lap1, outer,
    far, near_b, near_a, own, extra2, side, side2, row, row2,
):
    size_x, size_y = adj4.shape[0], adj4.shape[1]
    outer_parts(ya, yb, xa, xb, outer, (side, side2), (row, row2))
    start = offsets[0]
    low = start // HALF
    shift_by = lax.rem(start, HALF)

    me = lax.axis_index("shot")
    turn = jnp.where(even("shot"), 1, 3)
    which = [(lax.rem(me + away, 4) - low, tile) for away, tile in ((2, far), (turn, near_a), (4 - turn, near_b), (0, own))]

    lane = lax.broadcasted_iota(jnp.int32, (size_y, HALF), 1)
    high = lane >= shift_by
    for x in range(size_x):
        rolled = []
        for z in halves():
            more = outer_of(side2, row2, x, z)
            extra2[x, :, z] = more
            grad = grad_in[x, :, z] + adj4[x, :, z] * outer_of(side, row, x, z) + lap1[x, :, z] * more
            rolled.append(pltpu.roll(grad, shift_by, 1))
        first = jnp.where(high, rolled[0], 0.0)
        second = jnp.where(high, rolled[1], rolled[0])
        third = jnp.where(high, 0.0, rolled[1])
        for n, tile in which:
            value = jnp.where(n == 0, first, jnp.where(n == 1, second, third))
            tile[x] = jnp.where((n >= 0) & (n <= 2), value, 0.0)


def adjoint_kernel(adj2_in, extra, adj2):
    adj2[...] = adj2_in[...] + extra[...]


def sum_kernel(own, far, b, a, out):
    out[...] = (own[...] + far[...]) + (a[...] + b[...])


def local(model_vel2, offsets, wave_prev, wave_cur, adj_cur, adj_next, src_cell, src_amp, rec_cell, rec_res):
    size_x, size_y, depth = wave_cur.shape[1:]
    wave0, wave1, adj4, adj5 = wave_prev[0], wave_cur[0], adj_cur[0], adj_next[0]
    block = shaped(size_x, size_y, depth)
    edge_y, edge_x = shaped(size_x, 8, depth), shaped(8, size_y, depth)
    tile = shaped(size_x, size_y, HALF)
    whole = pltpu.VMEM((size_x, size_y, depth), F32)
    side = pltpu.VMEM((8, size_y, depth), F32)
    rows, bf16 = size_x // 2 * size_y, jnp.bfloat16
    rows8 = pltpu.VMEM((size_x, 8, depth), F32)

    copies = pl.pallas_call(
        copies_kernel,
        out_shape=shaped(4, size_x, size_y, HALF),
        in_specs=[pl.BlockSpec(memory_space=pltpu.HBM)],
        out_specs=pl.BlockSpec(memory_space=pltpu.HBM),
        scratch_shapes=[pltpu.SemaphoreType.DMA((4,))],
        compiler_params=pltpu.CompilerParams(vmem_limit_bytes=1 << 20),
    )(model_vel2)
    column = lax.all_to_all(copies, "shot", 0, 0)
    edges = call(
        edges_kernel, (shaped(size_x // 2, 8, depth),) * 2 + (shaped(4, size_y, depth),) * 2, n_in=1, room=1
    )(wave1)
    halos = exchange(edges)
    yb, ya, xb, xa = halos
    matrices = ((rows, rows), (depth, depth), (2, size_x // 2 * 8, size_x // 2 * 16))
    own = tuple(pltpu.VMEM(dims, bf16) for dims in matrices)
    lap1 = call(first_inner_kernel, block, (whole, *own, rows8), n_in=7, room=2)(
        wave1, yb, ya, wave0, adj4, src_cell, src_amp
    )
    lap1 = call(first_kernel, block, (side,), n_in=3, room=1, aliases={0: 0})(lap1, xb, xa)
    vel, wave2, image, *edges = call(
        second_kernel, (block,) * 3 + (edge_y,) * 2 + (edge_x,) * 2,
        smem=1, n_in=7, room=4,
    )(offsets, column, lap1, wave0, wave1, adj4, src_cell, src_amp)
    cells, res = jnp.transpose(rec_cell[0]), jnp.transpose(rec_res[0])
    inject0, along_y, along_z, outer = pl.pallas_call(
        functools.partial(tables_kernel, size_x, size_y),
        out_shape=(block, *(jax.ShapeDtypeStruct(dims, bf16) for dims in matrices)),
        in_specs=[pl.BlockSpec(memory_space=pltpu.VMEM)] * 2 + [pl.BlockSpec(memory_space=pl.ANY)],
        out_specs=(pl.BlockSpec(memory_space=pltpu.VMEM),) * 4,
        compiler_params=pltpu.CompilerParams(vmem_limit_bytes=4 << 20),
    )(cells, res, vel)
    halos = exchange(edges)
    inner = call(third_inner_kernel, (block,) * 3, (whole,) * 2, n_in=11, room=10)(
        wave1, wave2, adj4, adj5, vel, image, src_cell, src_amp, inject0, along_y, along_z
    )
    lap2, wave3, adj3, image3, *edges = call(
        third_kernel, (block,) * 4 + (edge_y,) * 2 + (edge_x,) * 2, (side, side, rows8, rows8), n_in=9,
        room=10, aliases={4: 0, 5: 1, 6: 2},
    )(*halos, *inner, vel, outer)
    halos = exchange(edges)
    inject1 = pl.pallas_call(
        functools.partial(inject_kernel, size_x, size_y, 1),
        out_shape=block,
        in_specs=[pl.BlockSpec(memory_space=pltpu.VMEM)] * 2 + [pl.BlockSpec(memory_space=pl.ANY)],
        out_specs=pl.BlockSpec(memory_space=pltpu.VMEM),
        compiler_params=pltpu.CompilerParams(vmem_limit_bytes=4 << 20),
    )(cells, res, adj3)
    inner_adj2, inner_grad = call(fourth_inner_kernel, (block,) * 2, (whole,) * 2, n_in=9, room=10)(
        wave3, image3, adj3, adj4, lap1, lap2, inject1, along_y, along_z
    )
    far, near_b, near_a, own, extra = call(
        fourth_kernel, (tile, tile, tile, tile, block), (side, side, rows8, rows8), smem=1, n_in=8, room=10
    )(offsets, *halos, inner_grad, adj4, lap1, outer)
    far, b, a = swap_across(far), swap_shot(near_b, 1), swap_shot(near_a, 0)
    adj2 = call(adjoint_kernel, block, n_in=2)(inner_adj2, extra)
    owned = call(sum_kernel, tile, n_in=4)(own, far, b, a)
    return owned, adj2[None]


def solution(mesh):
    return jax.shard_map(
        local,
        mesh=mesh,
        in_specs=(
            P("gx", "gy", "shot"),
            P("shot"),
            P("shot", "gx", "gy", None),
            P("shot", "gx", "gy", None),
            P("shot", "gx", "gy", None),
            P("shot", "gx", "gy", None),
            P("shot", None),
            P("shot", None),
            P("shot", None, None),
            P("shot", None, None),
        ),
        out_specs=(P("gx", "gy", "shot"), P("shot", "gx", "gy", None)),
        check_vma=False,
    )
```
